256 devices in a mesh: ctx: 32 (over y, x, core), head: 8 (over z).
Axes of the slice: x: 4, y: 4, z: 8, core: 2. Of those that a mesh axis runs over, the one named last changes fastest.
Arguments:
- byte_rows: bfloat16 [98304, 2048], P('ctx'), may hold values from -6 to 6
- boundary: int32 [98304], P('ctx'), may hold values from 0 to 1, as said below
- gate_proj: bfloat16 [2048, 4096], P(None, 'head'), may hold values from -0.125 to 0.125
- value_proj: bfloat16 [2048, 4096], P(None, 'head'), may hold values from -0.125 to 0.125
- state_proj: bfloat16 [2048, 256], replicated, may hold values from -0.125 to 0.125
- step_proj: bfloat16 [2048, 64], P(None, 'head'), may hold values from -0.125 to 0.125
- step_bias: float32 [64], P('head'), may hold values from -1 to 0.5
- decay_log: float32 [64], P('head'), may hold values from -12 to -2
- skip_gain: float32 [64], P('head'), may hold values from 0.5 to 1.5
- value_conv: float32 [4, 4096], P(None, 'head'), may hold values from -3 to 3
- value_shift: float32 [4096], P('head'), may hold values from -3 to 3
- state_conv: float32 [4, 256], replicated, may hold values from -3 to 3
- state_shift: float32 [256], replicated, may hold values from -3 to 3
- norm_gain: float32 [4096], P('head'), may hold values from 0.1 to 1.9
Outputs:
- byte_output: float32 [98304, 4096], P('ctx', 'head')
The draws below stay inside these ranges and needn't reach their ends.
Inputs may be any that keep to these rules, and one draw needn't show every extreme that they name: The first byte is a boundary, and exactly 32768 bytes are boundaries. For every s, the boundaries among bytes s * 3072 to (s + 1) * 3072 - 1 have group numbers from s * 1024 - 512 to (s + 1) * 1024 + 511, and such a range of bytes holds at most 2048 boundaries; in every draw one range reaches both ends of its group numbers and holds 2048 boundaries.
All inputs are finite; a program needn't handle non-finite values.
Results may differ from the reference program's by a relative error of at most 0.008.
Values may be sent and summed in bfloat16 or wider, within the bound.
A program may use at most 128 MiB of HBM per device.

```python
import jax
import jax.numpy as jnp
from jax import lax

D = 2048
HEADS = 64
HEAD_DIM = 64
STATE = 128
CONV = 4
SSD_BLOCK = 256
GROUP_DEV = 1024
INNER = 4096
BYTES_DEV = 3072
DRIFT = 512
GROUPS = 32768
BYTES = 98304


def draw_boundary(key, part):
    key = jax.random.fold_in(key, 11)
    first_key, second_key, third_key, fourth_key = jax.random.split(key, 4)
    shards = BYTES // BYTES_DEV
    magnitude = jax.random.randint(first_key, (shards,), DRIFT - DRIFT // 4, DRIFT + 1)
    direction = jax.random.randint(fourth_key, (shards,), 0, 2) * 2 - 1
    drifts = magnitude * direction
    chosen = jax.random.randint(second_key, (), 1, shards - 1)
    positions = jnp.arange(shards)
    drifts = jnp.where(positions == chosen - 1, -DRIFT, drifts)
    drifts = jnp.where(positions == chosen, DRIFT, drifts)
    drifts = jnp.where(positions == shards - 1, 0, drifts)
    before = jnp.concatenate([jnp.zeros((1,), drifts.dtype), drifts[:-1]])
    counts = GROUP_DEV + drifts - before
    scores = jax.random.randint(third_key, (shards, BYTES_DEV), 0, 1 << 18) * BYTES_DEV + jnp.arange(BYTES_DEV)[None, :]
    scores = scores.at[0, 0].set(-1)
    ordering = jnp.argsort(scores, axis=1)
    placing = jnp.argsort(ordering, axis=1)
    flags = (placing < counts[:, None]).astype(jnp.int32)
    return flags.reshape(-1)


def draw_decay_log(key, part):
    key = jax.random.fold_in(key, 23)
    first_key, second_key, third_key = jax.random.split(key, 3)
    middle = jnp.log(3.0 / GROUPS)
    top = jnp.log(1.0 / 15.0)
    lasting = jax.random.uniform(first_key, (HEADS,)) < 0.5
    bottom = jnp.log(0.5 / GROUPS)
    slow_rate = bottom + (middle - bottom) * jax.random.uniform(second_key, (HEADS,))
    fast_rate = middle + (top - middle) * jax.random.uniform(third_key, (HEADS,))
    return jnp.where(lasting, slow_rate, fast_rate).astype(jnp.float32)


def block_scale(key, dims, cuts, smallest, largest):
    def one(dim, blocks):
        steps = jax.random.uniform(jax.random.fold_in(jax.random.fold_in(key, 6), dim), (blocks,), jnp.float32, smallest / len(cuts), largest / len(cuts))
        return jnp.repeat(jnp.exp(steps), dims[dim] // blocks).reshape((-1,) + (1,) * (len(dims) - dim - 1))

    factor_of = one(*cuts[0])
    for cut in cuts[1:]:
        factor_of = factor_of * one(*cut)
    return factor_of


def scatter_about(rng, shape, scale, most, cuts=(), kind=jnp.bfloat16):
    loudness = block_scale(rng, shape, cuts, -0.22, 0.18) if cuts else 1.0
    array = jax.random.normal(rng, shape, jnp.float32) * scale * loudness
    return jnp.minimum(jnp.maximum(array, -most), most).astype(kind)


def setup_inputs(seed: int = 0) -> dict:
    seeds = jax.random.split(jax.random.key(seed), 15)
    byte_rows = scatter_about(seeds[0], (BYTES, D), 1.0, 6.0, ((0, 32),))
    boundary = draw_boundary(jax.random.fold_in(seeds[14], 71), 0)
    gate_proj = scatter_about(seeds[2], (D, INNER), D ** -0.5, 0.125, ((1, 8),))
    value_proj = scatter_about(seeds[3], (D, INNER), D ** -0.5, 0.125, ((1, 8),))
    state_proj = scatter_about(seeds[4], (D, 2 * STATE), D ** -0.5, 0.125)
    step_proj = scatter_about(seeds[5], (D, HEADS), D ** -0.5, 0.125, ((1, 8),))
    step_bias = jnp.clip(-1.0 + 1.5 * jax.random.uniform(seeds[6], (HEADS,), jnp.float32) ** block_scale(seeds[6], (HEADS,), ((0, 8),), -0.2, 0.2), -1.0, 0.5)
    decay_log = draw_decay_log(jax.random.fold_in(seeds[14], 71), 0)
    skip_gain = jnp.clip(0.5 + 1.0 * jax.random.uniform(seeds[8], (HEADS,), jnp.float32) ** block_scale(seeds[8], (HEADS,), ((0, 8),), -0.2, 0.2), 0.5, 1.5)
    value_conv = scatter_about(seeds[9], (CONV, INNER), CONV ** -0.5, 3.0, ((1, 8),), jnp.float32)
    value_shift = scatter_about(seeds[10], (INNER,), 0.5, 3.0, ((0, 8),), jnp.float32)
    state_conv = scatter_about(seeds[11], (CONV, 2 * STATE), CONV ** -0.5, 3.0, (), jnp.float32)
    state_shift = scatter_about(seeds[12], (2 * STATE,), 0.5, 3.0, (), jnp.float32)
    norm_gain = jnp.clip(1.0 + 0.18 * jax.random.normal(seeds[13], (INNER,), jnp.float32), 0.1, 1.9)
    return dict(byte_rows=byte_rows, boundary=boundary, gate_proj=gate_proj, value_proj=value_proj, state_proj=state_proj, step_proj=step_proj, step_bias=step_bias, decay_log=decay_log, skip_gain=skip_gain, value_conv=value_conv, value_shift=value_shift, state_conv=state_conv, state_shift=state_shift, norm_gain=norm_gain)


EPSILON = 1e-05

def conv_silu(raw, weight, shift):
    taps = weight.shape[0]
    length = raw.shape[0]
    padded = jnp.concatenate([jnp.zeros((taps - 1, raw.shape[1]), raw.dtype), raw], 0).astype(jnp.float32)
    total = jnp.zeros((length, raw.shape[1]), jnp.float32) + shift[None, :]
    for kernel_tap in range(taps):
        total = total + weight[kernel_tap][None, :] * padded[kernel_tap:kernel_tap + length]
    return jax.nn.silu(total).astype(jnp.bfloat16)

def state_space(values, in_maps, out_maps, steps, rates):
    block = min(SSD_BLOCK, GROUPS)
    blocks = GROUPS // block
    value_blocks = values.reshape(blocks, block, HEADS, HEAD_DIM)
    in_blocks = in_maps.reshape(blocks, block, STATE)
    out_blocks = out_maps.reshape(blocks, block, STATE)
    step_blocks = steps.reshape(blocks, block, HEADS)
    lower = jnp.arange(block)[:, None] >= jnp.arange(block)[None, :]

    def advance(carried, pieces):
        value_block, in_block, out_block, step_block = pieces
        decays = -step_block * rates[None, :]
        running = jnp.cumsum(decays, axis=0)
        scores = jnp.dot(out_block, in_block.T, preferred_element_type=jnp.float32)
        spread = running[:, None, :] - running[None, :, :]
        masked = lower[:, :, None]
        weights = jnp.where(masked, scores[:, :, None] * jnp.exp(jnp.where(masked, spread, 0.0)) * step_block[None, :, :], 0.0)
        weights = weights.astype(jnp.bfloat16)
        intra = jnp.einsum('tsh,shp->thp', weights.astype(jnp.float32), value_block.astype(jnp.float32))
        inter = jnp.exp(running)[:, :, None] * jnp.einsum('tn,hpn->thp', out_block.astype(jnp.float32), carried, precision=lax.Precision.HIGHEST)
        tail = jnp.exp(running[-1:, :] - running) * step_block
        weighted = value_block.astype(jnp.float32) * tail[:, :, None]
        fresh = jnp.einsum('shp,sn->hpn', weighted, in_block.astype(jnp.float32), precision=lax.Precision.HIGHEST)
        carried = jnp.exp(running[-1])[:, None, None] * carried + fresh
        return (carried, intra + inter)
    start_state = jnp.zeros((HEADS, HEAD_DIM, STATE), jnp.float32)
    unused, outputs = lax.scan(advance, start_state, (value_blocks, in_blocks, out_blocks, step_blocks))
    return outputs.reshape(GROUPS, HEADS, HEAD_DIM)

def reference(byte_rows, boundary, gate_proj, value_proj, state_proj, step_proj, step_bias, decay_log, skip_gain, value_conv, value_shift, state_conv, state_shift, norm_gain):
    places = jnp.nonzero(boundary > 0, size=GROUPS)[0].astype(jnp.int32)
    group_rows = jnp.take(byte_rows, places, axis=0)
    gate = jnp.dot(group_rows, gate_proj, preferred_element_type=jnp.float32).astype(jnp.bfloat16)
    value_raw = jnp.dot(group_rows, value_proj, preferred_element_type=jnp.float32).astype(jnp.bfloat16)
    state_raw = jnp.dot(group_rows, state_proj, preferred_element_type=jnp.float32).astype(jnp.bfloat16)
    step_raw = jnp.dot(group_rows, step_proj, preferred_element_type=jnp.float32).astype(jnp.bfloat16)
    values = conv_silu(value_raw, value_conv, value_shift)
    states = conv_silu(state_raw, state_conv, state_shift)
    steps = jax.nn.softplus(step_raw.astype(jnp.float32) + step_bias[None, :])
    rates = jnp.exp(decay_log)
    mixed = state_space(values, states[:, :STATE], states[:, STATE:], steps, rates)
    mixed = mixed + skip_gain[None, :, None] * values.reshape(GROUPS, HEADS, HEAD_DIM).astype(jnp.float32)
    gated = mixed.reshape(GROUPS, INNER) * jax.nn.silu(gate.astype(jnp.float32))
    power = lax.optimization_barrier(jnp.sum(gated * gated, axis=1)) / INNER
    group_out = gated * lax.rsqrt(power + EPSILON)[:, None] * norm_gain[None, :]
    ranks = (jnp.cumsum(boundary) - 1).astype(jnp.int32)
    return jnp.take(group_out, ranks, axis=0)
```

```python
import functools

import jax
import jax.numpy as jnp
from jax import lax
from jax.experimental import pallas as pl
from jax.experimental.pallas import tpu as pltpu
from jax.sharding import PartitionSpec as P

F32 = jnp.float32
BF16 = jnp.bfloat16
I32 = jnp.int32
HEAD_DIM = 64
STATE = 128
HEADS_HERE = 8
WIDE = HEADS_HERE * HEAD_DIM
INNER = 4096
T = 128
BLOCK = 256
SPAN = BLOCK + 16
LEAD = 24
EPSILON = 1e-05
LOG_FLOOR = -1e4
MESH = pl.DeviceIdType.MESH


def on_chip(shape, kind):
    return pltpu.VMEM(shape, kind)


def keep_on_chip(array):
    return pltpu.with_memory_space_constraint(array, pltpu.VMEM)


def keep_off_chip(array):
    return pltpu.with_memory_space_constraint(array, pltpu.HBM)


def dot(a, b):
    return jnp.dot(a, b, preferred_element_type=F32)


def dot_tn(a, b):
    return lax.dot_general(a, b, (((0,), (0,)), ((), ())), preferred_element_type=F32)


def dot_nt(a, b):
    return lax.dot_general(a, b, (((1,), (1,)), ((), ())), preferred_element_type=F32)


def iota(shape, axis):
    return lax.broadcasted_iota(I32, shape, axis)


def silu(v):
    return 0.5 * v * (1.0 + jnp.tanh(0.5 * v))


def flag(condition):
    return jnp.where(condition, 1.0, 0.0).astype(BF16)


def pieces(v, count):
    out = []
    for _ in range(count):
        top = v.astype(BF16).astype(F32)
        out.append(top)
        v = v - top
    return out


def compact_kernel(
    groups,
    bnd_ref,
    bytes_hbm,
    rows_ref,
    tail_ref,
    count_ref,
    rank_ref,
    start_ref,
    held,
    target,
    sems,
):
    blocks = bytes_hbm.shape[0] // BLOCK
    lines = 2 * blocks
    width = rows_ref.shape[1]

    def fetch(j):
        at = pl.ds(pl.multiple_of(j * BLOCK, BLOCK), BLOCK)
        return pltpu.make_async_copy(bytes_hbm.at[at], held.at[at], sems.at[j])

    def begin(j, carry):
        fetch(j).start()
        return carry

    lax.fori_loop(0, blocks, begin, 0)

    bnd = bnd_ref[...].reshape(lines, 128).astype(F32)
    bnd16 = bnd.astype(BF16)
    inside = dot(bnd16, flag(iota((128, 128), 0) <= iota((128, 128), 1)))
    above = dot(flag(iota((lines, lines), 1) < iota((lines, lines), 0)), bnd16)
    before = jnp.sum(above, axis=1, keepdims=True)
    upto = inside + before
    target[...] = jnp.where(bnd > 0, upto - 1.0, -1.0).astype(I32)
    rank_ref[...] = jnp.concatenate([upto, jnp.zeros((128 - lines, 128), F32)], 0).T
    for j in range(blocks):
        start_ref[j] = before[2 * j, 0].astype(I32)
    count = upto[lines - 1, 127].astype(I32)
    count_ref[...] = jnp.full(count_ref.shape, count, I32)
    rows_ref[0:16, :] = jnp.zeros((16, width), BF16)

    def step(j, carry):
        fetch(j).wait()
        base = pl.multiple_of((start_ref[j] // 16) * 16, 16)
        places = iota((SPAN, 128), 0) + base
        left = places == target[pl.ds(2 * j, 1), :]
        right = places == target[pl.ds(2 * j + 1, 1), :]
        choose = jnp.concatenate([flag(left), flag(right)], 1)
        here = pl.ds(pl.multiple_of(j * BLOCK, BLOCK), BLOCK)
        piece = min(512, width)
        for c in range(0, width, piece):
            cols = pl.ds(c, piece)
            picked = dot(choose, held[here, cols]).astype(BF16)
            rows_ref[pl.ds(base, 16), cols] = rows_ref[pl.ds(base, 16), cols] + picked[:16]
            rows_ref[pl.ds(pl.multiple_of(base + 16, 16), BLOCK), cols] = picked[16:]
        return carry

    lax.fori_loop(0, blocks, step, 0)

    clear = (start_ref[blocks - 1] // 16) * 16 + SPAN

    def wipe(i, carry):
        rows_ref[pl.ds(pl.multiple_of(clear + 16 * i, 16), 16), :] = jnp.zeros((16, width), BF16)
        return carry

    lax.fori_loop(0, jnp.maximum(groups + 32 - clear, 0) // 16, wipe, 0)
    near = pl.multiple_of((jnp.maximum(count - 4, 0) // 16) * 16, 16)
    row, column = iota((16, 32), 0), iota((16, 32), 1)
    wanted = count - 16 + row
    choose = flag((row >= 12) & (wanted >= 0) & (column + near == wanted))
    last = dot(choose, rows_ref[pl.ds(near, 32), :])
    few = jnp.minimum(count, 4).astype(F32)
    tail_ref[...] = jnp.where(iota(last.shape, 0) == 0, few, last).astype(BF16)


def compact(boundary, byte_rows, groups):
    length, width = byte_rows.shape
    blocks = length // BLOCK
    vmem = pl.BlockSpec(memory_space=pltpu.VMEM)
    return pl.pallas_call(
        functools.partial(compact_kernel, groups),
        out_shape=[
            on_chip((groups + SPAN, width), BF16),
            on_chip((16, width), BF16),
            on_chip((8, 128), I32),
            on_chip((128, 128), F32),
            jax.ShapeDtypeStruct((blocks,), I32),
        ],
        in_specs=[vmem, pl.BlockSpec(memory_space=pltpu.HBM)],
        out_specs=[vmem, vmem, vmem, vmem, pl.BlockSpec(memory_space=pltpu.SMEM)],
        scratch_shapes=[
            pltpu.VMEM((length, width), BF16),
            pltpu.VMEM((2 * blocks, 128), I32),
            pltpu.SemaphoreType.DMA((blocks,)),
        ],
        compiler_params=pltpu.CompilerParams(vmem_limit_bytes=30 << 20),
        cost_estimate=pl.CostEstimate(
            flops=2 * SPAN * length * width, bytes_accessed=2 * length * width, transcendentals=0
        ),
    )(boundary, byte_rows)


def head_column(ref, shape):
    head = iota(shape, 0) % HEADS_HERE
    out = jnp.zeros(shape, F32)
    for h in range(HEADS_HERE):
        out = jnp.where(head == h, ref[h], out)
    return out


def layer_kernel(
    n_ctx,
    n_head,
    groups,
    rows_ref,
    tail_ref,
    count_ref,
    value_ref,
    gate_ref,
    state_ref,
    step_ref,
    bias_ref,
    log_ref,
    skip_ref,
    vconv_ref,
    vshift_ref,
    sconv_ref,
    sshift_ref,
    table_ref,
    inv_ref,
    ext,
    xs,
    maps,
    mix,
    open_gate,
    grow,
    fresh,
    raw_step,
    lead_t,
    lead_e,
    minus,
    sel_d,
    sel_e,
    near,
    halo_gate,
    out_slices,
    in_slices,
    ret_out,
    ret_in,
    entry,
    squares,
    near_send,
    near_recv,
    out_send,
    out_recv,
    ret_send,
    ret_recv,
    sq_send,
    sq_recv,
):
    me = lax.axis_index("ctx")
    column = lax.axis_index("head")
    subs = groups // T
    share = STATE * 4 // n_ctx
    big = 2 * T
    bigs = groups // big

    barrier = pltpu.get_barrier_semaphore()

    def greet_ctx(d, carry):
        pl.semaphore_signal(
            barrier, inc=1, device_id={"ctx": lax.rem(me + d, n_ctx)}, device_id_type=MESH
        )
        return carry

    def greet_head(d, carry):
        pl.semaphore_signal(
            barrier, inc=1, device_id={"head": lax.rem(column + d, n_head)}, device_id_type=MESH
        )
        return carry

    lax.fori_loop(1, n_ctx, greet_ctx, 0)
    lax.fori_loop(1, n_head, greet_head, 0)
    pl.semaphore_wait(barrier, n_ctx - 1 + n_head - 1)

    def near_copy(d):
        return pltpu.make_async_remote_copy(
            src_ref=tail_ref,
            dst_ref=near.at[d - 1],
            send_sem=near_send.at[d - 1],
            recv_sem=near_recv.at[d - 1],
            device_id={"ctx": lax.rem(me + d, n_ctx)},
            device_id_type=MESH,
        )

    near_copy(1).start()
    near_copy(2).start()

    for i in range(groups // 512):
        got = dot_nt(step_ref[...], rows_ref[i * 512 : (i + 1) * 512, :])
        for q in range(4):
            k = i * 4 + q
            raw_step[k * 8 : (k + 1) * 8, :] = got[:8, q * T : (q + 1) * T]
    shape = (subs * 8, T)
    raw = raw_step[...] + head_column(bias_ref, shape)
    soft = jnp.maximum(raw, 0.0) + jnp.log1p(jnp.exp(-jnp.abs(raw)))
    valid = (iota(shape, 0) // 8) * T + iota(shape, 1) < count_ref[0:1, :]
    step = jnp.where(valid, soft, 0.0)
    logs = jnp.where(valid, jnp.maximum(jnp.log(soft), LOG_FLOOR), LOG_FLOOR)
    decay = -step * jnp.exp(head_column(log_ref, shape))
    tri = flag(iota((T, T), 0) <= iota((T, T), 1))
    d0, d1, d2 = pieces(decay, 3)
    cum = (dot(d0.astype(BF16), tri) + dot(d1.astype(BF16), tri)) + dot(d2.astype(BF16), tri)
    total = jnp.broadcast_to(cum[:, T - 1 : T], shape)
    cums = pieces(cum, 3)
    lows = pieces(logs - cum, 3)
    grows = pieces(jnp.exp(cum), 2)
    tails = pieces(jnp.exp(total - cum) * step, 2)
    for k in range(subs):
        at = slice(k * 8, (k + 1) * 8)
        lead_t[k] = jnp.concatenate([p[at] for p in cums] + [jnp.ones((24, T), F32)], 0).astype(BF16)
        lead_e[k] = jnp.concatenate([p[at] for p in grows + tails], 0).astype(BF16)
        minus[k] = jnp.concatenate([p[at] for p in lows], 0)
    head_of = iota((24, 8 * T), 0) % 8
    sel_d[...] = flag(head_of == iota((24, 8 * T), 1) // T).astype(F32)
    row, lane = iota((32, 2 * WIDE), 0), iota((32, 2 * WIDE), 1)
    sel_e[...] = flag((row % 8 == (lane % WIDE) // HEAD_DIM) & ((row < 16) == (lane < WIDE)))

    near_copy(1).wait()
    near_copy(2).wait()
    first = jnp.where(me >= 1, near[0].astype(F32), 0.0)
    second = jnp.where(me >= 2, near[1].astype(F32), 0.0)
    few = jnp.broadcast_to(near[0][0:1, 0:16].astype(F32), (16, 16))
    few = jnp.where(me >= 1, few, 4.0)
    row, lane = iota((16, 16), 0), iota((16, 16), 1)
    shift = flag((row >= 12) & (lane >= 12) & (lane.astype(F32) == row.astype(F32) + few))
    halo = dot(shift, second.astype(BF16)) + jnp.where(iota(first.shape, 0) >= 12, first, 0.0)
    halo = halo.astype(BF16)
    ext[0 : LEAD - 16, :] = jnp.zeros((LEAD - 16, ext.shape[1]), F32)
    ext[LEAD - 16 : LEAD, :WIDE] = dot(halo, value_ref[...])
    ext[LEAD - 16 : LEAD, WIDE:] = dot(halo, state_ref[...])
    halo_gate[...] = silu(dot(halo, gate_ref[...]))

    def convolve(at, length):
        seen = ext[pl.ds(at, length + 8), :]
        for taps, shifts, lo, hi in (
            (vconv_ref, vshift_ref, 0, WIDE),
            (sconv_ref, sshift_ref, WIDE, WIDE + 2 * STATE),
        ):
            sum_ = shifts[...] + taps[0:1, :] * seen[5 : 5 + length, lo:hi]
            for j in range(1, 4):
                sum_ = sum_ + taps[j : j + 1, :] * seen[5 + j : 5 + j + length, lo:hi]
            yield silu(sum_).astype(BF16)

    x_h, m_h = convolve(0, 16)

    def local(i, carry):
        state, product = carry
        g0 = pl.multiple_of(i * big, big)
        here = pl.ds(g0, big)
        ext[pl.ds(g0 + LEAD, big), :WIDE] = dot(rows_ref[here, :], value_ref[...])
        ext[pl.ds(g0 + LEAD, big), WIDE:] = dot(rows_ref[here, :], state_ref[...])
        x, m = convolve(g0 + LEAD - 8, big)
        xs[here, :] = x
        maps[here, :] = m
        for q in range(big // T):
            k = i * (big // T) + q
            at = slice(q * T, (q + 1) * T)
            both = dot_tn(lead_e[k], sel_e[...])
            grow[k] = both[:, :WIDE]
            weighted = (x[at].astype(F32) * both[:, WIDE:]).astype(BF16)
            new = dot_tn(m[at, :STATE], weighted)
            fresh[k] = new
            factor = both[T - 1 : T, :WIDE]
            state = factor * state + new
            product = factor * product
        return state, product

    state, product = lax.fori_loop(
        0, bigs, local, (jnp.zeros((STATE, WIDE), F32), jnp.ones((1, WIDE), F32))
    )

    high, low = pieces(jnp.broadcast_to(product, (8, WIDE)), 2)
    ends = jnp.concatenate([high, low], 0).astype(BF16)
    whole = state.astype(BF16)
    for k in range(n_ctx):
        r, c = (k // 4) * share, (k % 4) * 128
        out_slices[k, :share, :] = whole[r : r + share, c : c + 128]
        out_slices[k, share:, :] = ends[:, c : c + 128]

    def out_copy(d):
        to = lax.rem(me + d, n_ctx)
        return pltpu.make_async_remote_copy(
            src_ref=out_slices.at[to],
            dst_ref=in_slices.at[me],
            send_sem=out_send.at[d],
            recv_sem=out_recv.at[d],
            device_id={"ctx": to},
            device_id_type=MESH,
        )

    def ret_copy(d):
        to = lax.rem(me + d, n_ctx)
        return pltpu.make_async_remote_copy(
            src_ref=ret_out.at[to],
            dst_ref=ret_in.at[me],
            send_sem=ret_send.at[d],
            recv_sem=ret_recv.at[d],
            device_id={"ctx": to},
            device_id_type=MESH,
        )

    def start_all(copy, count):
        lax.fori_loop(1, count, lambda d, c: (copy(d).start(), c)[1], 0)

    def wait_all(copy, count):
        lax.fori_loop(1, count, lambda d, c: (copy(d).wait(), c)[1], 0)

    in_slices[me] = out_slices[me]
    start_all(out_copy, n_ctx)

    skip = jnp.zeros((1, WIDE), F32)
    for h in range(HEADS_HERE):
        skip = jnp.where(iota((1, WIDE), 1) // HEAD_DIM == h, skip_ref[h], skip)
    lower = iota((T, T), 1) <= iota((T, T), 0)
    left_half = iota((T, T), 1) < HEAD_DIM

    def inside(i, carry):
        g0 = pl.multiple_of(i * big, big)
        here = pl.ds(g0, big)
        open_gate[here, :] = silu(dot(rows_ref[here, :], gate_ref[...]))
        for q in range(big // T):
            k = i * (big // T) + q
            at = pl.ds(pl.multiple_of(g0 + q * T, T), T)
            x, m = xs[at, :], maps[at, :]
            scores = jnp.where(lower, dot_nt(m[:, STATE:], m[:, :STATE]), 0.0)
            lows = minus[k]
            tile = jnp.concatenate([lows] * HEADS_HERE, 1) * sel_d[...]
            right = jnp.concatenate([sel_d[...], tile], 0).astype(BF16)
            spread = dot_tn(lead_t[k], right)
            weight = jnp.exp(jnp.minimum(spread, 60.0))
            weight = (weight * jnp.concatenate([scores] * HEADS_HERE, 1)).astype(BF16)
            for p in range(HEADS_HERE // 2):
                pair = x[:, p * T : (p + 1) * T]
                stacked = jnp.concatenate(
                    [
                        jnp.where(left_half, pair, jnp.zeros_like(pair)),
                        jnp.where(left_half, jnp.zeros_like(pair), pair),
                    ],
                    0,
                )
                got = dot(weight[:, 2 * p * T : 2 * (p + 1) * T], stacked)
                cols = slice(p * T, (p + 1) * T)
                mix[at, cols] = got + skip[:, cols] * pair.astype(F32)
        return carry

    half = bigs // 2
    lax.fori_loop(0, half, inside, 0)

    wait_all(out_copy, n_ctx)
    running = jnp.zeros((share, 128), F32)
    for i in range(n_ctx):
        ret_out[i] = running.astype(BF16)
        got = in_slices[i].astype(F32)
        factor = got[share : share + 1] + got[share + 8 : share + 9]
        running = factor * running + got[:share]
    ret_in[me] = ret_out[me]
    start_all(ret_copy, n_ctx)

    lax.fori_loop(half, bigs, inside, 0)

    wait_all(ret_copy, n_ctx)
    for k in range(n_ctx):
        r, c = (k // 4) * share, (k % 4) * 128
        entry[r : r + share, c : c + 128] = ret_in[k]

    ones = jnp.ones((8, WIDE), BF16)
    y_h = dot(m_h[:, STATE:], entry[...]) + skip * x_h.astype(F32)
    g_h = y_h * halo_gate[...]
    table_ref[0 : T - 16, :] = jnp.zeros((T - 16, WIDE), BF16)
    table_ref[T - 16 : T, :] = g_h.astype(BF16)
    power = jnp.concatenate([jnp.zeros((T - 16, WIDE), F32), g_h * g_h], 0).astype(BF16)
    mine = squares.at[column]
    mine[...] = jnp.zeros(mine.shape, F32)
    mine[0:1, :] = dot_nt(ones, power)[0:1, :]

    def outer(k, state):
        at = pl.ds(pl.multiple_of(k * T, T), T)
        factor = grow[k]
        inter = dot(maps[at, STATE:], state.astype(BF16))
        gated = (mix[at, :] + factor * inter) * open_gate[at, :]
        table_ref[pl.ds(pl.multiple_of((k + 1) * T, T), T), :] = gated.astype(BF16)
        squares[column, pl.ds(k + 1, 1), :] = dot_nt(ones, (gated * gated).astype(BF16))[0:1, :]
        return factor[T - 1 : T, :] * state + fresh[k]

    lax.fori_loop(0, subs, outer, entry[...].astype(F32))

    def sq_copy(d):
        return pltpu.make_async_remote_copy(
            src_ref=squares.at[column],
            dst_ref=squares.at[column],
            send_sem=sq_send.at[d],
            recv_sem=sq_recv.at[d],
            device_id={"head": lax.rem(column + d, n_head)},
            device_id_type=MESH,
        )

    start_all(sq_copy, n_head)
    wait_all(sq_copy, n_head)
    power = squares[0]
    for i in range(1, n_head):
        power = power + squares[i]
    inv_ref[...] = lax.rsqrt(power * (1.0 / (n_head * WIDE)) + EPSILON)


def layer(n_ctx, n_head, groups, *args):
    subs = groups // T
    share = STATE * 4 // n_ctx
    lines = -(-(subs + 1) // 8) * 8
    vmem = pl.BlockSpec(memory_space=pltpu.VMEM)
    smem = pl.BlockSpec(memory_space=pltpu.SMEM)
    width = args[0].shape[1]
    sem = pltpu.SemaphoreType.DMA
    return pl.pallas_call(
        functools.partial(layer_kernel, n_ctx, n_head, groups),
        out_shape=[
            on_chip((groups + T, WIDE), BF16),
            on_chip((lines, T), F32),
        ],
        in_specs=[vmem] * 7 + [smem] * 3 + [vmem] * 4,
        out_specs=[vmem, vmem],
        scratch_shapes=[
            pltpu.VMEM((groups + LEAD, WIDE + 2 * STATE), F32),
            pltpu.VMEM((groups, WIDE), BF16),
            pltpu.VMEM((groups, 2 * STATE), BF16),
            pltpu.VMEM((groups, WIDE), F32),
            pltpu.VMEM((groups, WIDE), F32),
            pltpu.VMEM((subs, T, WIDE), F32),
            pltpu.VMEM((subs, STATE, WIDE), F32),
            pltpu.VMEM((subs * 8, T), F32),
            pltpu.VMEM((subs, 48, T), BF16),
            pltpu.VMEM((subs, 32, T), BF16),
            pltpu.VMEM((subs, 24, T), F32),
            pltpu.VMEM((24, 8 * T), F32),
            pltpu.VMEM((32, 2 * WIDE), BF16),
            pltpu.VMEM((2, 16, width), BF16),
            pltpu.VMEM((16, WIDE), F32),
            pltpu.VMEM((n_ctx, share + 16, 128), BF16),
            pltpu.VMEM((n_ctx, share + 16, 128), BF16),
            pltpu.VMEM((n_ctx, share, 128), BF16),
            pltpu.VMEM((n_ctx, share, 128), BF16),
            pltpu.VMEM((STATE, WIDE), BF16),
            pltpu.VMEM((n_head, lines, T), F32),
            sem((2,)),
            sem((2,)),
            sem((n_ctx,)),
            sem((n_ctx,)),
            sem((n_ctx,)),
            sem((n_ctx,)),
            sem((n_head,)),
            sem((n_head,)),
        ],
        compiler_params=pltpu.CompilerParams(
            collective_id=0, has_side_effects=True, vmem_limit_bytes=32 << 20
        ),
        cost_estimate=pl.CostEstimate(
            flops=2 * groups * width * 1536, bytes_accessed=8 << 20, transcendentals=1 << 22
        ),
    )(*args)


def expand_kernel(
    groups, start_ref, rank_ref, table_ref, inv_ref, gain_ref, out_hbm, ready, sems
):
    blocks = out_hbm.shape[0] // BLOCK
    window = min(3 * T, groups + T)

    def send(j):
        at = pl.ds(pl.multiple_of(j * BLOCK, BLOCK), BLOCK)
        return pltpu.make_async_copy(ready.at[at], out_hbm.at[at], sems.at[j])

    def step(j, carry):
        line = jnp.minimum((start_ref[j] + T - 1) // T, (groups + T - window) // T)
        base = pl.multiple_of(line * T, T)
        lane = iota((T, T), 1)
        places, scales = [], []
        for half in range(2):
            rank = jnp.sum(
                jnp.where(lane == 2 * j + half, rank_ref[...], 0.0), axis=1, keepdims=True
            )
            place = jnp.broadcast_to(rank.astype(I32) + (T - 1) - base, (T, T))
            hits = [place == lane + w * T for w in range(window // T)]
            places.append(jnp.concatenate([flag(hit) for hit in hits], 1))
            scale = jnp.zeros((T, T), F32)
            for w, hit in enumerate(hits):
                scale = jnp.where(hit, inv_ref[pl.ds(line + w, 1), :], scale)
            scales.append(jnp.sum(scale, axis=1, keepdims=True))
        got = dot(jnp.concatenate(places, 0), table_ref[pl.ds(base, window), :])
        got = got * gain_ref[...] * jnp.concatenate(scales, 0)
        ready[pl.ds(pl.multiple_of(j * BLOCK, BLOCK), BLOCK), :] = got
        send(j).start()
        return carry

    lax.fori_loop(0, blocks, step, 0)

    def finish(j, carry):
        send(j).wait()
        return carry

    lax.fori_loop(0, blocks, finish, 0)


def expand(length, groups, starts, rank, table, inv, gain):
    vmem = pl.BlockSpec(memory_space=pltpu.VMEM)
    return pl.pallas_call(
        functools.partial(expand_kernel, groups),
        out_shape=jax.ShapeDtypeStruct((length, WIDE), F32),
        in_specs=[pl.BlockSpec(memory_space=pltpu.SMEM), vmem, vmem, vmem, vmem],
        out_specs=pl.BlockSpec(memory_space=pl.ANY),
        scratch_shapes=[
            pltpu.VMEM((length, WIDE), F32),
            pltpu.SemaphoreType.DMA((length // BLOCK,)),
        ],
        compiler_params=pltpu.CompilerParams(vmem_limit_bytes=24 << 20),
        cost_estimate=pl.CostEstimate(
            flops=2 * length * 3 * T * WIDE, bytes_accessed=4 * length * WIDE, transcendentals=0
        ),
    )(starts, rank, table, inv, gain)


def shards(
    groups,
    byte_rows,
    boundary,
    gate_proj,
    value_proj,
    state_proj,
    step_proj,
    step_bias,
    decay_log,
    skip_gain,
    value_conv,
    value_shift,
    state_conv,
    state_shift,
    norm_gain,
):
    n_ctx, n_head = lax.axis_size("ctx"), lax.axis_size("head")
    step_t = jnp.concatenate([step_proj.T, jnp.zeros_like(step_proj.T)], 0)
    weights = [keep_on_chip(w) for w in (value_proj, gate_proj, state_proj)]
    rows, tail, count, rank, starts = compact(boundary, keep_off_chip(byte_rows), groups)
    table, inv = layer(
        n_ctx,
        n_head,
        groups,
        rows,
        tail,
        count,
        *weights,
        step_t,
        step_bias,
        decay_log,
        skip_gain,
        value_conv,
        value_shift.reshape(1, -1),
        state_conv,
        state_shift.reshape(1, -1),
    )
    return expand(byte_rows.shape[0], groups, starts, rank, table, inv, norm_gain.reshape(1, -1))


def solution(mesh, groups=2048):
    placed = (
        P("ctx", None),
        P("ctx"),
        P(None, "head"),
        P(None, "head"),
        P(),
        P(None, "head"),
        P("head"),
        P("head"),
        P("head"),
        P(None, "head"),
        P("head"),
        P(),
        P(),
        P("head"),
    )
    return jax.shard_map(
        functools.partial(shards, groups),
        mesh=mesh,
        in_specs=placed,
        out_specs=P("ctx", "head"),
        check_vma=False,
    )
```

```python
import functools

import jax
import jax.numpy as jnp
from jax import lax
from jax.experimental import pallas as pl
from jax.experimental.pallas import tpu as pltpu
from jax.sharding import PartitionSpec as P

F32 = jnp.float32
BF16 = jnp.bfloat16
I32 = jnp.int32
HEAD_DIM = 64
STATE = 128
HEADS_HERE = 8
WIDE = HEADS_HERE * HEAD_DIM
INNER = 4096
T = 128
BLOCK = 256
SPAN = BLOCK + 16
UNROLL = 3
EPSILON = 1e-05
LOG_FLOOR = -1e4
MESH = pl.DeviceIdType.MESH


def on_chip(shape, kind):
    return pltpu.VMEM(shape, kind)


def keep_on_chip(array):
    return pltpu.with_memory_space_constraint(array, pltpu.VMEM)


def keep_off_chip(array):
    return pltpu.with_memory_space_constraint(array, pltpu.HBM)


def dot(a, b):
    return jnp.dot(a, b, preferred_element_type=F32)


def dot_tn(a, b):
    return lax.dot_general(a, b, (((0,), (0,)), ((), ())), preferred_element_type=F32)


def dot_nt(a, b):
    return lax.dot_general(a, b, (((1,), (1,)), ((), ())), preferred_element_type=F32)


def iota(shape, axis):
    return lax.broadcasted_iota(I32, shape, axis)


def silu(v):
    return 0.5 * v * (1.0 + jnp.tanh(0.5 * v))


def flag(condition):
    return jnp.where(condition, 1.0, 0.0).astype(BF16)


def pieces(v, count):
    out = []
    for _ in range(count):
        top = v.astype(BF16).astype(F32)
        out.append(top)
        v = v - top
    return out


def compact_kernel(
    groups,
    bnd_hbm,
    bytes_hbm,
    rows_ref,
    tail_ref,
    count_ref,
    rank_ref,
    start_ref,
    held,
    target,
    bnd_ref,
    sems,
    bnd_sem,
):
    blocks = bytes_hbm.shape[0] // BLOCK
    lines = 2 * blocks
    width = rows_ref.shape[1]

    def fetch(j):
        at = pl.ds(pl.multiple_of(j * BLOCK, BLOCK), BLOCK)
        return pltpu.make_async_copy(bytes_hbm.at[at], held.at[at], sems.at[j])

    def begin(j, carry):
        fetch(j).start()
        return carry

    flags = pltpu.make_async_copy(bnd_hbm, bnd_ref, bnd_sem)
    flags.start()
    lax.fori_loop(0, blocks, begin, 0)
    flags.wait()

    bnd = bnd_ref[...].reshape(lines, 128).astype(F32)
    bnd16 = bnd.astype(BF16)
    inside = dot(bnd16, flag(iota((128, 128), 0) <= iota((128, 128), 1)))
    above = dot(flag(iota((lines, lines), 1) < iota((lines, lines), 0)), bnd16)
    before = jnp.sum(above, axis=1, keepdims=True)
    upto = inside + before
    target[...] = jnp.where(bnd > 0, upto - 1.0, -1.0).astype(I32)
    rank_ref[...] = jnp.concatenate([upto, jnp.zeros((128 - lines, 128), F32)], 0).T
    for j in range(blocks):
        start_ref[j] = before[2 * j, 0].astype(I32)
    count = upto[lines - 1, 127].astype(I32)
    count_ref[...] = jnp.full(count_ref.shape, count, I32)
    rows_ref[0:16, :] = jnp.zeros((16, width), BF16)

    def step(j, carry):
        fetch(j).wait()
        base = pl.multiple_of((start_ref[j] // 16) * 16, 16)
        places = iota((SPAN, 128), 0) + base
        left = places == target[pl.ds(2 * j, 1), :]
        right = places == target[pl.ds(2 * j + 1, 1), :]
        choose = jnp.concatenate([flag(left), flag(right)], 1)
        here = pl.ds(pl.multiple_of(j * BLOCK, BLOCK), BLOCK)
        piece = min(512, width)
        for c in range(0, width, piece):
            cols = pl.ds(c, piece)
            picked = dot(choose, held[here, cols]).astype(BF16)
            rows_ref[pl.ds(base, 16), cols] = rows_ref[pl.ds(base, 16), cols] + picked[:16]
            rows_ref[pl.ds(pl.multiple_of(base + 16, 16), BLOCK), cols] = picked[16:]
        return carry

    lax.fori_loop(0, blocks, step, 0)

    clear = (start_ref[blocks - 1] // 16) * 16 + SPAN

    def wipe(i, carry):
        rows_ref[pl.ds(pl.multiple_of(clear + 16 * i, 16), 16), :] = jnp.zeros((16, width), BF16)
        return carry

    lax.fori_loop(0, jnp.maximum(groups + 32 - clear, 0) // 16, wipe, 0)
    near = pl.multiple_of((jnp.maximum(count - 4, 0) // 16) * 16, 16)
    row, column = iota((16, 32), 0), iota((16, 32), 1)
    wanted = count - 16 + row
    choose = flag((row >= 12) & (wanted >= 0) & (column + near == wanted))
    last = dot(choose, rows_ref[pl.ds(near, 32), :])
    few = jnp.minimum(count, 4).astype(F32)
    tail_ref[...] = jnp.where(iota(last.shape, 0) == 0, few, last).astype(BF16)


def compact(boundary, byte_rows, groups):
    length, width = byte_rows.shape
    blocks = length // BLOCK
    vmem = pl.BlockSpec(memory_space=pltpu.VMEM)
    return pl.pallas_call(
        functools.partial(compact_kernel, groups),
        out_shape=[
            on_chip((groups + SPAN, width), BF16),
            on_chip((16, width), BF16),
            on_chip((8, 128), I32),
            on_chip((128, 128), F32),
            jax.ShapeDtypeStruct((blocks,), I32),
        ],
        in_specs=[pl.BlockSpec(memory_space=pltpu.HBM)] * 2,
        out_specs=[vmem, vmem, vmem, vmem, pl.BlockSpec(memory_space=pltpu.SMEM)],
        scratch_shapes=[
            pltpu.VMEM((length, width), BF16),
            pltpu.VMEM((2 * blocks, 128), I32),
            pltpu.VMEM((length,), I32),
            pltpu.SemaphoreType.DMA((blocks,)),
            pltpu.SemaphoreType.DMA,
        ],
        compiler_params=pltpu.CompilerParams(vmem_limit_bytes=30 << 20),
        cost_estimate=pl.CostEstimate(
            flops=2 * SPAN * length * width, bytes_accessed=2 * length * width, transcendentals=0
        ),
    )(boundary, byte_rows)


def head_column(ref, shape):
    head = iota(shape, 0) % HEADS_HERE
    out = jnp.zeros(shape, F32)
    for h in range(HEADS_HERE):
        out = jnp.where(head == h, ref[h], out)
    return out


def layer_kernel(
    n_ctx,
    n_head,
    groups,
    rows_ref,
    tail_ref,
    count_ref,
    value_ref,
    gate_ref,
    state_ref,
    step_ref,
    vconv_ref,
    vshift_ref,
    sconv_ref,
    sshift_ref,
    bias_ref,
    log_ref,
    skip_ref,
    table,
    inv_ref,
    ext_a,
    ext_b,
    ext_h,
    taps,
    xs,
    maps,
    mix,
    open_gate,
    grow,
    locs,
    fades,
    raw_step,
    lead_t,
    lead_e,
    minus,
    sel_d,
    sel_e,
    near,
    halo_gate,
    ends_out,
    ends_in,
    out_slices,
    in_slices,
    ret_out,
    ret_in,
    entry,
    squares,
    near_send,
    near_recv,
    end_send,
    end_recv,
    out_send,
    out_recv,
    ret_send,
    ret_recv,
    sq_send,
    sq_recv,
):
    me = lax.axis_index("ctx")
    column = lax.axis_index("head")
    subs = groups // T
    share = STATE * 4 // n_ctx
    big = 2 * T
    bigs = groups // big

    barrier = pltpu.get_barrier_semaphore()

    def greet_ctx(d, carry):
        pl.semaphore_signal(
            barrier, inc=1, device_id={"ctx": lax.rem(me + d, n_ctx)}, device_id_type=MESH
        )
        return carry

    def greet_head(d, carry):
        pl.semaphore_signal(
            barrier, inc=1, device_id={"head": lax.rem(column + d, n_head)}, device_id_type=MESH
        )
        return carry

    lax.fori_loop(1, n_ctx, greet_ctx, 0)
    lax.fori_loop(1, n_head, greet_head, 0)

    def near_copy(d):
        return pltpu.make_async_remote_copy(
            src_ref=tail_ref,
            dst_ref=near.at[d - 1],
            send_sem=near_send.at[d - 1],
            recv_sem=near_recv.at[d - 1],
            device_id={"ctx": lax.rem(me + d, n_ctx)},
            device_id_type=MESH,
        )

    def end_copy(d):
        to = lax.rem(me + d, n_ctx)
        return pltpu.make_async_remote_copy(
            src_ref=ends_out.at[lax.rem(to, 4)],
            dst_ref=ends_in.at[me],
            send_sem=end_send.at[d],
            recv_sem=end_recv.at[d],
            device_id={"ctx": to},
            device_id_type=MESH,
        )

    def out_copy(d):
        to = lax.rem(me + d, n_ctx)
        return pltpu.make_async_remote_copy(
            src_ref=out_slices.at[to],
            dst_ref=in_slices.at[me],
            send_sem=out_send.at[d],
            recv_sem=out_recv.at[d],
            device_id={"ctx": to},
            device_id_type=MESH,
        )

    def ret_copy(d):
        to = lax.rem(me + d, n_ctx)
        return pltpu.make_async_remote_copy(
            src_ref=ret_out.at[to],
            dst_ref=ret_in.at[me],
            send_sem=ret_send.at[d],
            recv_sem=ret_recv.at[d],
            device_id={"ctx": to},
            device_id_type=MESH,
        )

    def sq_copy(d):
        return pltpu.make_async_remote_copy(
            src_ref=squares.at[column],
            dst_ref=squares.at[column],
            send_sem=sq_send.at[d],
            recv_sem=sq_recv.at[d],
            device_id={"head": lax.rem(column + d, n_head)},
            device_id_type=MESH,
        )

    def start_all(copy, count):
        lax.fori_loop(1, count, lambda d, c: (copy(d).start(), c)[1], 0)

    def wait_all(copy, count):
        lax.fori_loop(1, count, lambda d, c: (copy(d).wait(), c)[1], 0)

    for i in range(groups // 512):
        got = dot_nt(step_ref[...], rows_ref[i * 512 : (i + 1) * 512, :])
        for q in range(4):
            k = i * 4 + q
            raw_step[k * 8 : (k + 1) * 8, :] = got[:, q * T : (q + 1) * T]

    pl.semaphore_wait(barrier, n_ctx - 1 + n_head - 1)
    near_copy(1).start()
    near_copy(2).start()

    shape = (subs * 8, T)
    raw = raw_step[...] + head_column(bias_ref, shape)
    soft = jnp.maximum(raw, 0.0) + jnp.log1p(jnp.exp(-jnp.abs(raw)))
    valid = (iota(shape, 0) // 8) * T + iota(shape, 1) < count_ref[0:1, :]
    step = jnp.where(valid, soft, 0.0)
    logs = jnp.where(valid, jnp.maximum(jnp.log(soft), LOG_FLOOR), LOG_FLOOR)
    decay = -step * jnp.exp(head_column(log_ref, shape))
    tri = flag(iota((T, T), 0) <= iota((T, T), 1))
    d0, d1, d2 = pieces(decay, 3)
    cum = (dot(d0.astype(BF16), tri) + dot(d1.astype(BF16), tri)) + dot(d2.astype(BF16), tri)
    total = jnp.broadcast_to(cum[:, T - 1 : T], shape)
    cums = pieces(cum, 3)
    lows = pieces(logs - cum, 3)
    grows = pieces(jnp.exp(cum), 2)
    tails = pieces(jnp.exp(total - cum) * step, 2)

    over = total[0:8]
    for k in range(1, subs):
        over = over + total[k * 8 : (k + 1) * 8]
    high, low = pieces(jnp.exp(over), 2)
    first_half = iota((8, T), 1) < HEAD_DIM
    for c in range(4):
        both = [
            jnp.where(
                first_half,
                jnp.broadcast_to(part[2 * c : 2 * c + 1], (8, T)),
                jnp.broadcast_to(part[2 * c + 1 : 2 * c + 2], (8, T)),
            )
            for part in (high, low)
        ]
        ends_out[c] = jnp.concatenate(both, 0).astype(BF16)
    ends_in[me] = ends_out[lax.rem(me, 4)]
    start_all(end_copy, n_ctx)

    for k in range(subs):
        at = slice(k * 8, (k + 1) * 8)
        lead_t[k] = jnp.concatenate([p[at] for p in cums] + [jnp.ones((24, T), F32)], 0).astype(BF16)
        lead_e[k] = jnp.concatenate([p[at] for p in grows + tails], 0).astype(BF16)
        minus[k] = jnp.concatenate([p[at] for p in lows], 0)
    head_of = iota((24, 8 * T), 0) % 8
    sel_d[...] = flag(head_of == iota((24, 8 * T), 1) // T).astype(F32)
    row, lane = iota((32, 2 * WIDE), 0), iota((32, 2 * WIDE), 1)
    sel_e[...] = flag((row % 8 == (lane % WIDE) // HEAD_DIM) & ((row < 16) == (lane < WIDE)))
    for c in range(6):
        tap, move, at = (
            (vconv_ref, vshift_ref, slice(c * 128, (c + 1) * 128))
            if c < 4
            else (sconv_ref, sshift_ref, slice((c - 4) * 128, (c - 3) * 128))
        )
        taps[c, 0:4, :] = 0.5 * tap[:, at]
        taps[c, 4:5, :] = 0.5 * move[:, at]

    def weights_of(n):
        return value_ref[:, n * 256 : (n + 1) * 256] if n < 2 else state_ref[...]

    def project(block, ext, n):
        here = pl.ds(pl.multiple_of(block * big, big), big)
        got = dot(rows_ref[here, :], weights_of(n))
        ext[2 * n, 8 : 8 + big, :] = got[:, :128]
        ext[2 * n + 1, 8 : 8 + big, :] = got[:, 128:]

    def convolve(ext, c, at, length):
        h = taps[c, 4:5, :] + taps[c, 0:1, :] * ext[c, at + 5 : at + 5 + length, :]
        for j in range(1, 4):
            h = h + taps[c, j : j + 1, :] * ext[c, at + 5 + j : at + 5 + j + length, :]
        return h + h * jnp.tanh(h)

    for n in range(3):
        project(0, ext_a, n)

    near_copy(1).wait()
    near_copy(2).wait()
    first = jnp.where(me >= 1, near[0].astype(F32), 0.0)
    second = jnp.where(me >= 2, near[1].astype(F32), 0.0)
    few = jnp.broadcast_to(near[0][0:1, 0:16].astype(F32), (16, 16))
    few = jnp.where(me >= 1, few, 4.0)
    row, lane = iota((16, 16), 0), iota((16, 16), 1)
    shift = flag((row >= 12) & (lane >= 12) & (lane.astype(F32) == row.astype(F32) + few))
    halo = dot(shift, second.astype(BF16)) + jnp.where(iota(first.shape, 0) >= 12, first, 0.0)
    halo = halo.astype(BF16)
    for n in range(3):
        got = dot(halo, weights_of(n))
        ext_h[2 * n, 8:24, :] = got[:, :128]
        ext_h[2 * n + 1, 8:24, :] = got[:, 128:]
    halo_gate[...] = silu(dot(halo, gate_ref[...]))
    for c in range(6):
        ext_h[c, 0:8, :] = jnp.zeros((8, 128), F32)
        ext_a[c, 0:8, :] = ext_h[c, 16:24, :]
    x_h = jnp.concatenate([convolve(ext_h, c, 0, 16) for c in range(4)], 1)
    c_h = convolve(ext_h, 5, 0, 16).astype(BF16)

    locs[0] = jnp.zeros((STATE, WIDE), F32)
    fades[0] = jnp.ones((1, WIDE), F32)

    def advance(block, ext, onto, target):
        for q in range(2):
            k = block * 2 + q
            at = pl.ds(pl.multiple_of(k * T, T), T)
            if target is not None:
                project(target, onto, 2 * q)
                if q == 0:
                    project(target, onto, 1)
            both = dot_tn(lead_e[k], sel_e[...])
            grow[k] = both[:, :WIDE]
            weighted = []
            for c in range(4):
                x = convolve(ext, c, q * T, T)
                xs[at, c * 128 : (c + 1) * 128] = x.astype(BF16)
                tail = both[:, WIDE + c * 128 : WIDE + (c + 1) * 128]
                weighted.append((x * tail).astype(BF16))
            for c in range(2):
                maps[at, c * 128 : (c + 1) * 128] = convolve(ext, 4 + c, q * T, T).astype(BF16)
            new = dot_tn(maps[at, :STATE], jnp.concatenate(weighted, 1))
            factor = both[T - 1 : T, :WIDE]
            locs[k + 1] = factor * locs[k] + new
            fades[k + 1] = factor * fades[k]

    def hand_on(source, ext):
        for c in range(6):
            ext[c, 0:8, :] = source[c, big : big + 8, :]

    def local(j, carry):
        advance(2 * j, ext_a, ext_b, 2 * j + 1)
        hand_on(ext_a, ext_b)
        advance(2 * j + 1, ext_b, ext_a, 2 * j + 2)
        hand_on(ext_b, ext_a)
        return carry

    lax.fori_loop(0, bigs // 2 - 1, local, 0)
    advance(bigs - 2, ext_a, ext_b, bigs - 1)
    hand_on(ext_a, ext_b)
    advance(bigs - 1, ext_b, None, None)

    for k in range(n_ctx):
        r, c = (k // 4) * share, (k % 4) * 128
        out_slices[k] = locs[subs, r : r + share, c : c + 128].astype(BF16)
    in_slices[me] = out_slices[me]
    start_all(out_copy, n_ctx)

    skip = jnp.zeros((1, WIDE), F32)
    for h in range(HEADS_HERE):
        skip = jnp.where(iota((1, WIDE), 1) // HEAD_DIM == h, skip_ref[h], skip)
    lower = iota((T, T), 1) <= iota((T, T), 0)
    left_half = iota((T, T), 1) < HEAD_DIM

    def inside(i, carry):
        g0 = pl.multiple_of(i * big, big)
        here = pl.ds(g0, big)
        open_gate[here, :] = silu(dot(rows_ref[here, :], gate_ref[...]))
        for q in range(big // T):
            k = i * (big // T) + q
            at = pl.ds(pl.multiple_of(g0 + q * T, T), T)
            x, m = xs[at, :], maps[at, :]
            scores = jnp.where(lower, dot_nt(m[:, STATE:], m[:, :STATE]), 0.0)
            lows = minus[k]
            tile = jnp.concatenate([lows] * HEADS_HERE, 1) * sel_d[...]
            right = jnp.concatenate([sel_d[...], tile], 0).astype(BF16)
            spread = dot_tn(lead_t[k], right)
            weight = jnp.exp(jnp.minimum(spread, 60.0))
            weight = (weight * jnp.concatenate([scores] * HEADS_HERE, 1)).astype(BF16)
            for p in range(HEADS_HERE // 2):
                pair = x[:, p * T : (p + 1) * T]
                stacked = jnp.concatenate(
                    [
                        jnp.where(left_half, pair, jnp.zeros_like(pair)),
                        jnp.where(left_half, jnp.zeros_like(pair), pair),
                    ],
                    0,
                )
                got = dot(weight[:, 2 * p * T : 2 * (p + 1) * T], stacked)
                cols = slice(p * T, (p + 1) * T)
                mix[at, cols] = got + skip[:, cols] * pair.astype(F32)
        return carry

    half = bigs // 2
    lax.fori_loop(0, half, inside, 0)

    wait_all(end_copy, n_ctx)
    wait_all(out_copy, n_ctx)
    running = jnp.zeros((share, 128), F32)
    for i in range(n_ctx):
        ret_out[i] = running.astype(BF16)
        factor = ends_in[i].astype(F32)
        factor = factor[0:1] + factor[8:9]
        running = factor * running + in_slices[i].astype(F32)
    ret_in[me] = ret_out[me]
    start_all(ret_copy, n_ctx)

    lax.fori_loop(half, bigs, inside, 0)

    wait_all(ret_copy, n_ctx)
    for k in range(n_ctx):
        r, c = (k // 4) * share, (k % 4) * 128
        entry[r : r + share, c : c + 128] = ret_in[k]

    ones = jnp.ones((8, WIDE), BF16)
    y_h = dot(c_h, entry[...]) + skip * x_h
    g_h = y_h * halo_gate[...]
    table[0 : T - 16, :] = jnp.zeros((T - 16, WIDE), BF16)
    table[T - 16 : T, :] = g_h.astype(BF16)
    power = jnp.concatenate([jnp.zeros((T - 16, WIDE), F32), g_h * g_h], 0).astype(BF16)
    mine = squares.at[column]
    mine[...] = jnp.zeros(mine.shape, F32)
    mine[0:1, :] = dot_nt(ones, power)[0:1, :]
    entering = entry[...].astype(F32)

    def outer(i, carry):
        for q in range(4):
            k = i * 4 + q
            at = pl.ds(pl.multiple_of(k * T, T), T)
            state = (locs[k] + fades[k] * entering).astype(BF16)
            gated = mix[at, :] + grow[k] * dot(maps[at, STATE:], state)
            gated = gated * open_gate[at, :]
            table[pl.ds(pl.multiple_of((k + 1) * T, T), T), :] = gated.astype(BF16)
            squares[column, pl.ds(k + 1, 1), :] = dot_nt(ones, (gated * gated).astype(BF16))[0:1, :]
        return carry

    lax.fori_loop(0, subs // 4, outer, 0)
    start_all(sq_copy, n_head)

    wait_all(sq_copy, n_head)
    power = squares[0]
    for i in range(1, n_head):
        power = power + squares[i]
    inv_ref[...] = lax.rsqrt(power * (1.0 / (n_head * WIDE)) + EPSILON)


def layer(n_ctx, n_head, groups, *args):
    subs = groups // T
    share = STATE * 4 // n_ctx
    lines = -(-(subs + 1) // 8) * 8
    vmem = pl.BlockSpec(memory_space=pltpu.VMEM)
    smem = pl.BlockSpec(memory_space=pltpu.SMEM)
    width = args[0].shape[1]
    sem = pltpu.SemaphoreType.DMA
    return pl.pallas_call(
        functools.partial(layer_kernel, n_ctx, n_head, groups),
        out_shape=[on_chip((groups + T, WIDE), BF16), on_chip((lines, T), F32)],
        in_specs=[vmem] * 11 + [smem] * 3,
        out_specs=[vmem, vmem],
        scratch_shapes=[
            pltpu.VMEM((6, 2 * T + 8, 128), F32),
            pltpu.VMEM((6, 2 * T + 8, 128), F32),
            pltpu.VMEM((6, 24, 128), F32),
            pltpu.VMEM((6, 8, 128), F32),
            pltpu.VMEM((groups, WIDE), BF16),
            pltpu.VMEM((groups, 2 * STATE), BF16),
            pltpu.VMEM((groups, WIDE), F32),
            pltpu.VMEM((groups, WIDE), F32),
            pltpu.VMEM((subs, T, WIDE), F32),
            pltpu.VMEM((subs + 1, STATE, WIDE), F32),
            pltpu.VMEM((subs + 1, 1, WIDE), F32),
            pltpu.VMEM((subs * 8, T), F32),
            pltpu.VMEM((subs, 48, T), BF16),
            pltpu.VMEM((subs, 32, T), BF16),
            pltpu.VMEM((subs, 24, T), F32),
            pltpu.VMEM((24, 8 * T), F32),
            pltpu.VMEM((32, 2 * WIDE), BF16),
            pltpu.VMEM((2, 16, width), BF16),
            pltpu.VMEM((16, WIDE), F32),
            pltpu.VMEM((4, 16, 128), BF16),
            pltpu.VMEM((n_ctx, 16, 128), BF16),
            pltpu.VMEM((n_ctx, share, 128), BF16),
            pltpu.VMEM((n_ctx, share, 128), BF16),
            pltpu.VMEM((n_ctx, share, 128), BF16),
            pltpu.VMEM((n_ctx, share, 128), BF16),
            pltpu.VMEM((STATE, WIDE), BF16),
            pltpu.VMEM((n_head, lines, T), F32),
            sem((2,)),
            sem((2,)),
            sem((n_ctx,)),
            sem((n_ctx,)),
            sem((n_ctx,)),
            sem((n_ctx,)),
            sem((n_ctx,)),
            sem((n_ctx,)),
            sem((n_head,)),
            sem((n_head,)),
        ],
        compiler_params=pltpu.CompilerParams(
            collective_id=0, has_side_effects=True, vmem_limit_bytes=32 << 20
        ),
        cost_estimate=pl.CostEstimate(
            flops=2 * groups * width * 1536, bytes_accessed=8 << 20, transcendentals=1 << 22
        ),
    )(*args)


def expand_kernel(
    groups, start_ref, rank_ref, table_ref, inv_ref, gain_ref, out_hbm, ready, sems
):
    blocks = out_hbm.shape[0] // BLOCK
    window = min(3 * T, groups + T)

    def send(j):
        at = pl.ds(pl.multiple_of(j * BLOCK, BLOCK), BLOCK)
        return pltpu.make_async_copy(ready.at[at], out_hbm.at[at], sems.at[j])

    def step(j, carry):
        line = jnp.minimum((start_ref[j] + T - 1) // T, (groups + T - window) // T)
        base = pl.multiple_of(line * T, T)
        lane = iota((T, T), 1)
        places, scales = [], []
        for half in range(2):
            rank = jnp.sum(
                jnp.where(lane == 2 * j + half, rank_ref[...], 0.0), axis=1, keepdims=True
            )
            place = jnp.broadcast_to(rank.astype(I32) + (T - 1) - base, (T, T))
            hits = [place == lane + w * T for w in range(window // T)]
            places.append(jnp.concatenate([flag(hit) for hit in hits], 1))
            scale = jnp.zeros((T, T), F32)
            for w, hit in enumerate(hits):
                scale = jnp.where(hit, inv_ref[pl.ds(line + w, 1), :], scale)
            scales.append(jnp.sum(scale, axis=1, keepdims=True))
        got = dot(jnp.concatenate(places, 0), table_ref[pl.ds(base, window), :])
        got = got * gain_ref[...] * jnp.concatenate(scales, 0)
        ready[pl.ds(pl.multiple_of(j * BLOCK, BLOCK), BLOCK), :] = got
        send(j).start()
        return carry

    def steps(i, carry):
        for q in range(UNROLL):
            step(i * UNROLL + q, 0)
        return carry

    lax.fori_loop(0, blocks // UNROLL, steps, 0)

    def finish(j, carry):
        send(j).wait()
        return carry

    lax.fori_loop(0, blocks, finish, 0)


def expand(length, groups, starts, rank, table, inv, gain):
    vmem = pl.BlockSpec(memory_space=pltpu.VMEM)
    return pl.pallas_call(
        functools.partial(expand_kernel, groups),
        out_shape=jax.ShapeDtypeStruct((length, WIDE), F32),
        in_specs=[pl.BlockSpec(memory_space=pltpu.SMEM), vmem, vmem, vmem, vmem],
        out_specs=pl.BlockSpec(memory_space=pl.ANY),
        scratch_shapes=[
            pltpu.VMEM((length, WIDE), F32),
            pltpu.SemaphoreType.DMA((length // BLOCK,)),
        ],
        compiler_params=pltpu.CompilerParams(vmem_limit_bytes=24 << 20),
        cost_estimate=pl.CostEstimate(
            flops=2 * length * 3 * T * WIDE, bytes_accessed=4 * length * WIDE, transcendentals=0
        ),
    )(starts, rank, table, inv, gain)


def shards(
    groups,
    byte_rows,
    boundary,
    gate_proj,
    value_proj,
    state_proj,
    step_proj,
    step_bias,
    decay_log,
    skip_gain,
    value_conv,
    value_shift,
    state_conv,
    state_shift,
    norm_gain,
):
    n_ctx, n_head = lax.axis_size("ctx"), lax.axis_size("head")
    weights = [keep_on_chip(w) for w in (value_proj, gate_proj, state_proj, step_proj.T)]
    rows, tail, count, rank, starts = compact(
        keep_off_chip(boundary), keep_off_chip(byte_rows), groups
    )
    table, inv = layer(
        n_ctx,
        n_head,
        groups,
        rows,
        tail,
        count,
        *weights,
        value_conv,
        value_shift.reshape(1, -1),
        state_conv,
        state_shift.reshape(1, -1),
        step_bias,
        decay_log,
        skip_gain,
    )
    return expand(byte_rows.shape[0], groups, starts, rank, table, inv, norm_gain.reshape(1, -1))


def solution(mesh, groups=2048):
    placed = (
        P("ctx", None),
        P("ctx"),
        P(None, "head"),
        P(None, "head"),
        P(),
        P(None, "head"),
        P("head"),
        P("head"),
        P("head"),
        P(None, "head"),
        P("head"),
        P(),
        P(),
        P("head"),
    )
    return jax.shard_map(
        functools.partial(shards, groups),
        mesh=mesh,
        in_specs=placed,
        out_specs=P("ctx", "head"),
        check_vma=False,
    )
```

```python
import functools

import jax
import jax.numpy as jnp
from jax import lax
from jax.experimental import pallas as pl
from jax.experimental.pallas import tpu as pltpu
from jax.sharding import PartitionSpec as P

F32 = jnp.float32
BF16 = jnp.bfloat16
I32 = jnp.int32
HEAD_DIM = 64
STATE = 128
HEADS_HERE = 8
WIDE = HEADS_HERE * HEAD_DIM
INNER = 4096
T = 128
BLOCK = 256
SPAN = BLOCK + 16
UNROLL = 3
JOINED = 1
EPSILON = 1e-05
LOG_FLOOR = -1e4
MESH = pl.DeviceIdType.MESH


def on_chip(shape, kind):
    return pltpu.VMEM(shape, kind)


def keep_on_chip(array):
    return pltpu.with_memory_space_constraint(array, pltpu.VMEM)


def keep_off_chip(array):
    return pltpu.with_memory_space_constraint(array, pltpu.HBM)


def dot(a, b):
    return jnp.dot(a, b, preferred_element_type=F32)


def dot_tn(a, b):
    return lax.dot_general(a, b, (((0,), (0,)), ((), ())), preferred_element_type=F32)


def dot_nt(a, b):
    return lax.dot_general(a, b, (((1,), (1,)), ((), ())), preferred_element_type=F32)


def iota(shape, axis):
    return lax.broadcasted_iota(I32, shape, axis)


def silu(v):
    return 0.5 * v * (1.0 + jnp.tanh(0.5 * v))


def flag(condition):
    return jnp.where(condition, 1.0, 0.0).astype(BF16)


def pieces(v, count):
    out = []
    for _ in range(count):
        top = v.astype(BF16).astype(F32)
        out.append(top)
        v = v - top
    return out


def compact_kernel(
    groups,
    bnd_hbm,
    bytes_hbm,
    rows_ref,
    tail_ref,
    count_ref,
    rank_ref,
    start_ref,
    held,
    target,
    bnd_ref,
    sems,
    bnd_sem,
):
    blocks = bytes_hbm.shape[0] // BLOCK
    lines = 2 * blocks
    width = rows_ref.shape[1]

    def fetch(j):
        at = pl.ds(pl.multiple_of(j * BLOCK, BLOCK), BLOCK)
        return pltpu.make_async_copy(bytes_hbm.at[at], held.at[at], sems.at[j])

    def begin(j, carry):
        fetch(j).start()
        return carry

    flags = pltpu.make_async_copy(bnd_hbm, bnd_ref, bnd_sem)
    flags.start()
    lax.fori_loop(0, blocks, begin, 0)
    flags.wait()

    bnd = bnd_ref[...].reshape(lines, 128).astype(F32)
    bnd16 = bnd.astype(BF16)
    inside = dot(bnd16, flag(iota((128, 128), 0) <= iota((128, 128), 1)))
    above = dot(flag(iota((lines, lines), 1) < iota((lines, lines), 0)), bnd16)
    before = jnp.sum(above, axis=1, keepdims=True)
    upto = inside + before
    target[...] = jnp.where(bnd > 0, upto - 1.0, -1.0).astype(I32)
    rank_ref[...] = jnp.concatenate([upto, jnp.zeros((128 - lines, 128), F32)], 0).T
    for j in range(blocks):
        start_ref[j] = before[2 * j, 0].astype(I32)
    count = upto[lines - 1, 127].astype(I32)
    count_ref[...] = jnp.full(count_ref.shape, count, I32)
    rows_ref[0:16, :] = jnp.zeros((16, width), BF16)

    def step(j, carry):
        fetch(j).wait()
        base = pl.multiple_of((start_ref[j] // 16) * 16, 16)
        places = iota((SPAN, 128), 0) + base
        left = places == target[pl.ds(2 * j, 1), :]
        right = places == target[pl.ds(2 * j + 1, 1), :]
        choose = jnp.concatenate([flag(left), flag(right)], 1)
        here = pl.ds(pl.multiple_of(j * BLOCK, BLOCK), BLOCK)
        piece = min(512, width)
        for c in range(0, width, piece):
            cols = pl.ds(c, piece)
            picked = dot(choose, held[here, cols]).astype(BF16)
            rows_ref[pl.ds(base, 16), cols] = rows_ref[pl.ds(base, 16), cols] + picked[:16]
            rows_ref[pl.ds(pl.multiple_of(base + 16, 16), BLOCK), cols] = picked[16:]
        return carry

    def steps(i, carry):
        for q in range(JOINED):
            step(i * JOINED + q, 0)
        return carry

    lax.fori_loop(0, blocks // JOINED, steps, 0)

    clear = (start_ref[blocks - 1] // 16) * 16 + SPAN

    def wipe(i, carry):
        rows_ref[pl.ds(pl.multiple_of(clear + 16 * i, 16), 16), :] = jnp.zeros((16, width), BF16)
        return carry

    lax.fori_loop(0, jnp.maximum(groups + 32 - clear, 0) // 16, wipe, 0)
    near = pl.multiple_of((jnp.maximum(count - 4, 0) // 16) * 16, 16)
    row, column = iota((16, 32), 0), iota((16, 32), 1)
    wanted = count - 16 + row
    choose = flag((row >= 12) & (wanted >= 0) & (column + near == wanted))
    last = dot(choose, rows_ref[pl.ds(near, 32), :])
    few = jnp.minimum(count, 4).astype(F32)
    tail_ref[...] = jnp.where(iota(last.shape, 0) == 0, few, last).astype(BF16)


def compact(boundary, byte_rows, groups):
    length, width = byte_rows.shape
    blocks = length // BLOCK
    vmem = pl.BlockSpec(memory_space=pltpu.VMEM)
    return pl.pallas_call(
        functools.partial(compact_kernel, groups),
        out_shape=[
            on_chip((groups + SPAN, width), BF16),
            on_chip((16, width), BF16),
            on_chip((8, 128), I32),
            on_chip((128, 128), F32),
            jax.ShapeDtypeStruct((blocks,), I32),
        ],
        in_specs=[pl.BlockSpec(memory_space=pltpu.HBM)] * 2,
        out_specs=[vmem, vmem, vmem, vmem, pl.BlockSpec(memory_space=pltpu.SMEM)],
        scratch_shapes=[
            pltpu.VMEM((length, width), BF16),
            pltpu.VMEM((2 * blocks, 128), I32),
            pltpu.VMEM((length,), I32),
            pltpu.SemaphoreType.DMA((blocks,)),
            pltpu.SemaphoreType.DMA,
        ],
        compiler_params=pltpu.CompilerParams(vmem_limit_bytes=30 << 20),
        cost_estimate=pl.CostEstimate(
            flops=2 * SPAN * length * width, bytes_accessed=2 * length * width, transcendentals=0
        ),
    )(boundary, byte_rows)


def head_column(ref, shape):
    head = iota(shape, 0) % HEADS_HERE
    out = jnp.zeros(shape, F32)
    for h in range(HEADS_HERE):
        out = jnp.where(head == h, ref[h], out)
    return out


def layer_kernel(
    n_ctx,
    n_head,
    groups,
    rows_ref,
    tail_ref,
    count_ref,
    value_ref,
    gate_ref,
    state_ref,
    step_ref,
    vconv_ref,
    vshift_ref,
    sconv_ref,
    sshift_ref,
    bias_ref,
    log_ref,
    skip_ref,
    table,
    inv_ref,
    ext_0,
    ext_a,
    ext_b,
    ext_h,
    taps,
    xs,
    maps,
    mix,
    open_gate,
    grow,
    locs,
    fades,
    raw_step,
    lead_t,
    lead_e,
    minus,
    sel_d,
    sel_e,
    near,
    halo_gate,
    ends_out,
    ends_in,
    out_slices,
    in_slices,
    ret_out,
    ret_in,
    entry,
    base,
    squares,
    near_send,
    near_recv,
    end_send,
    end_recv,
    out_send,
    out_recv,
    ret_send,
    ret_recv,
    sq_send,
    sq_recv,
):
    me = lax.axis_index("ctx")
    column = lax.axis_index("head")
    subs = groups // T
    share = STATE * 4 // n_ctx
    big = 2 * T
    bigs = groups // big

    barrier = pltpu.get_barrier_semaphore()

    def greet_ctx(d, carry):
        pl.semaphore_signal(
            barrier, inc=1, device_id={"ctx": lax.rem(me + d, n_ctx)}, device_id_type=MESH
        )
        return carry

    def greet_head(d, carry):
        pl.semaphore_signal(
            barrier, inc=1, device_id={"head": lax.rem(column + d, n_head)}, device_id_type=MESH
        )
        return carry

    lax.fori_loop(1, n_ctx, greet_ctx, 0)
    lax.fori_loop(1, n_head, greet_head, 0)

    def near_copy(d):
        return pltpu.make_async_remote_copy(
            src_ref=tail_ref,
            dst_ref=near.at[d - 1],
            send_sem=near_send.at[d - 1],
            recv_sem=near_recv.at[d - 1],
            device_id={"ctx": lax.rem(me + d, n_ctx)},
            device_id_type=MESH,
        )

    def end_copy(d):
        to = lax.rem(me + d, n_ctx)
        return pltpu.make_async_remote_copy(
            src_ref=ends_out.at[lax.rem(to, 4)],
            dst_ref=ends_in.at[me],
            send_sem=end_send,
            recv_sem=end_recv,
            device_id={"ctx": to},
            device_id_type=MESH,
        )

    def out_copy(d):
        to = lax.rem(me + d, n_ctx)
        return pltpu.make_async_remote_copy(
            src_ref=out_slices.at[to],
            dst_ref=in_slices.at[me],
            send_sem=out_send,
            recv_sem=out_recv,
            device_id={"ctx": to},
            device_id_type=MESH,
        )

    def ret_copy(d):
        to = lax.rem(me + d, n_ctx)
        return pltpu.make_async_remote_copy(
            src_ref=ret_out.at[to],
            dst_ref=ret_in.at[me],
            send_sem=ret_send,
            recv_sem=ret_recv,
            device_id={"ctx": to},
            device_id_type=MESH,
        )

    def sq_copy(d):
        return pltpu.make_async_remote_copy(
            src_ref=squares.at[column],
            dst_ref=squares.at[column],
            send_sem=sq_send,
            recv_sem=sq_recv,
            device_id={"head": lax.rem(column + d, n_head)},
            device_id_type=MESH,
        )

    def start_all(copy, count):
        lax.fori_loop(1, count, lambda d, c: (copy(d).start(), c)[1], 0)

    def wait_all(sent, send_sem, landed, recv_sem):
        for ref, sem in ((sent, send_sem), (landed, recv_sem)):
            both = ref.at[pl.ds(0, landed.shape[0] - 1)]
            pltpu.make_async_copy(both, both, sem).wait()

    for i in range(groups // 512):
        got = dot_nt(step_ref[...], rows_ref[i * 512 : (i + 1) * 512, :])
        for q in range(4):
            k = i * 4 + q
            raw_step[k * 8 : (k + 1) * 8, :] = got[:, q * T : (q + 1) * T]

    pl.semaphore_wait(barrier, n_ctx - 1 + n_head - 1)
    near_copy(1).start()
    near_copy(2).start()

    shape = (subs * 8, T)
    raw = raw_step[...] + head_column(bias_ref, shape)
    soft = jnp.maximum(raw, 0.0) + jnp.log1p(jnp.exp(-jnp.abs(raw)))
    valid = (iota(shape, 0) // 8) * T + iota(shape, 1) < count_ref[0:1, :]
    step = jnp.where(valid, soft, 0.0)
    logs = jnp.where(valid, jnp.maximum(jnp.log(soft), LOG_FLOOR), LOG_FLOOR)
    decay = -step * jnp.exp(head_column(log_ref, shape))
    tri = flag(iota((T, T), 0) <= iota((T, T), 1))
    d0, d1, d2 = pieces(decay, 3)
    cum = (dot(d0.astype(BF16), tri) + dot(d1.astype(BF16), tri)) + dot(d2.astype(BF16), tri)
    total = jnp.broadcast_to(cum[:, T - 1 : T], shape)
    cums = pieces(cum, 3)
    lows = pieces(logs - cum, 3)
    grows = pieces(jnp.exp(cum), 2)
    tails = pieces(jnp.exp(total - cum) * step, 2)

    over = total[0:8]
    for k in range(1, subs):
        over = over + total[k * 8 : (k + 1) * 8]
    high, low = pieces(jnp.exp(over), 2)
    first_half = iota((8, T), 1) < HEAD_DIM
    for c in range(4):
        both = [
            jnp.where(
                first_half,
                jnp.broadcast_to(part[2 * c : 2 * c + 1], (8, T)),
                jnp.broadcast_to(part[2 * c + 1 : 2 * c + 2], (8, T)),
            )
            for part in (high, low)
        ]
        ends_out[c] = jnp.concatenate(both, 0).astype(BF16)
    ends_in[me] = ends_out[lax.rem(me, 4)]
    start_all(end_copy, n_ctx)

    for k in range(subs):
        at = slice(k * 8, (k + 1) * 8)
        lead_t[k] = jnp.concatenate([p[at] for p in cums] + [jnp.ones((24, T), F32)], 0).astype(BF16)
        lead_e[k] = jnp.concatenate([p[at] for p in grows + tails], 0).astype(BF16)
        minus[k] = jnp.concatenate([p[at] for p in lows], 0)
    head_of = iota((24, 8 * T), 0) % 8
    sel_d[...] = flag(head_of == iota((24, 8 * T), 1) // T).astype(F32)
    row, lane = iota((32, 2 * WIDE), 0), iota((32, 2 * WIDE), 1)
    sel_e[...] = flag((row % 8 == (lane % WIDE) // HEAD_DIM) & ((row < 16) == (lane < WIDE)))
    for c in range(6):
        tap, move, at = (
            (vconv_ref, vshift_ref, slice(c * 128, (c + 1) * 128))
            if c < 4
            else (sconv_ref, sshift_ref, slice((c - 4) * 128, (c - 3) * 128))
        )
        taps[c, 0:4, :] = 0.5 * tap[:, at]
        taps[c, 4:5, :] = 0.5 * move[:, at]

    def project(block, ext):
        here = pl.ds(pl.multiple_of(block * big, big), big)
        for weights, first, count in ((value_ref, 0, 4), (state_ref, 4, 2)):
            got = dot(rows_ref[here, :], weights[...])
            for c in range(count):
                ext[first + c, 8 : 8 + big, :] = got[:, c * 128 : (c + 1) * 128]

    def convolve(ext, c, at, length):
        h = taps[c, 4:5, :] + taps[c, 0:1, :] * ext[c, at + 5 : at + 5 + length, :]
        for j in range(1, 4):
            h = h + taps[c, j : j + 1, :] * ext[c, at + 5 + j : at + 5 + j + length, :]
        return h + h * jnp.tanh(h)

    for k in (0, 2):
        locs[k] = jnp.zeros((STATE, WIDE), F32)
        fades[k] = jnp.ones((1, WIDE), F32)

    def advance(block, ext, onto, target):
        both = [dot_tn(lead_e[block * 2 + q], sel_e[...]) for q in range(2)]
        if target is not None:
            project(target, onto)
        for q in range(2):
            k = block * 2 + q
            at = pl.ds(pl.multiple_of(k * T, T), T)
            grow[k] = both[q][:, :WIDE]
            weighted = []
            for c in range(4):
                x = convolve(ext, c, q * T, T)
                xs[at, c * 128 : (c + 1) * 128] = x.astype(BF16)
                tail = both[q][:, WIDE + c * 128 : WIDE + (c + 1) * 128]
                weighted.append((x * tail).astype(BF16))
            for c in range(2):
                maps[at, c * 128 : (c + 1) * 128] = convolve(ext, 4 + c, q * T, T).astype(BF16)
            new = dot_tn(maps[at, :STATE], jnp.concatenate(weighted, 1))
            factor = both[q][T - 1 : T, :WIDE]
            locs[k + 1] = factor * locs[k] + new
            fades[k + 1] = factor * fades[k]

    def hand_on(source, ext):
        for c in range(6):
            ext[c, 0:8, :] = source[c, big : big + 8, :]

    def local(j, carry):
        advance(2 * j + 1, ext_a, ext_b, 2 * j + 2)
        hand_on(ext_a, ext_b)
        advance(2 * j + 2, ext_b, ext_a, 2 * j + 3)
        hand_on(ext_b, ext_a)
        return carry

    project(0, ext_0)
    project(1, ext_a)
    hand_on(ext_0, ext_a)
    lax.fori_loop(0, bigs // 2 - 1, local, 0)

    near_copy(1).wait()
    near_copy(2).wait()
    first = jnp.where(me >= 1, near[0].astype(F32), 0.0)
    second = jnp.where(me >= 2, near[1].astype(F32), 0.0)
    few = jnp.broadcast_to(near[0][0:1, 0:16].astype(F32), (16, 16))
    few = jnp.where(me >= 1, few, 4.0)
    row, lane = iota((16, 16), 0), iota((16, 16), 1)
    shift = flag((row >= 12) & (lane >= 12) & (lane.astype(F32) == row.astype(F32) + few))
    halo = dot(shift, second.astype(BF16)) + jnp.where(iota(first.shape, 0) >= 12, first, 0.0)
    halo = halo.astype(BF16)
    for weights, first, count in ((value_ref, 0, 4), (state_ref, 4, 2)):
        got = dot(halo, weights[...])
        for c in range(count):
            ext_h[first + c, 8:24, :] = got[:, c * 128 : (c + 1) * 128]
    halo_gate[...] = silu(dot(halo, gate_ref[...]))
    for c in range(6):
        ext_h[c, 0:8, :] = jnp.zeros((8, 128), F32)
        ext_0[c, 0:8, :] = ext_h[c, 16:24, :]
    advance(bigs - 1, ext_a, None, None)
    advance(0, ext_0, None, None)
    x_h = jnp.concatenate([convolve(ext_h, c, 0, 16) for c in range(4)], 1)
    c_h = convolve(ext_h, 5, 0, 16).astype(BF16)

    locs[subs] = locs[subs] + fades[subs] * locs[2]

    for k in range(n_ctx):
        r, c = (k // 4) * share, (k % 4) * 128
        out_slices[k] = locs[subs, r : r + share, c : c + 128].astype(BF16)
    in_slices[me] = out_slices[me]
    start_all(out_copy, n_ctx)

    skip = jnp.zeros((1, WIDE), F32)
    for h in range(HEADS_HERE):
        skip = jnp.where(iota((1, WIDE), 1) // HEAD_DIM == h, skip_ref[h], skip)
    lower = iota((T, T), 1) <= iota((T, T), 0)
    left_half = iota((T, T), 1) < HEAD_DIM

    def inside(i, carry):
        g0 = pl.multiple_of(i * big, big)
        here = pl.ds(g0, big)
        parts = []
        for q in range(big // T):
            k = i * (big // T) + q
            at = pl.ds(pl.multiple_of(g0 + q * T, T), T)
            m = maps[at, :]
            scores = jnp.where(lower, dot_nt(m[:, STATE:], m[:, :STATE]), 0.0)
            tile = jnp.concatenate([minus[k]] * HEADS_HERE, 1) * sel_d[...]
            right = jnp.concatenate([sel_d[...], tile], 0).astype(BF16)
            parts.append((at, scores, dot_tn(lead_t[k], right)))
        opened = dot(rows_ref[here, :], gate_ref[...])
        for at, scores, spread in parts:
            x = xs[at, :]
            for p in range(HEADS_HERE // 2):
                pair = x[:, p * T : (p + 1) * T]
                weight = jnp.exp(jnp.minimum(spread[:, 2 * p * T : 2 * (p + 1) * T], 60.0))
                weight = (weight * jnp.concatenate([scores, scores], 1)).astype(BF16)
                stacked = jnp.concatenate(
                    [
                        jnp.where(left_half, pair, jnp.zeros_like(pair)),
                        jnp.where(left_half, jnp.zeros_like(pair), pair),
                    ],
                    0,
                )
                got = dot(weight, stacked)
                cols = slice(p * T, (p + 1) * T)
                mix[at, cols] = got + skip[:, cols] * pair.astype(F32)
        open_gate[here, :] = silu(opened)
        return carry

    half = bigs // 2
    lax.fori_loop(0, half, inside, 0)

    wait_all(ends_in, end_send, ends_in, end_recv)
    wait_all(out_slices, out_send, in_slices, out_recv)
    running = jnp.zeros((share, 128), F32)
    for i in range(n_ctx):
        ret_out[i] = running.astype(BF16)
        factor = ends_in[i].astype(F32)
        factor = factor[0:1] + factor[8:9]
        running = factor * running + in_slices[i].astype(F32)
    ret_in[me] = ret_out[me]
    start_all(ret_copy, n_ctx)

    lax.fori_loop(half, bigs, inside, 0)

    wait_all(ret_out, ret_send, ret_in, ret_recv)
    for k in range(n_ctx):
        r, c = (k // 4) * share, (k % 4) * 128
        entry[r : r + share, c : c + 128] = ret_in[k]

    ones = jnp.ones((8, WIDE), BF16)
    y_h = dot(c_h, entry[...]) + skip * x_h
    g_h = y_h * halo_gate[...]
    table[0 : T - 16, :] = jnp.zeros((T - 16, WIDE), BF16)
    table[T - 16 : T, :] = g_h.astype(BF16)
    power = jnp.concatenate([jnp.zeros((T - 16, WIDE), F32), g_h * g_h], 0).astype(BF16)
    mine = squares.at[column]
    mine[...] = jnp.zeros(mine.shape, F32)
    mine[0:1, :] = dot_nt(ones, power)[0:1, :]
    base[0] = entry[...].astype(F32)
    base[1] = locs[2] + fades[2] * base[0]

    def outer(i, carry):
        for q in range(4):
            k = i * 4 + q
            at = pl.ds(pl.multiple_of(k * T, T), T)
            state = (locs[k] + fades[k] * base[jnp.where(k > 2, 1, 0)]).astype(BF16)
            gated = mix[at, :] + grow[k] * dot(maps[at, STATE:], state)
            gated = gated * open_gate[at, :]
            table[pl.ds(pl.multiple_of((k + 1) * T, T), T), :] = gated.astype(BF16)
            squares[column, pl.ds(k + 1, 1), :] = dot_nt(ones, (gated * gated).astype(BF16))[0:1, :]
        return carry

    lax.fori_loop(0, subs // 4, outer, 0)
    start_all(sq_copy, n_head)

    wait_all(squares, sq_send, squares, sq_recv)
    power = squares[0]
    for i in range(1, n_head):
        power = power + squares[i]
    inv_ref[...] = lax.rsqrt(power * (1.0 / (n_head * WIDE)) + EPSILON)


def layer(n_ctx, n_head, groups, *args):
    subs = groups // T
    share = STATE * 4 // n_ctx
    lines = -(-(subs + 1) // 8) * 8
    vmem = pl.BlockSpec(memory_space=pltpu.VMEM)
    smem = pl.BlockSpec(memory_space=pltpu.SMEM)
    width = args[0].shape[1]
    sem = pltpu.SemaphoreType.DMA
    return pl.pallas_call(
        functools.partial(layer_kernel, n_ctx, n_head, groups),
        out_shape=[on_chip((groups + T, WIDE), BF16), on_chip((lines, T), F32)],
        in_specs=[vmem] * 11 + [smem] * 3,
        out_specs=[vmem, vmem],
        scratch_shapes=[
            pltpu.VMEM((6, 2 * T + 8, 128), F32),
            pltpu.VMEM((6, 2 * T + 8, 128), F32),
            pltpu.VMEM((6, 2 * T + 8, 128), F32),
            pltpu.VMEM((6, 24, 128), F32),
            pltpu.VMEM((6, 8, 128), F32),
            pltpu.VMEM((groups, WIDE), BF16),
            pltpu.VMEM((groups, 2 * STATE), BF16),
            pltpu.VMEM((groups, WIDE), F32),
            pltpu.VMEM((groups, WIDE), F32),
            pltpu.VMEM((subs, T, WIDE), F32),
            pltpu.VMEM((subs + 1, STATE, WIDE), F32),
            pltpu.VMEM((subs + 1, 1, WIDE), F32),
            pltpu.VMEM((subs * 8, T), F32),
            pltpu.VMEM((subs, 48, T), BF16),
            pltpu.VMEM((subs, 32, T), BF16),
            pltpu.VMEM((subs, 24, T), F32),
            pltpu.VMEM((24, 8 * T), F32),
            pltpu.VMEM((32, 2 * WIDE), BF16),
            pltpu.VMEM((2, 16, width), BF16),
            pltpu.VMEM((16, WIDE), F32),
            pltpu.VMEM((4, 16, 128), BF16),
            pltpu.VMEM((n_ctx, 16, 128), BF16),
            pltpu.VMEM((n_ctx, share, 128), BF16),
            pltpu.VMEM((n_ctx, share, 128), BF16),
            pltpu.VMEM((n_ctx, share, 128), BF16),
            pltpu.VMEM((n_ctx, share, 128), BF16),
            pltpu.VMEM((STATE, WIDE), BF16),
            pltpu.VMEM((2, STATE, WIDE), F32),
            pltpu.VMEM((n_head, lines, T), F32),
            sem((2,)),
            sem((2,)),
            sem,
            sem,
            sem,
            sem,
            sem,
            sem,
            sem,
            sem,
        ],
        compiler_params=pltpu.CompilerParams(
            collective_id=0, has_side_effects=True, vmem_limit_bytes=32 << 20
        ),
        cost_estimate=pl.CostEstimate(
            flops=2 * groups * width * 1536, bytes_accessed=8 << 20, transcendentals=1 << 22
        ),
    )(*args)


def expand_kernel(
    groups, start_ref, rank_ref, table_ref, inv_ref, gain_ref, out_hbm, ready, sems
):
    blocks = out_hbm.shape[0] // BLOCK
    window = min(3 * T, groups + T)

    def send(j):
        at = pl.ds(pl.multiple_of(j * BLOCK, BLOCK), BLOCK)
        return pltpu.make_async_copy(ready.at[at], out_hbm.at[at], sems.at[j])

    def step(j, carry):
        line = jnp.minimum((start_ref[j] + T - 1) // T, (groups + T - window) // T)
        base = pl.multiple_of(line * T, T)
        lane = iota((T, T), 1)
        places, scales = [], []
        for half in range(2):
            rank = jnp.sum(
                jnp.where(lane == 2 * j + half, rank_ref[...], 0.0), axis=1, keepdims=True
            )
            place = jnp.broadcast_to(rank.astype(I32) + (T - 1) - base, (T, T))
            hits = [place == lane + w * T for w in range(window // T)]
            places.append(jnp.concatenate([flag(hit) for hit in hits], 1))
            scale = jnp.zeros((T, T), F32)
            for w, hit in enumerate(hits):
                scale = jnp.where(hit, inv_ref[pl.ds(line + w, 1), :], scale)
            scales.append(jnp.sum(scale, axis=1, keepdims=True))
        got = dot(jnp.concatenate(places, 0), table_ref[pl.ds(base, window), :])
        got = got * gain_ref[...] * jnp.concatenate(scales, 0)
        ready[pl.ds(pl.multiple_of(j * BLOCK, BLOCK), BLOCK), :] = got
        send(j).start()
        return carry

    def steps(i, carry):
        for q in range(UNROLL):
            step(i * UNROLL + q, 0)
        return carry

    lax.fori_loop(0, blocks // UNROLL, steps, 0)

    def finish(j, carry):
        send(j).wait()
        return carry

    lax.fori_loop(0, blocks, finish, 0)


def expand(length, groups, starts, rank, table, inv, gain):
    vmem = pl.BlockSpec(memory_space=pltpu.VMEM)
    return pl.pallas_call(
        functools.partial(expand_kernel, groups),
        out_shape=jax.ShapeDtypeStruct((length, WIDE), F32),
        in_specs=[pl.BlockSpec(memory_space=pltpu.SMEM), vmem, vmem, vmem, vmem],
        out_specs=pl.BlockSpec(memory_space=pl.ANY),
        scratch_shapes=[
            pltpu.VMEM((length, WIDE), F32),
            pltpu.SemaphoreType.DMA((length // BLOCK,)),
        ],
        compiler_params=pltpu.CompilerParams(vmem_limit_bytes=24 << 20),
        cost_estimate=pl.CostEstimate(
            flops=2 * length * 3 * T * WIDE, bytes_accessed=4 * length * WIDE, transcendentals=0
        ),
    )(starts, rank, table, inv, gain)


def shards(
    groups,
    byte_rows,
    boundary,
    gate_proj,
    value_proj,
    state_proj,
    step_proj,
    step_bias,
    decay_log,
    skip_gain,
    value_conv,
    value_shift,
    state_conv,
    state_shift,
    norm_gain,
):
    n_ctx, n_head = lax.axis_size("ctx"), lax.axis_size("head")
    weights = [keep_on_chip(w) for w in (value_proj, gate_proj, state_proj, step_proj.T)]
    rows, tail, count, rank, starts = compact(
        keep_off_chip(boundary), keep_off_chip(byte_rows), groups
    )
    table, inv = layer(
        n_ctx,
        n_head,
        groups,
        rows,
        tail,
        count,
        *weights,
        value_conv,
        value_shift.reshape(1, -1),
        state_conv,
        state_shift.reshape(1, -1),
        step_bias,
        decay_log,
        skip_gain,
    )
    return expand(byte_rows.shape[0], groups, starts, rank, table, inv, norm_gain.reshape(1, -1))


def solution(mesh, groups=2048):
    placed = (
        P("ctx", None),
        P("ctx"),
        P(None, "head"),
        P(None, "head"),
        P(),
        P(None, "head"),
        P("head"),
        P("head"),
        P("head"),
        P(None, "head"),
        P("head"),
        P(),
        P(),
        P("head"),
    )
    return jax.shard_map(
        functools.partial(shards, groups),
        mesh=mesh,
        in_specs=placed,
        out_specs=P("ctx", "head"),
        check_vma=False,
    )
```

```python
import functools

import jax
import jax.numpy as jnp
from jax import lax
from jax.experimental import pallas as pl
from jax.experimental.pallas import tpu as pltpu
from jax.sharding import PartitionSpec as P

F32 = jnp.float32
BF16 = jnp.bfloat16
I32 = jnp.int32
HEAD_DIM = 64
STATE = 128
HEADS_HERE = 8
WIDE = HEADS_HERE * HEAD_DIM
INNER = 4096
T = 128
BLOCK = 256
SPAN = BLOCK + 16
UNROLL = 3
JOINED = 1
EPSILON = 1e-05
LOG_FLOOR = -1e4
MESH = pl.DeviceIdType.MESH


def on_chip(shape, kind):
    return pltpu.VMEM(shape, kind)


def keep_on_chip(array):
    return pltpu.with_memory_space_constraint(array, pltpu.VMEM)


def keep_off_chip(array):
    return pltpu.with_memory_space_constraint(array, pltpu.HBM)


def dot(a, b):
    return jnp.dot(a, b, preferred_element_type=F32)


def dot_tn(a, b):
    return lax.dot_general(a, b, (((0,), (0,)), ((), ())), preferred_element_type=F32)


def dot_nt(a, b):
    return lax.dot_general(a, b, (((1,), (1,)), ((), ())), preferred_element_type=F32)


def iota(shape, axis):
    return lax.broadcasted_iota(I32, shape, axis)


def silu(v):
    return 0.5 * v * (1.0 + jnp.tanh(0.5 * v))


def flag(condition):
    return jnp.where(condition, 1.0, 0.0).astype(BF16)


def pieces(v, count):
    out = []
    for _ in range(count):
        top = v.astype(BF16).astype(F32)
        out.append(top)
        v = v - top
    return out


def compact_kernel(
    groups,
    bnd_hbm,
    bytes_hbm,
    rows_ref,
    tail_ref,
    count_ref,
    rank_ref,
    start_ref,
    held,
    target,
    bnd_ref,
    sems,
    bnd_sem,
):
    blocks = bytes_hbm.shape[0] // BLOCK
    lines = 2 * blocks
    width = rows_ref.shape[1]

    def fetch(j):
        at = pl.ds(pl.multiple_of(j * BLOCK, BLOCK), BLOCK)
        return pltpu.make_async_copy(bytes_hbm.at[at], held.at[at], sems.at[j])

    def begin(j, carry):
        fetch(j).start()
        return carry

    flags = pltpu.make_async_copy(bnd_hbm, bnd_ref, bnd_sem)
    flags.start()
    lax.fori_loop(0, blocks, begin, 0)
    flags.wait()

    bnd = bnd_ref[...].reshape(lines, 128).astype(F32)
    bnd16 = bnd.astype(BF16)
    inside = dot(bnd16, flag(iota((128, 128), 0) <= iota((128, 128), 1)))
    above = dot(flag(iota((lines, lines), 1) < iota((lines, lines), 0)), bnd16)
    before = jnp.sum(above, axis=1, keepdims=True)
    upto = inside + before
    target[...] = jnp.where(bnd > 0, upto - 1.0, -1.0).astype(I32)
    rank_ref[...] = jnp.concatenate([upto, jnp.zeros((128 - lines, 128), F32)], 0).T
    for j in range(blocks):
        start_ref[j] = before[2 * j, 0].astype(I32)
    count = upto[lines - 1, 127].astype(I32)
    count_ref[...] = jnp.full(count_ref.shape, count, I32)
    rows_ref[0:16, :] = jnp.zeros((16, width), BF16)

    def step(j, carry):
        fetch(j).wait()
        base = pl.multiple_of((start_ref[j] // 16) * 16, 16)
        places = iota((SPAN, 128), 0) + base
        left = places == target[pl.ds(2 * j, 1), :]
        right = places == target[pl.ds(2 * j + 1, 1), :]
        choose = jnp.concatenate([flag(left), flag(right)], 1)
        here = pl.ds(pl.multiple_of(j * BLOCK, BLOCK), BLOCK)
        piece = min(512, width)
        for c in range(0, width, piece):
            cols = pl.ds(c, piece)
            picked = dot(choose, held[here, cols]).astype(BF16)
            rows_ref[pl.ds(base, 16), cols] = rows_ref[pl.ds(base, 16), cols] + picked[:16]
            rows_ref[pl.ds(pl.multiple_of(base + 16, 16), BLOCK), cols] = picked[16:]
        return carry

    def steps(i, carry):
        for q in range(JOINED):
            step(i * JOINED + q, 0)
        return carry

    lax.fori_loop(0, blocks // JOINED, steps, 0)

    clear = (start_ref[blocks - 1] // 16) * 16 + SPAN

    def wipe(i, carry):
        rows_ref[pl.ds(pl.multiple_of(clear + 16 * i, 16), 16), :] = jnp.zeros((16, width), BF16)
        return carry

    lax.fori_loop(0, jnp.maximum(groups + 32 - clear, 0) // 16, wipe, 0)
    near = pl.multiple_of((jnp.maximum(count - 4, 0) // 16) * 16, 16)
    row, column = iota((16, 32), 0), iota((16, 32), 1)
    wanted = count - 16 + row
    choose = flag((row >= 12) & (wanted >= 0) & (column + near == wanted))
    last = dot(choose, rows_ref[pl.ds(near, 32), :])
    few = jnp.minimum(count, 4).astype(F32)
    tail_ref[...] = jnp.where(iota(last.shape, 0) == 0, few, last).astype(BF16)


def compact(boundary, byte_rows, groups):
    length, width = byte_rows.shape
    blocks = length // BLOCK
    vmem = pl.BlockSpec(memory_space=pltpu.VMEM)
    return pl.pallas_call(
        functools.partial(compact_kernel, groups),
        out_shape=[
            on_chip((groups + SPAN, width), BF16),
            on_chip((16, width), BF16),
            on_chip((8, 128), I32),
            on_chip((128, 128), F32),
            jax.ShapeDtypeStruct((blocks,), I32),
        ],
        in_specs=[pl.BlockSpec(memory_space=pltpu.HBM)] * 2,
        out_specs=[vmem, vmem, vmem, vmem, pl.BlockSpec(memory_space=pltpu.SMEM)],
        scratch_shapes=[
            pltpu.VMEM((length, width), BF16),
            pltpu.VMEM((2 * blocks, 128), I32),
            pltpu.VMEM((length,), I32),
            pltpu.SemaphoreType.DMA((blocks,)),
            pltpu.SemaphoreType.DMA,
        ],
        compiler_params=pltpu.CompilerParams(vmem_limit_bytes=18 << 20),
        cost_estimate=pl.CostEstimate(
            flops=2 * SPAN * length * width, bytes_accessed=2 * length * width, transcendentals=0
        ),
    )(boundary, byte_rows)


def head_column(ref, shape):
    head = iota(shape, 0) % HEADS_HERE
    out = jnp.zeros(shape, F32)
    for h in range(HEADS_HERE):
        out = jnp.where(head == h, ref[h], out)
    return out


def start_all(copy, count):
    lax.fori_loop(1, count, lambda d, c: (copy(d).start(), c)[1], 0)


def wait_all(sent, send_sem, landed, recv_sem):
    for ref, sem in ((sent, send_sem), (landed, recv_sem)):
        both = ref.at[pl.ds(0, landed.shape[0] - 1)]
        pltpu.make_async_copy(both, both, sem).wait()


def layer_kernel(
    n_ctx,
    groups,
    rows_ref,
    tail_ref,
    count_ref,
    value_ref,
    gate_ref,
    state_ref,
    step_ref,
    vconv_ref,
    vshift_ref,
    sconv_ref,
    sshift_ref,
    bias_ref,
    log_ref,
    skip_ref,
    mix,
    open_gate,
    grow,
    locs,
    fades,
    maps,
    base,
    lead_ref,
    ext_0,
    ext_a,
    ext_b,
    ext_h,
    taps,
    xs,
    raw_step,
    lead_t,
    lead_e,
    minus,
    sel_d,
    sel_e,
    near,
    halo_gate,
    ends_out,
    ends_in,
    out_slices,
    in_slices,
    ret_out,
    ret_in,
    entry,
    near_send,
    near_recv,
    end_send,
    end_recv,
    out_send,
    out_recv,
    ret_send,
    ret_recv,
):
    me = lax.axis_index("ctx")
    subs = groups // T
    share = STATE * 4 // n_ctx
    big = 2 * T
    bigs = groups // big

    barrier = pltpu.get_barrier_semaphore()

    def greet_ctx(d, carry):
        pl.semaphore_signal(
            barrier, inc=1, device_id={"ctx": lax.rem(me + d, n_ctx)}, device_id_type=MESH
        )
        return carry

    lax.fori_loop(1, n_ctx, greet_ctx, 0)

    def near_copy(d):
        return pltpu.make_async_remote_copy(
            src_ref=tail_ref,
            dst_ref=near.at[d - 1],
            send_sem=near_send.at[d - 1],
            recv_sem=near_recv.at[d - 1],
            device_id={"ctx": lax.rem(me + d, n_ctx)},
            device_id_type=MESH,
        )

    def end_copy(d):
        to = lax.rem(me + d, n_ctx)
        return pltpu.make_async_remote_copy(
            src_ref=ends_out.at[lax.rem(to, 4)],
            dst_ref=ends_in.at[me],
            send_sem=end_send,
            recv_sem=end_recv,
            device_id={"ctx": to},
            device_id_type=MESH,
        )

    def out_copy(d):
        to = lax.rem(me + d, n_ctx)
        return pltpu.make_async_remote_copy(
            src_ref=out_slices.at[to],
            dst_ref=in_slices.at[me],
            send_sem=out_send,
            recv_sem=out_recv,
            device_id={"ctx": to},
            device_id_type=MESH,
        )

    def ret_copy(d):
        to = lax.rem(me + d, n_ctx)
        return pltpu.make_async_remote_copy(
            src_ref=ret_out.at[to],
            dst_ref=ret_in.at[me],
            send_sem=ret_send,
            recv_sem=ret_recv,
            device_id={"ctx": to},
            device_id_type=MESH,
        )

    for i in range(groups // 512):
        got = dot_nt(step_ref[...], rows_ref[i * 512 : (i + 1) * 512, :])
        for q in range(4):
            k = i * 4 + q
            raw_step[k * 8 : (k + 1) * 8, :] = got[:, q * T : (q + 1) * T]

    pl.semaphore_wait(barrier, n_ctx - 1)
    near_copy(1).start()
    near_copy(2).start()

    shape = (subs * 8, T)
    raw = raw_step[...] + head_column(bias_ref, shape)
    soft = jnp.maximum(raw, 0.0) + jnp.log1p(jnp.exp(-jnp.abs(raw)))
    valid = (iota(shape, 0) // 8) * T + iota(shape, 1) < count_ref[0:1, :]
    step = jnp.where(valid, soft, 0.0)
    logs = jnp.where(valid, jnp.maximum(jnp.log(soft), LOG_FLOOR), LOG_FLOOR)
    decay = -step * jnp.exp(head_column(log_ref, shape))
    tri = flag(iota((T, T), 0) <= iota((T, T), 1))
    d0, d1, d2 = pieces(decay, 3)
    cum = (dot(d0.astype(BF16), tri) + dot(d1.astype(BF16), tri)) + dot(d2.astype(BF16), tri)
    total = jnp.broadcast_to(cum[:, T - 1 : T], shape)
    cums = pieces(cum, 3)
    lows = pieces(logs - cum, 3)
    grows = pieces(jnp.exp(cum), 2)
    tails = pieces(jnp.exp(total - cum) * step, 2)

    over = total[0:8]
    for k in range(1, subs):
        over = over + total[k * 8 : (k + 1) * 8]
    high, low = pieces(jnp.exp(over), 2)
    first_half = iota((8, T), 1) < HEAD_DIM
    for c in range(4):
        both = [
            jnp.where(
                first_half,
                jnp.broadcast_to(part[2 * c : 2 * c + 1], (8, T)),
                jnp.broadcast_to(part[2 * c + 1 : 2 * c + 2], (8, T)),
            )
            for part in (high, low)
        ]
        ends_out[c] = jnp.concatenate(both, 0).astype(BF16)
    ends_in[me] = ends_out[lax.rem(me, 4)]
    start_all(end_copy, n_ctx)

    for k in range(subs):
        at = slice(k * 8, (k + 1) * 8)
        lead_t[k] = jnp.concatenate([p[at] for p in cums] + [jnp.ones((24, T), F32)], 0).astype(BF16)
        lead_e[k] = jnp.concatenate([p[at] for p in grows + tails], 0).astype(BF16)
        minus[k] = jnp.concatenate([p[at] for p in lows], 0)
    head_of = iota((24, 8 * T), 0) % 8
    sel_d[...] = flag(head_of == iota((24, 8 * T), 1) // T).astype(F32)
    row, lane = iota((32, 2 * WIDE), 0), iota((32, 2 * WIDE), 1)
    sel_e[...] = flag((row % 8 == (lane % WIDE) // HEAD_DIM) & ((row < 16) == (lane < WIDE)))
    for c in range(6):
        tap, move, at = (
            (vconv_ref, vshift_ref, slice(c * 128, (c + 1) * 128))
            if c < 4
            else (sconv_ref, sshift_ref, slice((c - 4) * 128, (c - 3) * 128))
        )
        taps[c, 0:4, :] = 0.5 * tap[:, at]
        taps[c, 4:5, :] = 0.5 * move[:, at]

    def project(block, ext):
        here = pl.ds(pl.multiple_of(block * big, big), big)
        for weights, first, count in ((value_ref, 0, 4), (state_ref, 4, 2)):
            got = dot(rows_ref[here, :], weights[...])
            for c in range(count):
                ext[first + c, 8 : 8 + big, :] = got[:, c * 128 : (c + 1) * 128]

    def convolve(ext, c, at, length):
        h = taps[c, 4:5, :] + taps[c, 0:1, :] * ext[c, at + 5 : at + 5 + length, :]
        for j in range(1, 4):
            h = h + taps[c, j : j + 1, :] * ext[c, at + 5 + j : at + 5 + j + length, :]
        return h + h * jnp.tanh(h)

    for k in (0, 2):
        locs[k] = jnp.zeros((STATE, WIDE), F32)
        fades[k] = jnp.ones((1, WIDE), F32)

    def advance(block, ext, onto, target):
        both = [dot_tn(lead_e[block * 2 + q], sel_e[...]) for q in range(2)]
        if target is not None:
            project(target, onto)
        for q in range(2):
            k = block * 2 + q
            at = pl.ds(pl.multiple_of(k * T, T), T)
            grow[k] = both[q][:, :WIDE]
            weighted = []
            for c in range(4):
                x = convolve(ext, c, q * T, T)
                xs[at, c * 128 : (c + 1) * 128] = x.astype(BF16)
                tail = both[q][:, WIDE + c * 128 : WIDE + (c + 1) * 128]
                weighted.append((x * tail).astype(BF16))
            for c in range(2):
                maps[at, c * 128 : (c + 1) * 128] = convolve(ext, 4 + c, q * T, T).astype(BF16)
            new = dot_tn(maps[at, :STATE], jnp.concatenate(weighted, 1))
            factor = both[q][T - 1 : T, :WIDE]
            locs[k + 1] = factor * locs[k] + new
            fades[k + 1] = factor * fades[k]

    def hand_on(source, ext):
        for c in range(6):
            ext[c, 0:8, :] = source[c, big : big + 8, :]

    def local(j, carry):
        advance(2 * j + 1, ext_a, ext_b, 2 * j + 2)
        hand_on(ext_a, ext_b)
        advance(2 * j + 2, ext_b, ext_a, 2 * j + 3)
        hand_on(ext_b, ext_a)
        return carry

    project(0, ext_0)
    project(1, ext_a)
    hand_on(ext_0, ext_a)
    lax.fori_loop(0, bigs // 2 - 1, local, 0)

    near_copy(1).wait()
    near_copy(2).wait()
    first = jnp.where(me >= 1, near[0].astype(F32), 0.0)
    second = jnp.where(me >= 2, near[1].astype(F32), 0.0)
    few = jnp.broadcast_to(near[0][0:1, 0:16].astype(F32), (16, 16))
    few = jnp.where(me >= 1, few, 4.0)
    row, lane = iota((16, 16), 0), iota((16, 16), 1)
    shift = flag((row >= 12) & (lane >= 12) & (lane.astype(F32) == row.astype(F32) + few))
    halo = dot(shift, second.astype(BF16)) + jnp.where(iota(first.shape, 0) >= 12, first, 0.0)
    halo = halo.astype(BF16)
    for weights, first, count in ((value_ref, 0, 4), (state_ref, 4, 2)):
        got = dot(halo, weights[...])
        for c in range(count):
            ext_h[first + c, 8:24, :] = got[:, c * 128 : (c + 1) * 128]
    halo_gate[...] = silu(dot(halo, gate_ref[...]))
    for c in range(6):
        ext_h[c, 0:8, :] = jnp.zeros((8, 128), F32)
        ext_0[c, 0:8, :] = ext_h[c, 16:24, :]
    advance(bigs - 1, ext_a, None, None)
    advance(0, ext_0, None, None)
    x_h = jnp.concatenate([convolve(ext_h, c, 0, 16) for c in range(4)], 1)
    c_h = convolve(ext_h, 5, 0, 16).astype(BF16)

    locs[subs] = locs[subs] + fades[subs] * locs[2]

    for k in range(n_ctx):
        r, c = (k // 4) * share, (k % 4) * 128
        out_slices[k] = locs[subs, r : r + share, c : c + 128].astype(BF16)
    in_slices[me] = out_slices[me]
    start_all(out_copy, n_ctx)

    skip = jnp.zeros((1, WIDE), F32)
    for h in range(HEADS_HERE):
        skip = jnp.where(iota((1, WIDE), 1) // HEAD_DIM == h, skip_ref[h], skip)
    lower = iota((T, T), 1) <= iota((T, T), 0)
    left_half = iota((T, T), 1) < HEAD_DIM

    def inside(i, carry):
        g0 = pl.multiple_of(i * big, big)
        here = pl.ds(g0, big)
        parts = []
        for q in range(big // T):
            k = i * (big // T) + q
            at = pl.ds(pl.multiple_of(g0 + q * T, T), T)
            m = maps[at, :]
            scores = jnp.where(lower, dot_nt(m[:, STATE:], m[:, :STATE]), 0.0)
            tile = jnp.concatenate([minus[k]] * HEADS_HERE, 1) * sel_d[...]
            right = jnp.concatenate([sel_d[...], tile], 0).astype(BF16)
            parts.append((at, scores, dot_tn(lead_t[k], right)))
        opened = dot(rows_ref[here, :], gate_ref[...])
        for at, scores, spread in parts:
            x = xs[at, :]
            for p in range(HEADS_HERE // 2):
                pair = x[:, p * T : (p + 1) * T]
                weight = jnp.exp(jnp.minimum(spread[:, 2 * p * T : 2 * (p + 1) * T], 60.0))
                weight = (weight * jnp.concatenate([scores, scores], 1)).astype(BF16)
                stacked = jnp.concatenate(
                    [
                        jnp.where(left_half, pair, jnp.zeros_like(pair)),
                        jnp.where(left_half, jnp.zeros_like(pair), pair),
                    ],
                    0,
                )
                got = dot(weight, stacked)
                cols = slice(p * T, (p + 1) * T)
                mix[at, cols] = got + skip[:, cols] * pair.astype(F32)
        open_gate[here, :] = silu(opened)
        return carry

    half = bigs // 2
    lax.fori_loop(0, half, inside, 0)

    wait_all(ends_in, end_send, ends_in, end_recv)
    wait_all(out_slices, out_send, in_slices, out_recv)
    running = jnp.zeros((share, 128), F32)
    for i in range(n_ctx):
        ret_out[i] = running.astype(BF16)
        factor = ends_in[i].astype(F32)
        factor = factor[0:1] + factor[8:9]
        running = factor * running + in_slices[i].astype(F32)
    ret_in[me] = ret_out[me]
    start_all(ret_copy, n_ctx)

    lax.fori_loop(half, bigs, inside, 0)

    wait_all(ret_out, ret_send, ret_in, ret_recv)
    for k in range(n_ctx):
        r, c = (k // 4) * share, (k % 4) * 128
        entry[r : r + share, c : c + 128] = ret_in[k]

    base[0] = entry[...].astype(F32)
    base[1] = locs[2] + fades[2] * base[0]
    y_h = dot(c_h, entry[...]) + skip * x_h
    lead_ref[...] = y_h * halo_gate[...]


def line_of(start, groups):
    return jnp.minimum((start + T - 1) // T, (groups + T - window_of(groups)) // T)


def window_of(groups):
    return min(3 * T, groups + T)


def norm_kernel(
    n_head,
    groups,
    mix,
    open_gate,
    grow,
    locs,
    fades,
    maps,
    base,
    lead_ref,
    rank_ref,
    start_ref,
    table,
    inv_ref,
    place_ref,
    squares,
    sq_send,
    sq_recv,
):
    column = lax.axis_index("head")
    subs = groups // T
    blocks = place_ref.shape[0] // BLOCK
    barrier = pltpu.get_barrier_semaphore()

    def greet_head(d, carry):
        pl.semaphore_signal(
            barrier, inc=1, device_id={"head": lax.rem(column + d, n_head)}, device_id_type=MESH
        )
        return carry

    lax.fori_loop(1, n_head, greet_head, 0)

    def sq_copy(d):
        return pltpu.make_async_remote_copy(
            src_ref=squares.at[column],
            dst_ref=squares.at[column],
            send_sem=sq_send,
            recv_sem=sq_recv,
            device_id={"head": lax.rem(column + d, n_head)},
            device_id_type=MESH,
        )

    ones = jnp.ones((8, WIDE), BF16)
    g_h = lead_ref[...]
    table[0 : T - 16, :] = jnp.zeros((T - 16, WIDE), BF16)
    table[T - 16 : T, :] = g_h.astype(BF16)
    power = jnp.concatenate([jnp.zeros((T - 16, WIDE), F32), g_h * g_h], 0).astype(BF16)
    mine = squares.at[column]
    mine[...] = jnp.zeros(mine.shape, F32)
    mine[0:1, :] = dot_nt(ones, power)[0:1, :]

    def outer(i, carry):
        for q in range(4):
            k = i * 4 + q
            at = pl.ds(pl.multiple_of(k * T, T), T)
            state = (locs[k] + fades[k] * base[jnp.where(k > 2, 1, 0)]).astype(BF16)
            gated = mix[at, :] + grow[k] * dot(maps[at, STATE:], state)
            gated = gated * open_gate[at, :]
            table[pl.ds(pl.multiple_of((k + 1) * T, T), T), :] = gated.astype(BF16)
            squares[column, pl.ds(k + 1, 1), :] = dot_nt(ones, (gated * gated).astype(BF16))[0:1, :]
        return carry

    lax.fori_loop(0, subs // 4, outer, 0)

    pl.semaphore_wait(barrier, n_head - 1)
    start_all(sq_copy, n_head)

    def locate(i, carry):
        for j in (2 * i, 2 * i + 1) if blocks % 2 == 0 else (i,):
            for half in range(2):
                lane = iota((T, T), 1)
                rank = jnp.sum(
                    jnp.where(lane == 2 * j + half, rank_ref[...], 0.0), axis=1, keepdims=True
                )
                first = (line_of(start_ref[j], groups) * T).astype(F32)
                place = jnp.broadcast_to(rank + ((T - 1.0) - first), (T, T))
                lane = lane.astype(F32)
                hits = [flag(place == lane + w * T) for w in range(window_of(groups) // T)]
                at = pl.ds(pl.multiple_of(j * BLOCK + half * T, T), T)
                place_ref[at, :] = jnp.concatenate(hits, 1)
        return carry

    lax.fori_loop(0, blocks // 2 if blocks % 2 == 0 else blocks, locate, 0)

    wait_all(squares, sq_send, squares, sq_recv)
    power = squares[0]
    for i in range(1, n_head):
        power = power + squares[i]
    inv_ref[...] = lax.rsqrt(power * (1.0 / (n_head * WIDE)) + EPSILON)


def norm(n_head, groups, length, *args):
    subs = groups // T
    lines = -(-(subs + 1) // 8) * 8
    vmem = pl.BlockSpec(memory_space=pltpu.VMEM)
    return pl.pallas_call(
        functools.partial(norm_kernel, n_head, groups),
        out_shape=[
            on_chip((groups + T, WIDE), BF16),
            on_chip((lines, T), F32),
            on_chip((length, window_of(groups)), BF16),
        ],
        in_specs=[vmem] * 9 + [pl.BlockSpec(memory_space=pltpu.SMEM)],
        out_specs=[vmem] * 3,
        scratch_shapes=[
            pltpu.VMEM((n_head, lines, T), F32),
            pltpu.SemaphoreType.DMA,
            pltpu.SemaphoreType.DMA,
        ],
        compiler_params=pltpu.CompilerParams(
            collective_id=1, has_side_effects=True, vmem_limit_bytes=8 << 20
        ),
        cost_estimate=pl.CostEstimate(
            flops=4 * groups * STATE * WIDE, bytes_accessed=1 << 20, transcendentals=0
        ),
    )(*args)


def layer(n_ctx, groups, *args):
    subs = groups // T
    share = STATE * 4 // n_ctx
    vmem = pl.BlockSpec(memory_space=pltpu.VMEM)
    smem = pl.BlockSpec(memory_space=pltpu.SMEM)
    width = args[0].shape[1]
    sem = pltpu.SemaphoreType.DMA
    return pl.pallas_call(
        functools.partial(layer_kernel, n_ctx, groups),
        out_shape=[
            on_chip((groups, WIDE), F32),
            on_chip((groups, WIDE), F32),
            on_chip((subs, T, WIDE), F32),
            on_chip((subs + 1, STATE, WIDE), F32),
            on_chip((subs + 1, 1, WIDE), F32),
            on_chip((groups, 2 * STATE), BF16),
            on_chip((2, STATE, WIDE), F32),
            on_chip((16, WIDE), F32),
        ],
        in_specs=[vmem] * 11 + [smem] * 3,
        out_specs=[vmem] * 8,
        scratch_shapes=[
            pltpu.VMEM((6, 2 * T + 8, 128), F32),
            pltpu.VMEM((6, 2 * T + 8, 128), F32),
            pltpu.VMEM((6, 2 * T + 8, 128), F32),
            pltpu.VMEM((6, 24, 128), F32),
            pltpu.VMEM((6, 8, 128), F32),
            pltpu.VMEM((groups, WIDE), BF16),
            pltpu.VMEM((subs * 8, T), F32),
            pltpu.VMEM((subs, 48, T), BF16),
            pltpu.VMEM((subs, 32, T), BF16),
            pltpu.VMEM((subs, 24, T), F32),
            pltpu.VMEM((24, 8 * T), F32),
            pltpu.VMEM((32, 2 * WIDE), BF16),
            pltpu.VMEM((2, 16, width), BF16),
            pltpu.VMEM((16, WIDE), F32),
            pltpu.VMEM((4, 16, 128), BF16),
            pltpu.VMEM((n_ctx, 16, 128), BF16),
            pltpu.VMEM((n_ctx, share, 128), BF16),
            pltpu.VMEM((n_ctx, share, 128), BF16),
            pltpu.VMEM((n_ctx, share, 128), BF16),
            pltpu.VMEM((n_ctx, share, 128), BF16),
            pltpu.VMEM((STATE, WIDE), BF16),
            sem((2,)),
            sem((2,)),
            sem,
            sem,
            sem,
            sem,
            sem,
            sem,
        ],
        compiler_params=pltpu.CompilerParams(
            collective_id=0, has_side_effects=True, vmem_limit_bytes=14 << 20
        ),
        cost_estimate=pl.CostEstimate(
            flops=2 * groups * width * 1536, bytes_accessed=8 << 20, transcendentals=1 << 22
        ),
    )(*args)


def expand_kernel(groups, start_ref, place_ref, table_ref, inv_ref, gain_ref, out_hbm, ready, sems):
    blocks = out_hbm.shape[0] // BLOCK
    window = window_of(groups)

    def send(j):
        at = pl.ds(pl.multiple_of(j * BLOCK, BLOCK), BLOCK)
        return pltpu.make_async_copy(ready.at[at], out_hbm.at[at], sems.at[j])

    def step(j, carry):
        line = line_of(start_ref[j], groups)
        at = pl.ds(pl.multiple_of(j * BLOCK, BLOCK), BLOCK)
        places = place_ref[at, :]
        got = dot(places, table_ref[pl.ds(pl.multiple_of(line * T, T), window), :])
        scale = jnp.zeros((BLOCK, T), F32)
        for w in range(window // T):
            scale = scale + places[:, w * T : (w + 1) * T].astype(F32) * inv_ref[pl.ds(line + w, 1), :]
        ready[at, :] = got * gain_ref[...] * jnp.sum(scale, axis=1, keepdims=True)
        send(j).start()
        return carry

    def steps(i, carry):
        for q in range(UNROLL):
            step(i * UNROLL + q, 0)
        return carry

    lax.fori_loop(0, blocks // UNROLL, steps, 0)

    def finish(j, carry):
        send(j).wait()
        return carry

    lax.fori_loop(0, blocks, finish, 0)


def expand(length, groups, starts, places, table, inv, gain):
    vmem = pl.BlockSpec(memory_space=pltpu.VMEM)
    return pl.pallas_call(
        functools.partial(expand_kernel, groups),
        out_shape=jax.ShapeDtypeStruct((length, WIDE), F32),
        in_specs=[pl.BlockSpec(memory_space=pltpu.SMEM), vmem, vmem, vmem, vmem],
        out_specs=pl.BlockSpec(memory_space=pl.ANY),
        scratch_shapes=[
            pltpu.VMEM((length, WIDE), F32),
            pltpu.SemaphoreType.DMA((length // BLOCK,)),
        ],
        compiler_params=pltpu.CompilerParams(vmem_limit_bytes=12 << 20),
        cost_estimate=pl.CostEstimate(
            flops=2 * length * 3 * T * WIDE, bytes_accessed=4 * length * WIDE, transcendentals=0
        ),
    )(starts, places, table, inv, gain)


def shards(
    groups,
    byte_rows,
    boundary,
    gate_proj,
    value_proj,
    state_proj,
    step_proj,
    step_bias,
    decay_log,
    skip_gain,
    value_conv,
    value_shift,
    state_conv,
    state_shift,
    norm_gain,
):
    n_ctx, n_head = lax.axis_size("ctx"), lax.axis_size("head")
    weights = [keep_on_chip(w) for w in (value_proj, gate_proj, state_proj, step_proj.T)]
    rows, tail, count, rank, starts = compact(
        keep_off_chip(boundary), keep_off_chip(byte_rows), groups
    )
    carried = layer(
        n_ctx,
        groups,
        rows,
        tail,
        count,
        *weights,
        value_conv,
        value_shift.reshape(1, -1),
        state_conv,
        state_shift.reshape(1, -1),
        step_bias,
        decay_log,
        skip_gain,
    )
    length = byte_rows.shape[0]
    table, inv, places = norm(n_head, groups, length, *carried, rank, starts)
    return expand(length, groups, starts, places, table, inv, norm_gain.reshape(1, -1))


def solution(mesh, groups=2048):
    placed = (
        P("ctx", None),
        P("ctx"),
        P(None, "head"),
        P(None, "head"),
        P(),
        P(None, "head"),
        P("head"),
        P("head"),
        P("head"),
        P(None, "head"),
        P("head"),
        P(),
        P(),
        P("head"),
    )
    return jax.shard_map(
        functools.partial(shards, groups),
        mesh=mesh,
        in_specs=placed,
        out_specs=P("ctx", "head"),
        check_vma=False,
    )
```

```python
import functools

import jax
import jax.numpy as jnp
from jax import lax
from jax.experimental import pallas as pl
from jax.experimental.pallas import tpu as pltpu
from jax.sharding import PartitionSpec as P

F32 = jnp.float32
BF16 = jnp.bfloat16
I32 = jnp.int32
HEAD_DIM = 64
STATE = 128
HEADS_HERE = 8
WIDE = HEADS_HERE * HEAD_DIM
INNER = 4096
T = 128
BLOCK = 256
SPAN = BLOCK + 16
UNROLL = 3
JOINED = 1
EPSILON = 1e-05
LOG_FLOOR = -1e4
MESH = pl.DeviceIdType.MESH


def on_chip(shape, kind):
    return pltpu.VMEM(shape, kind)


def keep_on_chip(array):
    return pltpu.with_memory_space_constraint(array, pltpu.VMEM)


def keep_off_chip(array):
    return pltpu.with_memory_space_constraint(array, pltpu.HBM)


def dot(a, b):
    return jnp.dot(a, b, preferred_element_type=F32)


def dot_tn(a, b):
    return lax.dot_general(a, b, (((0,), (0,)), ((), ())), preferred_element_type=F32)


def dot_nt(a, b):
    return lax.dot_general(a, b, (((1,), (1,)), ((), ())), preferred_element_type=F32)


def iota(shape, axis):
    return lax.broadcasted_iota(I32, shape, axis)


def silu(v):
    return 0.5 * v * (1.0 + jnp.tanh(0.5 * v))


def flag(condition):
    return jnp.where(condition, 1.0, 0.0).astype(BF16)


def pieces(v, count):
    out = []
    for _ in range(count):
        top = v.astype(BF16).astype(F32)
        out.append(top)
        v = v - top
    return out


def compact_kernel(
    groups,
    bnd_hbm,
    bytes_hbm,
    rows_ref,
    tail_ref,
    count_ref,
    rank_ref,
    start_ref,
    held,
    target,
    bnd_ref,
    sems,
    bnd_sem,
):
    blocks = bytes_hbm.shape[0] // BLOCK
    lines = 2 * blocks
    width = rows_ref.shape[1]

    def fetch(j):
        at = pl.ds(pl.multiple_of(j * BLOCK, BLOCK), BLOCK)
        return pltpu.make_async_copy(bytes_hbm.at[at], held.at[at], sems.at[j])

    def begin(j, carry):
        fetch(j).start()
        return carry

    flags = pltpu.make_async_copy(bnd_hbm, bnd_ref, bnd_sem)
    flags.start()
    lax.fori_loop(0, blocks, begin, 0)
    flags.wait()

    bnd = bnd_ref[...].reshape(lines, 128).astype(F32)
    bnd16 = bnd.astype(BF16)
    inside = dot(bnd16, flag(iota((128, 128), 0) <= iota((128, 128), 1)))
    above = dot(flag(iota((lines, lines), 1) < iota((lines, lines), 0)), bnd16)
    before = jnp.sum(above, axis=1, keepdims=True)
    upto = inside + before
    target[...] = jnp.where(bnd > 0, upto - 1.0, -1.0).astype(I32)
    rank_ref[...] = jnp.concatenate([upto, jnp.zeros((128 - lines, 128), F32)], 0).T
    for j in range(blocks):
        start_ref[j] = before[2 * j, 0].astype(I32)
    count = upto[lines - 1, 127].astype(I32)
    count_ref[...] = jnp.full(count_ref.shape, count, I32)
    rows_ref[0:16, :] = jnp.zeros((16, width), BF16)

    def step(j, carry):
        fetch(j).wait()
        base = pl.multiple_of((start_ref[j] // 16) * 16, 16)
        places = iota((SPAN, 128), 0) + base
        left = places == target[pl.ds(2 * j, 1), :]
        right = places == target[pl.ds(2 * j + 1, 1), :]
        choose = jnp.concatenate([flag(left), flag(right)], 1)
        here = pl.ds(pl.multiple_of(j * BLOCK, BLOCK), BLOCK)
        piece = min(512, width)
        for c in range(0, width, piece):
            cols = pl.ds(c, piece)
            picked = dot(choose, held[here, cols]).astype(BF16)
            rows_ref[pl.ds(base, 16), cols] = rows_ref[pl.ds(base, 16), cols] + picked[:16]
            rows_ref[pl.ds(pl.multiple_of(base + 16, 16), BLOCK), cols] = picked[16:]
        return carry

    def steps(i, carry):
        for q in range(JOINED):
            step(i * JOINED + q, 0)
        return carry

    lax.fori_loop(0, blocks // JOINED, steps, 0)

    clear = (start_ref[blocks - 1] // 16) * 16 + SPAN

    def wipe(i, carry):
        rows_ref[pl.ds(pl.multiple_of(clear + 16 * i, 16), 16), :] = jnp.zeros((16, width), BF16)
        return carry

    lax.fori_loop(0, jnp.maximum(groups + 32 - clear, 0) // 16, wipe, 0)
    near = pl.multiple_of((jnp.maximum(count - 4, 0) // 16) * 16, 16)
    row, column = iota((16, 32), 0), iota((16, 32), 1)
    wanted = count - 16 + row
    choose = flag((row >= 12) & (wanted >= 0) & (column + near == wanted))
    last = dot(choose, rows_ref[pl.ds(near, 32), :])
    few = jnp.minimum(count, 4).astype(F32)
    tail_ref[...] = jnp.where(iota(last.shape, 0) == 0, few, last).astype(BF16)


def compact(boundary, byte_rows, groups):
    length, width = byte_rows.shape
    blocks = length // BLOCK
    vmem = pl.BlockSpec(memory_space=pltpu.VMEM)
    return pl.pallas_call(
        functools.partial(compact_kernel, groups),
        out_shape=[
            on_chip((groups + SPAN, width), BF16),
            on_chip((16, width), BF16),
            on_chip((8, 128), I32),
            on_chip((128, 128), F32),
            jax.ShapeDtypeStruct((blocks,), I32),
        ],
        in_specs=[pl.BlockSpec(memory_space=pltpu.HBM)] * 2,
        out_specs=[vmem, vmem, vmem, vmem, pl.BlockSpec(memory_space=pltpu.SMEM)],
        scratch_shapes=[
            pltpu.VMEM((length, width), BF16),
            pltpu.VMEM((2 * blocks, 128), I32),
            pltpu.VMEM((length,), I32),
            pltpu.SemaphoreType.DMA((blocks,)),
            pltpu.SemaphoreType.DMA,
        ],
        compiler_params=pltpu.CompilerParams(vmem_limit_bytes=18 << 20),
        cost_estimate=pl.CostEstimate(
            flops=2 * SPAN * length * width, bytes_accessed=2 * length * width, transcendentals=0
        ),
    )(boundary, byte_rows)


def head_column(ref, shape):
    head = iota(shape, 0) % HEADS_HERE
    out = jnp.zeros(shape, F32)
    for h in range(HEADS_HERE):
        out = jnp.where(head == h, ref[h], out)
    return out


def start_all(copy, count):
    lax.fori_loop(1, count, lambda d, c: (copy(d).start(), c)[1], 0)


def wait_all(sent, send_sem, landed, recv_sem):
    for ref, sem in ((sent, send_sem), (landed, recv_sem)):
        both = ref.at[pl.ds(0, landed.shape[0] - 1)]
        pltpu.make_async_copy(both, both, sem).wait()


def layer_kernel(
    n_ctx,
    groups,
    rows_ref,
    tail_ref,
    count_ref,
    value_ref,
    gate_ref,
    state_ref,
    step_ref,
    vconv_ref,
    vshift_ref,
    sconv_ref,
    sshift_ref,
    bias_ref,
    log_ref,
    skip_ref,
    mix,
    open_gate,
    grow,
    locs,
    fades,
    maps,
    base,
    lead_ref,
    ext_0,
    ext_a,
    ext_b,
    ext_h,
    taps,
    xs,
    raw_step,
    lead_t,
    lead_e,
    minus,
    sel_d,
    sel_e,
    near,
    halo_gate,
    ends_out,
    ends_in,
    out_slices,
    in_slices,
    ret_out,
    ret_in,
    entry,
    near_send,
    near_recv,
    end_send,
    end_recv,
    out_send,
    out_recv,
    ret_send,
    ret_recv,
):
    me = lax.axis_index("ctx")
    subs = groups // T
    share = STATE * 4 // n_ctx
    big = 2 * T
    bigs = groups // big

    barrier = pltpu.get_barrier_semaphore()

    def greet_ctx(d, carry):
        pl.semaphore_signal(
            barrier, inc=1, device_id={"ctx": lax.rem(me + d, n_ctx)}, device_id_type=MESH
        )
        return carry

    lax.fori_loop(1, n_ctx, greet_ctx, 0)

    def near_copy(d):
        return pltpu.make_async_remote_copy(
            src_ref=tail_ref,
            dst_ref=near.at[d - 1],
            send_sem=near_send.at[d - 1],
            recv_sem=near_recv.at[d - 1],
            device_id={"ctx": lax.rem(me + d, n_ctx)},
            device_id_type=MESH,
        )

    def end_copy(d):
        to = lax.rem(me + d, n_ctx)
        return pltpu.make_async_remote_copy(
            src_ref=ends_out.at[lax.rem(to, 4)],
            dst_ref=ends_in.at[me],
            send_sem=end_send,
            recv_sem=end_recv,
            device_id={"ctx": to},
            device_id_type=MESH,
        )

    def out_copy(d):
        to = lax.rem(me + d, n_ctx)
        return pltpu.make_async_remote_copy(
            src_ref=out_slices.at[to],
            dst_ref=in_slices.at[me],
            send_sem=out_send,
            recv_sem=out_recv,
            device_id={"ctx": to},
            device_id_type=MESH,
        )

    def ret_copy(d):
        to = lax.rem(me + d, n_ctx)
        return pltpu.make_async_remote_copy(
            src_ref=ret_out.at[to],
            dst_ref=ret_in.at[me],
            send_sem=ret_send,
            recv_sem=ret_recv,
            device_id={"ctx": to},
            device_id_type=MESH,
        )

    for i in range(groups // 512):
        got = dot_nt(step_ref[...], rows_ref[i * 512 : (i + 1) * 512, :])
        for q in range(4):
            k = i * 4 + q
            raw_step[k * 8 : (k + 1) * 8, :] = got[:, q * T : (q + 1) * T]

    shape = (subs * 8, T)
    raw = raw_step[...] + head_column(bias_ref, shape)
    soft = jnp.maximum(raw, 0.0) + jnp.log1p(jnp.exp(-jnp.abs(raw)))
    valid = (iota(shape, 0) // 8) * T + iota(shape, 1) < count_ref[0:1, :]
    step = jnp.where(valid, soft, 0.0)
    logs = jnp.where(valid, jnp.maximum(jnp.log(soft), LOG_FLOOR), LOG_FLOOR)
    decay = -step * jnp.exp(head_column(log_ref, shape))
    tri = flag(iota((T, T), 0) <= iota((T, T), 1))
    d0, d1, d2 = pieces(decay, 3)
    cum = (dot(d0.astype(BF16), tri) + dot(d1.astype(BF16), tri)) + dot(d2.astype(BF16), tri)
    def project(block, ext):
        here = pl.ds(pl.multiple_of(block * big, big), big)
        for weights, first, count in ((value_ref, 0, 4), (state_ref, 4, 2)):
            got = dot(rows_ref[here, :], weights[...])
            for c in range(count):
                ext[first + c, 8 : 8 + big, :] = got[:, c * 128 : (c + 1) * 128]

    def hand_on(source, ext):
        for c in range(6):
            ext[c, 0:8, :] = source[c, big : big + 8, :]

    project(0, ext_0)
    project(1, ext_a)
    hand_on(ext_0, ext_a)
    total = jnp.broadcast_to(cum[:, T - 1 : T], shape)
    cums = pieces(cum, 3)
    lows = pieces(logs - cum, 3)
    grows = pieces(jnp.exp(cum), 2)
    tails = pieces(jnp.exp(total - cum) * step, 2)

    over = total[0:8]
    for k in range(1, subs):
        over = over + total[k * 8 : (k + 1) * 8]
    high, low = pieces(jnp.exp(over), 2)
    first_half = iota((8, T), 1) < HEAD_DIM
    for c in range(4):
        both = [
            jnp.where(
                first_half,
                jnp.broadcast_to(part[2 * c : 2 * c + 1], (8, T)),
                jnp.broadcast_to(part[2 * c + 1 : 2 * c + 2], (8, T)),
            )
            for part in (high, low)
        ]
        ends_out[c] = jnp.concatenate(both, 0).astype(BF16)

    for k in range(subs):
        at = slice(k * 8, (k + 1) * 8)
        lead_t[k] = jnp.concatenate([p[at] for p in cums] + [jnp.ones((24, T), F32)], 0).astype(BF16)
        lead_e[k] = jnp.concatenate([p[at] for p in grows + tails], 0).astype(BF16)
        minus[k] = jnp.concatenate([p[at] for p in lows], 0)
    head_of = iota((24, 8 * T), 0) % 8
    sel_d[...] = flag(head_of == iota((24, 8 * T), 1) // T).astype(F32)
    row, lane = iota((32, 2 * WIDE), 0), iota((32, 2 * WIDE), 1)
    sel_e[...] = flag((row % 8 == (lane % WIDE) // HEAD_DIM) & ((row < 16) == (lane < WIDE)))
    for c in range(6):
        tap, move, at = (
            (vconv_ref, vshift_ref, slice(c * 128, (c + 1) * 128))
            if c < 4
            else (sconv_ref, sshift_ref, slice((c - 4) * 128, (c - 3) * 128))
        )
        taps[c, 0:4, :] = 0.5 * tap[:, at]
        taps[c, 4:5, :] = 0.5 * move[:, at]

    def convolve(ext, c, at, length):
        h = taps[c, 4:5, :] + taps[c, 0:1, :] * ext[c, at + 5 : at + 5 + length, :]
        for j in range(1, 4):
            h = h + taps[c, j : j + 1, :] * ext[c, at + 5 + j : at + 5 + j + length, :]
        return h + h * jnp.tanh(h)

    for k in (0, 2):
        locs[k] = jnp.zeros((STATE, WIDE), F32)
        fades[k] = jnp.ones((1, WIDE), F32)

    def advance(block, ext, onto, target):
        both = [dot_tn(lead_e[block * 2 + q], sel_e[...]) for q in range(2)]
        if target is not None:
            project(target, onto)
        for q in range(2):
            k = block * 2 + q
            at = pl.ds(pl.multiple_of(k * T, T), T)
            grow[k] = both[q][:, :WIDE]
            weighted = []
            for c in range(4):
                x = convolve(ext, c, q * T, T)
                xs[at, c * 128 : (c + 1) * 128] = x.astype(BF16)
                tail = both[q][:, WIDE + c * 128 : WIDE + (c + 1) * 128]
                weighted.append((x * tail).astype(BF16))
            for c in range(2):
                maps[at, c * 128 : (c + 1) * 128] = convolve(ext, 4 + c, q * T, T).astype(BF16)
            new = dot_tn(maps[at, :STATE], jnp.concatenate(weighted, 1))
            factor = both[q][T - 1 : T, :WIDE]
            locs[k + 1] = factor * locs[k] + new
            fades[k + 1] = factor * fades[k]

    def local(j, carry):
        advance(2 * j + 1, ext_a, ext_b, 2 * j + 2)
        hand_on(ext_a, ext_b)
        advance(2 * j + 2, ext_b, ext_a, 2 * j + 3)
        hand_on(ext_b, ext_a)
        return carry

    pl.semaphore_wait(barrier, n_ctx - 1)
    near_copy(1).start()
    near_copy(2).start()

    ends_in[me] = ends_out[lax.rem(me, 4)]
    start_all(end_copy, n_ctx)

    lax.fori_loop(0, bigs // 2 - 1, local, 0)

    near_copy(1).wait()
    near_copy(2).wait()
    first = jnp.where(me >= 1, near[0].astype(F32), 0.0)
    second = jnp.where(me >= 2, near[1].astype(F32), 0.0)
    few = jnp.broadcast_to(near[0][0:1, 0:16].astype(F32), (16, 16))
    few = jnp.where(me >= 1, few, 4.0)
    row, lane = iota((16, 16), 0), iota((16, 16), 1)
    shift = flag((row >= 12) & (lane >= 12) & (lane.astype(F32) == row.astype(F32) + few))
    halo = dot(shift, second.astype(BF16)) + jnp.where(iota(first.shape, 0) >= 12, first, 0.0)
    halo = halo.astype(BF16)
    for weights, first, count in ((value_ref, 0, 4), (state_ref, 4, 2)):
        got = dot(halo, weights[...])
        for c in range(count):
            ext_h[first + c, 8:24, :] = got[:, c * 128 : (c + 1) * 128]
    halo_gate[...] = silu(dot(halo, gate_ref[...]))
    for c in range(6):
        ext_h[c, 0:8, :] = jnp.zeros((8, 128), F32)
        ext_0[c, 0:8, :] = ext_h[c, 16:24, :]
    advance(bigs - 1, ext_a, None, None)
    advance(0, ext_0, None, None)
    x_h = jnp.concatenate([convolve(ext_h, c, 0, 16) for c in range(4)], 1)
    c_h = convolve(ext_h, 5, 0, 16).astype(BF16)

    locs[subs] = locs[subs] + fades[subs] * locs[2]

    for k in range(n_ctx):
        r, c = (k // 4) * share, (k % 4) * 128
        out_slices[k] = locs[subs, r : r + share, c : c + 128].astype(BF16)
    in_slices[me] = out_slices[me]
    start_all(out_copy, n_ctx)

    skip = jnp.zeros((1, WIDE), F32)
    for h in range(HEADS_HERE):
        skip = jnp.where(iota((1, WIDE), 1) // HEAD_DIM == h, skip_ref[h], skip)
    lower = iota((T, T), 1) <= iota((T, T), 0)
    left_half = iota((T, T), 1) < HEAD_DIM

    wide = 4 * T

    def inside(i, carry):
        g0 = pl.multiple_of(i * wide, wide)
        here = pl.ds(g0, wide)
        parts = []
        for q in range(wide // T):
            k = i * (wide // T) + q
            at = pl.ds(pl.multiple_of(g0 + q * T, T), T)
            m = maps[at, :]
            scores = jnp.where(lower, dot_nt(m[:, STATE:], m[:, :STATE]), 0.0)
            tile = jnp.concatenate([minus[k]] * HEADS_HERE, 1) * sel_d[...]
            right = jnp.concatenate([sel_d[...], tile], 0).astype(BF16)
            parts.append((at, scores, dot_tn(lead_t[k], right)))
        opened = dot(rows_ref[here, :], gate_ref[...])
        for at, scores, spread in parts:
            x = xs[at, :]
            for p in range(HEADS_HERE // 2):
                pair = x[:, p * T : (p + 1) * T]
                weight = jnp.exp(jnp.minimum(spread[:, 2 * p * T : 2 * (p + 1) * T], 60.0))
                weight = (weight * jnp.concatenate([scores, scores], 1)).astype(BF16)
                stacked = jnp.concatenate(
                    [
                        jnp.where(left_half, pair, jnp.zeros_like(pair)),
                        jnp.where(left_half, jnp.zeros_like(pair), pair),
                    ],
                    0,
                )
                got = dot(weight, stacked)
                cols = slice(p * T, (p + 1) * T)
                mix[at, cols] = got + skip[:, cols] * pair.astype(F32)
        open_gate[here, :] = silu(opened)
        return carry

    half = groups // wide // 2
    lax.fori_loop(0, half, inside, 0)

    wait_all(ends_in, end_send, ends_in, end_recv)
    wait_all(out_slices, out_send, in_slices, out_recv)
    running = jnp.zeros((share, 128), F32)
    for i in range(n_ctx):
        ret_out[i] = running.astype(BF16)
        factor = ends_in[i].astype(F32)
        factor = factor[0:1] + factor[8:9]
        running = factor * running + in_slices[i].astype(F32)
    ret_in[me] = ret_out[me]
    start_all(ret_copy, n_ctx)

    lax.fori_loop(half, groups // wide, inside, 0)

    wait_all(ret_out, ret_send, ret_in, ret_recv)
    for k in range(n_ctx):
        r, c = (k // 4) * share, (k % 4) * 128
        entry[r : r + share, c : c + 128] = ret_in[k]

    base[0] = entry[...].astype(F32)
    base[1] = locs[2] + fades[2] * base[0]
    y_h = dot(c_h, entry[...]) + skip * x_h
    lead_ref[...] = y_h * halo_gate[...]


def line_of(start, groups):
    return jnp.minimum((start + T - 1) // T, (groups + T - window_of(groups)) // T)


def window_of(groups):
    return min(3 * T, groups + T)


def norm_kernel(
    n_head,
    groups,
    mix,
    open_gate,
    grow,
    locs,
    fades,
    maps,
    base,
    lead_ref,
    rank_ref,
    start_ref,
    table,
    inv_ref,
    place_ref,
    squares,
    sq_send,
    sq_recv,
):
    column = lax.axis_index("head")
    subs = groups // T
    blocks = place_ref.shape[0] // BLOCK
    barrier = pltpu.get_barrier_semaphore()

    def greet_head(d, carry):
        pl.semaphore_signal(
            barrier, inc=1, device_id={"head": lax.rem(column + d, n_head)}, device_id_type=MESH
        )
        return carry

    lax.fori_loop(1, n_head, greet_head, 0)

    def sq_copy(d):
        return pltpu.make_async_remote_copy(
            src_ref=squares.at[column],
            dst_ref=squares.at[column],
            send_sem=sq_send,
            recv_sem=sq_recv,
            device_id={"head": lax.rem(column + d, n_head)},
            device_id_type=MESH,
        )

    ones = jnp.ones((8, WIDE), BF16)
    g_h = lead_ref[...]
    table[0 : T - 16, :] = jnp.zeros((T - 16, WIDE), BF16)
    table[T - 16 : T, :] = g_h.astype(BF16)
    power = jnp.concatenate([jnp.zeros((T - 16, WIDE), F32), g_h * g_h], 0).astype(BF16)
    mine = squares.at[column]
    mine[...] = jnp.zeros(mine.shape, F32)
    mine[0:1, :] = dot_nt(ones, power)[0:1, :]

    def outer(i, carry):
        for q in range(4):
            k = i * 4 + q
            at = pl.ds(pl.multiple_of(k * T, T), T)
            state = (locs[k] + fades[k] * base[jnp.where(k > 2, 1, 0)]).astype(BF16)
            gated = mix[at, :] + grow[k] * dot(maps[at, STATE:], state)
            gated = gated * open_gate[at, :]
            table[pl.ds(pl.multiple_of((k + 1) * T, T), T), :] = gated.astype(BF16)
            squares[column, pl.ds(k + 1, 1), :] = dot_nt(ones, (gated * gated).astype(BF16))[0:1, :]
        return carry

    lax.fori_loop(0, subs // 4, outer, 0)

    pl.semaphore_wait(barrier, n_head - 1)
    start_all(sq_copy, n_head)

    def locate(i, carry):
        for j in (2 * i, 2 * i + 1) if blocks % 2 == 0 else (i,):
            for half in range(2):
                lane = iota((T, T), 1)
                rank = jnp.sum(
                    jnp.where(lane == 2 * j + half, rank_ref[...], 0.0), axis=1, keepdims=True
                )
                first = (line_of(start_ref[j], groups) * T).astype(F32)
                place = jnp.broadcast_to(rank + ((T - 1.0) - first), (T, T))
                lane = lane.astype(F32)
                hits = [flag(place == lane + w * T) for w in range(window_of(groups) // T)]
                at = pl.ds(pl.multiple_of(j * BLOCK + half * T, T), T)
                place_ref[at, :] = jnp.concatenate(hits, 1)
        return carry

    lax.fori_loop(0, blocks // 2 if blocks % 2 == 0 else blocks, locate, 0)

    wait_all(squares, sq_send, squares, sq_recv)
    power = squares[0]
    for i in range(1, n_head):
        power = power + squares[i]
    inv_ref[...] = lax.rsqrt(power * (1.0 / (n_head * WIDE)) + EPSILON)


def norm(n_head, groups, length, *args):
    subs = groups // T
    lines = -(-(subs + 1) // 8) * 8
    vmem = pl.BlockSpec(memory_space=pltpu.VMEM)
    return pl.pallas_call(
        functools.partial(norm_kernel, n_head, groups),
        out_shape=[
            on_chip((groups + T, WIDE), BF16),
            on_chip((lines, T), F32),
            on_chip((length, window_of(groups)), BF16),
        ],
        in_specs=[vmem] * 9 + [pl.BlockSpec(memory_space=pltpu.SMEM)],
        out_specs=[vmem] * 3,
        scratch_shapes=[
            pltpu.VMEM((n_head, lines, T), F32),
            pltpu.SemaphoreType.DMA,
            pltpu.SemaphoreType.DMA,
        ],
        compiler_params=pltpu.CompilerParams(
            collective_id=1, has_side_effects=True, vmem_limit_bytes=8 << 20
        ),
        cost_estimate=pl.CostEstimate(
            flops=4 * groups * STATE * WIDE, bytes_accessed=1 << 20, transcendentals=0
        ),
    )(*args)


def layer(n_ctx, groups, *args):
    subs = groups // T
    share = STATE * 4 // n_ctx
    vmem = pl.BlockSpec(memory_space=pltpu.VMEM)
    smem = pl.BlockSpec(memory_space=pltpu.SMEM)
    width = args[0].shape[1]
    sem = pltpu.SemaphoreType.DMA
    return pl.pallas_call(
        functools.partial(layer_kernel, n_ctx, groups),
        out_shape=[
            on_chip((groups, WIDE), F32),
            on_chip((groups, WIDE), F32),
            on_chip((subs, T, WIDE), F32),
            on_chip((subs + 1, STATE, WIDE), F32),
            on_chip((subs + 1, 1, WIDE), F32),
            on_chip((groups, 2 * STATE), BF16),
            on_chip((2, STATE, WIDE), F32),
            on_chip((16, WIDE), F32),
        ],
        in_specs=[vmem] * 11 + [smem] * 3,
        out_specs=[vmem] * 8,
        scratch_shapes=[
            pltpu.VMEM((6, 2 * T + 8, 128), F32),
            pltpu.VMEM((6, 2 * T + 8, 128), F32),
            pltpu.VMEM((6, 2 * T + 8, 128), F32),
            pltpu.VMEM((6, 24, 128), F32),
            pltpu.VMEM((6, 8, 128), F32),
            pltpu.VMEM((groups, WIDE), BF16),
            pltpu.VMEM((subs * 8, T), F32),
            pltpu.VMEM((subs, 48, T), BF16),
            pltpu.VMEM((subs, 32, T), BF16),
            pltpu.VMEM((subs, 24, T), F32),
            pltpu.VMEM((24, 8 * T), F32),
            pltpu.VMEM((32, 2 * WIDE), BF16),
            pltpu.VMEM((2, 16, width), BF16),
            pltpu.VMEM((16, WIDE), F32),
            pltpu.VMEM((4, 16, 128), BF16),
            pltpu.VMEM((n_ctx, 16, 128), BF16),
            pltpu.VMEM((n_ctx, share, 128), BF16),
            pltpu.VMEM((n_ctx, share, 128), BF16),
            pltpu.VMEM((n_ctx, share, 128), BF16),
            pltpu.VMEM((n_ctx, share, 128), BF16),
            pltpu.VMEM((STATE, WIDE), BF16),
            sem((2,)),
            sem((2,)),
            sem,
            sem,
            sem,
            sem,
            sem,
            sem,
        ],
        compiler_params=pltpu.CompilerParams(
            collective_id=0, has_side_effects=True, vmem_limit_bytes=14 << 20
        ),
        cost_estimate=pl.CostEstimate(
            flops=2 * groups * width * 1536, bytes_accessed=8 << 20, transcendentals=1 << 22
        ),
    )(*args)


def expand_kernel(groups, start_ref, place_ref, table_ref, inv_ref, gain_ref, out_hbm, ready, sems):
    blocks = out_hbm.shape[0] // BLOCK
    window = window_of(groups)

    def send(j):
        at = pl.ds(pl.multiple_of(j * BLOCK, BLOCK), BLOCK)
        return pltpu.make_async_copy(ready.at[at], out_hbm.at[at], sems.at[j])

    def step(j, carry):
        line = line_of(start_ref[j], groups)
        at = pl.ds(pl.multiple_of(j * BLOCK, BLOCK), BLOCK)
        places = place_ref[at, :]
        got = dot(places, table_ref[pl.ds(pl.multiple_of(line * T, T), window), :])
        scale = jnp.zeros((BLOCK, T), F32)
        for w in range(window // T):
            scale = scale + places[:, w * T : (w + 1) * T].astype(F32) * inv_ref[pl.ds(line + w, 1), :]
        ready[at, :] = got * gain_ref[...] * jnp.sum(scale, axis=1, keepdims=True)
        send(j).start()
        return carry

    def steps(i, carry):
        for q in range(UNROLL):
            step(i * UNROLL + q, 0)
        return carry

    lax.fori_loop(0, blocks // UNROLL, steps, 0)

    def finish(j, carry):
        send(j).wait()
        return carry

    lax.fori_loop(0, blocks, finish, 0)


def expand(length, groups, starts, places, table, inv, gain):
    vmem = pl.BlockSpec(memory_space=pltpu.VMEM)
    return pl.pallas_call(
        functools.partial(expand_kernel, groups),
        out_shape=jax.ShapeDtypeStruct((length, WIDE), F32),
        in_specs=[pl.BlockSpec(memory_space=pltpu.SMEM), vmem, vmem, vmem, vmem],
        out_specs=pl.BlockSpec(memory_space=pl.ANY),
        scratch_shapes=[
            pltpu.VMEM((length, WIDE), F32),
            pltpu.SemaphoreType.DMA((length // BLOCK,)),
        ],
        compiler_params=pltpu.CompilerParams(vmem_limit_bytes=12 << 20),
        cost_estimate=pl.CostEstimate(
            flops=2 * length * 3 * T * WIDE, bytes_accessed=4 * length * WIDE, transcendentals=0
        ),
    )(starts, places, table, inv, gain)


def shards(
    groups,
    byte_rows,
    boundary,
    gate_proj,
    value_proj,
    state_proj,
    step_proj,
    step_bias,
    decay_log,
    skip_gain,
    value_conv,
    value_shift,
    state_conv,
    state_shift,
    norm_gain,
):
    n_ctx, n_head = lax.axis_size("ctx"), lax.axis_size("head")
    weights = [keep_on_chip(w) for w in (value_proj, gate_proj, state_proj, step_proj.T)]
    rows, tail, count, rank, starts = compact(
        keep_off_chip(boundary), keep_off_chip(byte_rows), groups
    )
    carried = layer(
        n_ctx,
        groups,
        rows,
        tail,
        count,
        *weights,
        value_conv,
        value_shift.reshape(1, -1),
        state_conv,
        state_shift.reshape(1, -1),
        step_bias,
        decay_log,
        skip_gain,
    )
    length = byte_rows.shape[0]
    table, inv, places = norm(n_head, groups, length, *carried, rank, starts)
    return expand(length, groups, starts, places, table, inv, norm_gain.reshape(1, -1))


def solution(mesh, groups=2048):
    placed = (
        P("ctx", None),
        P("ctx"),
        P(None, "head"),
        P(None, "head"),
        P(),
        P(None, "head"),
        P("head"),
        P("head"),
        P("head"),
        P(None, "head"),
        P("head"),
        P(),
        P(),
        P("head"),
    )
    return jax.shard_map(
        functools.partial(shards, groups),
        mesh=mesh,
        in_specs=placed,
        out_specs=P("ctx", "head"),
        check_vma=False,
    )
```

```python
import functools

import jax
import jax.numpy as jnp
from jax import lax
from jax.experimental import pallas as pl
from jax.experimental.pallas import tpu as pltpu
from jax.sharding import PartitionSpec as P

F32 = jnp.float32
BF16 = jnp.bfloat16
I32 = jnp.int32
HEAD_DIM = 64
STATE = 128
HEADS_HERE = 8
WIDE = HEADS_HERE * HEAD_DIM
INNER = 4096
T = 128
BLOCK = 256
SPAN = BLOCK + 16
UNROLL = 6
JOINED = 1
EPSILON = 1e-05
LOG_FLOOR = -1e4
MESH = pl.DeviceIdType.MESH


def on_chip(shape, kind):
    return pltpu.VMEM(shape, kind)


def keep_on_chip(array):
    return pltpu.with_memory_space_constraint(array, pltpu.VMEM)


def keep_off_chip(array):
    return pltpu.with_memory_space_constraint(array, pltpu.HBM)


def dot(a, b):
    return jnp.dot(a, b, preferred_element_type=F32)


def dot_tn(a, b):
    return lax.dot_general(a, b, (((0,), (0,)), ((), ())), preferred_element_type=F32)


def dot_nt(a, b):
    return lax.dot_general(a, b, (((1,), (1,)), ((), ())), preferred_element_type=F32)


def iota(shape, axis):
    return lax.broadcasted_iota(I32, shape, axis)


def silu(v):
    return 0.5 * v * (1.0 + jnp.tanh(0.5 * v))


def flag(condition):
    return jnp.where(condition, 1.0, 0.0).astype(BF16)


def pieces(v, count):
    out = []
    for _ in range(count):
        top = v.astype(BF16).astype(F32)
        out.append(top)
        v = v - top
    return out


def compact_kernel(
    groups,
    bnd_hbm,
    bytes_hbm,
    rows_ref,
    tail_ref,
    count_ref,
    rank_ref,
    start_ref,
    held,
    target,
    bnd_ref,
    sems,
    bnd_sem,
):
    blocks = bytes_hbm.shape[0] // BLOCK
    lines = 2 * blocks
    width = rows_ref.shape[1]

    def fetch(j):
        at = pl.ds(pl.multiple_of(j * BLOCK, BLOCK), BLOCK)
        return pltpu.make_async_copy(bytes_hbm.at[at], held.at[at], sems.at[j])

    def begin(j, carry):
        fetch(j).start()
        return carry

    flags = pltpu.make_async_copy(bnd_hbm, bnd_ref, bnd_sem)
    flags.start()
    lax.fori_loop(0, blocks, begin, 0)
    flags.wait()

    bnd = bnd_ref[...].reshape(lines, 128).astype(F32)
    bnd16 = bnd.astype(BF16)
    inside = dot(bnd16, flag(iota((128, 128), 0) <= iota((128, 128), 1)))
    above = dot(flag(iota((lines, lines), 1) < iota((lines, lines), 0)), bnd16)
    before = jnp.sum(above, axis=1, keepdims=True)
    upto = inside + before
    target[...] = jnp.where(bnd > 0, upto - 1.0, -1.0).astype(I32)
    rank_ref[...] = jnp.concatenate([upto, jnp.zeros((128 - lines, 128), F32)], 0).T
    for j in range(blocks):
        start_ref[j] = before[2 * j, 0].astype(I32)
    count = upto[lines - 1, 127].astype(I32)
    count_ref[...] = jnp.full(count_ref.shape, count, I32)
    rows_ref[0:16, :] = jnp.zeros((16, width), BF16)

    def step(j, carry):
        fetch(j).wait()
        base = pl.multiple_of((start_ref[j] // 16) * 16, 16)
        places = iota((SPAN, 128), 0) + base
        left = places == target[pl.ds(2 * j, 1), :]
        right = places == target[pl.ds(2 * j + 1, 1), :]
        choose = jnp.concatenate([flag(left), flag(right)], 1)
        here = pl.ds(pl.multiple_of(j * BLOCK, BLOCK), BLOCK)
        piece = min(512, width)
        for c in range(0, width, piece):
            cols = pl.ds(c, piece)
            picked = dot(choose, held[here, cols]).astype(BF16)
            rows_ref[pl.ds(base, 16), cols] = rows_ref[pl.ds(base, 16), cols] + picked[:16]
            rows_ref[pl.ds(pl.multiple_of(base + 16, 16), BLOCK), cols] = picked[16:]
        return carry

    def steps(i, carry):
        for q in range(JOINED):
            step(i * JOINED + q, 0)
        return carry

    lax.fori_loop(0, blocks // JOINED, steps, 0)

    clear = (start_ref[blocks - 1] // 16) * 16 + SPAN

    def wipe(i, carry):
        rows_ref[pl.ds(pl.multiple_of(clear + 16 * i, 16), 16), :] = jnp.zeros((16, width), BF16)
        return carry

    lax.fori_loop(0, jnp.maximum(groups + 32 - clear, 0) // 16, wipe, 0)
    near = pl.multiple_of((jnp.maximum(count - 4, 0) // 16) * 16, 16)
    row, column = iota((16, 32), 0), iota((16, 32), 1)
    wanted = count - 16 + row
    choose = flag((row >= 12) & (wanted >= 0) & (column + near == wanted))
    last = dot(choose, rows_ref[pl.ds(near, 32), :])
    few = jnp.minimum(count, 4).astype(F32)
    tail_ref[...] = jnp.where(iota(last.shape, 0) == 0, few, last).astype(BF16)


def compact(boundary, byte_rows, groups):
    length, width = byte_rows.shape
    blocks = length // BLOCK
    vmem = pl.BlockSpec(memory_space=pltpu.VMEM)
    return pl.pallas_call(
        functools.partial(compact_kernel, groups),
        out_shape=[
            on_chip((groups + SPAN, width), BF16),
            on_chip((16, width), BF16),
            on_chip((8, 128), I32),
            on_chip((128, 128), F32),
            jax.ShapeDtypeStruct((blocks,), I32),
        ],
        in_specs=[pl.BlockSpec(memory_space=pltpu.HBM)] * 2,
        out_specs=[vmem, vmem, vmem, vmem, pl.BlockSpec(memory_space=pltpu.SMEM)],
        scratch_shapes=[
            pltpu.VMEM((length, width), BF16),
            pltpu.VMEM((2 * blocks, 128), I32),
            pltpu.VMEM((length,), I32),
            pltpu.SemaphoreType.DMA((blocks,)),
            pltpu.SemaphoreType.DMA,
        ],
        compiler_params=pltpu.CompilerParams(vmem_limit_bytes=18 << 20),
        cost_estimate=pl.CostEstimate(
            flops=2 * SPAN * length * width, bytes_accessed=2 * length * width, transcendentals=0
        ),
    )(boundary, byte_rows)


def head_column(ref, shape):
    head = iota(shape, 0) % HEADS_HERE
    out = jnp.zeros(shape, F32)
    for h in range(HEADS_HERE):
        out = jnp.where(head == h, ref[h], out)
    return out


def start_all(copy, count):
    lax.fori_loop(1, count, lambda d, c: (copy(d).start(), c)[1], 0)


def wait_all(sent, send_sem, landed, recv_sem):
    for ref, sem in ((sent, send_sem), (landed, recv_sem)):
        both = ref.at[pl.ds(0, landed.shape[0] - 1)]
        pltpu.make_async_copy(both, both, sem).wait()


def layer_kernel(
    n_ctx,
    groups,
    rows_ref,
    tail_ref,
    count_ref,
    value_ref,
    gate_ref,
    state_ref,
    step_ref,
    vconv_ref,
    vshift_ref,
    sconv_ref,
    sshift_ref,
    bias_ref,
    log_ref,
    skip_ref,
    mix,
    open_gate,
    grow,
    locs,
    fades,
    maps,
    base,
    lead_ref,
    ext_0,
    ext_a,
    ext_b,
    ext_h,
    taps,
    factors,
    xs,
    raw_step,
    lead_t,
    lead_e,
    minus,
    sel_d,
    sel_e,
    near,
    halo_gate,
    ends_out,
    ends_in,
    out_slices,
    in_slices,
    ret_out,
    ret_in,
    entry,
    near_send,
    near_recv,
    end_send,
    end_recv,
    out_send,
    out_recv,
    ret_send,
    ret_recv,
):
    me = lax.axis_index("ctx")
    subs = groups // T
    share = STATE * 4 // n_ctx
    big = 2 * T
    bigs = groups // big

    barrier = pltpu.get_barrier_semaphore()

    def greet_ctx(d, carry):
        pl.semaphore_signal(
            barrier, inc=1, device_id={"ctx": lax.rem(me + d, n_ctx)}, device_id_type=MESH
        )
        return carry

    lax.fori_loop(1, n_ctx, greet_ctx, 0)

    def near_copy(d):
        return pltpu.make_async_remote_copy(
            src_ref=tail_ref,
            dst_ref=near.at[d - 1],
            send_sem=near_send.at[d - 1],
            recv_sem=near_recv.at[d - 1],
            device_id={"ctx": lax.rem(me + d, n_ctx)},
            device_id_type=MESH,
        )

    def end_copy(d):
        to = lax.rem(me + d, n_ctx)
        return pltpu.make_async_remote_copy(
            src_ref=ends_out.at[lax.rem(to, 4)],
            dst_ref=ends_in.at[me],
            send_sem=end_send,
            recv_sem=end_recv,
            device_id={"ctx": to},
            device_id_type=MESH,
        )

    def out_copy(d):
        to = lax.rem(me + d, n_ctx)
        return pltpu.make_async_remote_copy(
            src_ref=out_slices.at[to],
            dst_ref=in_slices.at[me],
            send_sem=out_send,
            recv_sem=out_recv,
            device_id={"ctx": to},
            device_id_type=MESH,
        )

    def ret_copy(d):
        to = lax.rem(me + d, n_ctx)
        return pltpu.make_async_remote_copy(
            src_ref=ret_out.at[to],
            dst_ref=ret_in.at[me],
            send_sem=ret_send,
            recv_sem=ret_recv,
            device_id={"ctx": to},
            device_id_type=MESH,
        )

    for i in range(groups // 512):
        got = dot_nt(step_ref[...], rows_ref[i * 512 : (i + 1) * 512, :])
        for q in range(4):
            k = i * 4 + q
            raw_step[k * 8 : (k + 1) * 8, :] = got[:, q * T : (q + 1) * T]

    shape = (subs * 8, T)
    raw = raw_step[...] + head_column(bias_ref, shape)
    soft = jnp.maximum(raw, 0.0) + jnp.log1p(jnp.exp(-jnp.abs(raw)))
    valid = (iota(shape, 0) // 8) * T + iota(shape, 1) < count_ref[0:1, :]
    step = jnp.where(valid, soft, 0.0)
    logs = jnp.where(valid, jnp.maximum(jnp.log(soft), LOG_FLOOR), LOG_FLOOR)
    decay = -step * jnp.exp(head_column(log_ref, shape))
    tri = flag(iota((T, T), 0) <= iota((T, T), 1))
    d0, d1, d2 = pieces(decay, 3)
    cum = (dot(d0.astype(BF16), tri) + dot(d1.astype(BF16), tri)) + dot(d2.astype(BF16), tri)
    def project(block, ext):
        here = pl.ds(pl.multiple_of(block * big, big), big)
        for weights, first, count in ((value_ref, 0, 4), (state_ref, 4, 2)):
            got = dot(rows_ref[here, :], weights[...])
            for c in range(count):
                ext[first + c, 8 : 8 + big, :] = got[:, c * 128 : (c + 1) * 128]

    def hand_on(source, ext):
        for c in range(6):
            ext[c, 0:8, :] = source[c, big : big + 8, :]

    project(0, ext_0)
    project(1, ext_a)
    hand_on(ext_0, ext_a)
    total = jnp.broadcast_to(cum[:, T - 1 : T], shape)
    cums = pieces(cum, 3)
    lows = pieces(logs - cum, 3)
    grows = pieces(jnp.exp(cum), 2)
    tails = pieces(jnp.exp(total - cum) * step, 2)

    over = total[0:8]
    for k in range(1, subs):
        over = over + total[k * 8 : (k + 1) * 8]
    high, low = pieces(jnp.exp(over), 2)
    first_half = iota((8, T), 1) < HEAD_DIM
    for c in range(4):
        both = [
            jnp.where(
                first_half,
                jnp.broadcast_to(part[2 * c : 2 * c + 1], (8, T)),
                jnp.broadcast_to(part[2 * c + 1 : 2 * c + 2], (8, T)),
            )
            for part in (high, low)
        ]
        ends_out[c] = jnp.concatenate(both, 0).astype(BF16)

    for k in range(subs):
        at = slice(k * 8, (k + 1) * 8)
        lead_t[k] = jnp.concatenate([p[at] for p in cums] + [jnp.ones((24, T), F32)], 0).astype(BF16)
        lead_e[k] = jnp.concatenate([p[at] for p in grows + tails], 0).astype(BF16)
        minus[k] = jnp.concatenate([p[at] for p in lows], 0)
    wide_shape = (subs * 8, WIDE)
    own = iota(wide_shape, 0) % 8 == iota(wide_shape, 1) // HEAD_DIM
    fade = jnp.where(own, jnp.concatenate([jnp.exp(total)] * 4, 1), 0.0)
    which = flag(iota((subs, subs * 8), 1) // 8 == iota((subs, subs * 8), 0))
    f0, f1 = pieces(fade, 2)
    fade = dot(which, f0.astype(BF16)) + dot(which, f1.astype(BF16))
    for k in range(subs):
        factors[k] = fade[k : k + 1, :]
    head_of = iota((24, 8 * T), 0) % 8
    sel_d[...] = flag(head_of == iota((24, 8 * T), 1) // T).astype(F32)
    row, lane = iota((32, 2 * WIDE), 0), iota((32, 2 * WIDE), 1)
    sel_e[...] = flag((row % 8 == (lane % WIDE) // HEAD_DIM) & ((row < 16) == (lane < WIDE)))
    for c in range(6):
        tap, move, at = (
            (vconv_ref, vshift_ref, slice(c * 128, (c + 1) * 128))
            if c < 4
            else (sconv_ref, sshift_ref, slice((c - 4) * 128, (c - 3) * 128))
        )
        taps[c, 0:4, :] = 0.5 * tap[:, at]
        taps[c, 4:5, :] = 0.5 * move[:, at]

    def convolve(ext, c, at, length):
        h = taps[c, 4:5, :] + taps[c, 0:1, :] * ext[c, at + 5 : at + 5 + length, :]
        for j in range(1, 4):
            h = h + taps[c, j : j + 1, :] * ext[c, at + 5 + j : at + 5 + j + length, :]
        return h + h * jnp.tanh(h)

    for k in (0, 2):
        locs[k] = jnp.zeros((STATE, WIDE), F32)
        fades[k] = jnp.ones((1, WIDE), F32)

    def advance(block, ext, onto, target):
        tails = [dot_tn(lead_e[block * 2 + q], sel_e[:, WIDE:]) for q in range(2)]
        if target is not None:
            project(target, onto)
        for q in range(2):
            k = block * 2 + q
            at = pl.ds(pl.multiple_of(k * T, T), T)
            weighted = []
            for c in range(4):
                x = convolve(ext, c, q * T, T)
                xs[at, c * 128 : (c + 1) * 128] = x.astype(BF16)
                tail = tails[q][:, c * 128 : (c + 1) * 128]
                weighted.append((x * tail).astype(BF16))
            for c in range(2):
                maps[at, c * 128 : (c + 1) * 128] = convolve(ext, 4 + c, q * T, T).astype(BF16)
            new = dot_tn(maps[at, :STATE], jnp.concatenate(weighted, 1))
            factor = factors[k]
            locs[k + 1] = factor * locs[k] + new
            fades[k + 1] = factor * fades[k]

    def local(j, carry):
        advance(2 * j + 1, ext_a, ext_b, 2 * j + 2)
        hand_on(ext_a, ext_b)
        advance(2 * j + 2, ext_b, ext_a, 2 * j + 3)
        hand_on(ext_b, ext_a)
        return carry

    pl.semaphore_wait(barrier, n_ctx - 1)
    near_copy(1).start()
    near_copy(2).start()

    ends_in[me] = ends_out[lax.rem(me, 4)]
    start_all(end_copy, n_ctx)

    lax.fori_loop(0, bigs // 2 - 1, local, 0)

    near_copy(1).wait()
    near_copy(2).wait()
    first = jnp.where(me >= 1, near[0].astype(F32), 0.0)
    second = jnp.where(me >= 2, near[1].astype(F32), 0.0)
    few = jnp.broadcast_to(near[0][0:1, 0:16].astype(F32), (16, 16))
    few = jnp.where(me >= 1, few, 4.0)
    row, lane = iota((16, 16), 0), iota((16, 16), 1)
    shift = flag((row >= 12) & (lane >= 12) & (lane.astype(F32) == row.astype(F32) + few))
    halo = dot(shift, second.astype(BF16)) + jnp.where(iota(first.shape, 0) >= 12, first, 0.0)
    halo = halo.astype(BF16)
    for weights, first, count in ((value_ref, 0, 4), (state_ref, 4, 2)):
        got = dot(halo, weights[...])
        for c in range(count):
            ext_h[first + c, 8:24, :] = got[:, c * 128 : (c + 1) * 128]
    halo_gate[...] = silu(dot(halo, gate_ref[...]))
    for c in range(6):
        ext_h[c, 0:8, :] = jnp.zeros((8, 128), F32)
        ext_0[c, 0:8, :] = ext_h[c, 16:24, :]
    advance(bigs - 1, ext_a, None, None)
    advance(0, ext_0, None, None)
    x_h = jnp.concatenate([convolve(ext_h, c, 0, 16) for c in range(4)], 1)
    c_h = convolve(ext_h, 5, 0, 16).astype(BF16)

    locs[subs] = locs[subs] + fades[subs] * locs[2]

    for k in range(n_ctx):
        r, c = (k // 4) * share, (k % 4) * 128
        out_slices[k] = locs[subs, r : r + share, c : c + 128].astype(BF16)
    in_slices[me] = out_slices[me]
    start_all(out_copy, n_ctx)

    skip = jnp.zeros((1, WIDE), F32)
    for h in range(HEADS_HERE):
        skip = jnp.where(iota((1, WIDE), 1) // HEAD_DIM == h, skip_ref[h], skip)
    lower = iota((T, T), 1) <= iota((T, T), 0)
    left_half = iota((T, T), 1) < HEAD_DIM

    wide = min(8 * T, groups // 2)

    def inside(i, carry):
        g0 = pl.multiple_of(i * wide, wide)
        here = pl.ds(g0, wide)
        parts = []
        for q in range(wide // T):
            k = i * (wide // T) + q
            at = pl.ds(pl.multiple_of(g0 + q * T, T), T)
            grow[k] = dot_tn(lead_e[k], sel_e[:, :WIDE])
            m = maps[at, :]
            scores = jnp.where(lower, dot_nt(m[:, STATE:], m[:, :STATE]), 0.0)
            tile = jnp.concatenate([minus[k]] * HEADS_HERE, 1) * sel_d[...]
            right = jnp.concatenate([sel_d[...], tile], 0).astype(BF16)
            parts.append((at, scores, dot_tn(lead_t[k], right)))
        opened = dot(rows_ref[here, :], gate_ref[...])
        for at, scores, spread in parts:
            x = xs[at, :]
            for p in range(HEADS_HERE // 2):
                pair = x[:, p * T : (p + 1) * T]
                weight = jnp.exp(jnp.minimum(spread[:, 2 * p * T : 2 * (p + 1) * T], 60.0))
                weight = (weight * jnp.concatenate([scores, scores], 1)).astype(BF16)
                stacked = jnp.concatenate(
                    [
                        jnp.where(left_half, pair, jnp.zeros_like(pair)),
                        jnp.where(left_half, jnp.zeros_like(pair), pair),
                    ],
                    0,
                )
                got = dot(weight, stacked)
                cols = slice(p * T, (p + 1) * T)
                mix[at, cols] = got + skip[:, cols] * pair.astype(F32)
        open_gate[here, :] = silu(opened)
        return carry

    half = groups // wide // 2
    lax.fori_loop(0, half, inside, 0)

    wait_all(ends_in, end_send, ends_in, end_recv)
    wait_all(out_slices, out_send, in_slices, out_recv)
    running = jnp.zeros((share, 128), F32)
    for i in range(n_ctx):
        ret_out[i] = running.astype(BF16)
        factor = ends_in[i].astype(F32)
        factor = factor[0:1] + factor[8:9]
        running = factor * running + in_slices[i].astype(F32)
    ret_in[me] = ret_out[me]
    start_all(ret_copy, n_ctx)

    lax.fori_loop(half, groups // wide, inside, 0)

    wait_all(ret_out, ret_send, ret_in, ret_recv)
    for k in range(n_ctx):
        r, c = (k // 4) * share, (k % 4) * 128
        entry[r : r + share, c : c + 128] = ret_in[k]

    base[0] = entry[...].astype(F32)
    base[1] = locs[2] + fades[2] * base[0]
    y_h = dot(c_h, entry[...]) + skip * x_h
    lead_ref[...] = y_h * halo_gate[...]


def line_of(start, groups):
    return jnp.minimum((start + T - 1) // T, (groups + T - window_of(groups)) // T)


def window_of(groups):
    return min(3 * T, groups + T)


def norm_kernel(
    n_head,
    groups,
    mix,
    open_gate,
    grow,
    locs,
    fades,
    maps,
    base,
    lead_ref,
    rank_ref,
    start_ref,
    table,
    inv_ref,
    place_ref,
    squares,
    sq_send,
    sq_recv,
):
    column = lax.axis_index("head")
    subs = groups // T
    blocks = place_ref.shape[0] // BLOCK
    barrier = pltpu.get_barrier_semaphore()

    def greet_head(d, carry):
        pl.semaphore_signal(
            barrier, inc=1, device_id={"head": lax.rem(column + d, n_head)}, device_id_type=MESH
        )
        return carry

    lax.fori_loop(1, n_head, greet_head, 0)

    def sq_copy(d):
        return pltpu.make_async_remote_copy(
            src_ref=squares.at[column],
            dst_ref=squares.at[column],
            send_sem=sq_send,
            recv_sem=sq_recv,
            device_id={"head": lax.rem(column + d, n_head)},
            device_id_type=MESH,
        )

    ones = jnp.ones((8, WIDE), BF16)
    g_h = lead_ref[...]
    table[0 : T - 16, :] = jnp.zeros((T - 16, WIDE), BF16)
    table[T - 16 : T, :] = g_h.astype(BF16)
    power = jnp.concatenate([jnp.zeros((T - 16, WIDE), F32), g_h * g_h], 0).astype(BF16)
    mine = squares.at[column]
    mine[...] = jnp.zeros(mine.shape, F32)
    mine[0:1, :] = dot_nt(ones, power)[0:1, :]

    def outer(i, carry):
        for q in range(4):
            k = i * 4 + q
            at = pl.ds(pl.multiple_of(k * T, T), T)
            state = (locs[k] + fades[k] * base[jnp.where(k > 2, 1, 0)]).astype(BF16)
            gated = mix[at, :] + grow[k] * dot(maps[at, STATE:], state)
            gated = gated * open_gate[at, :]
            table[pl.ds(pl.multiple_of((k + 1) * T, T), T), :] = gated.astype(BF16)
            squares[column, pl.ds(k + 1, 1), :] = dot_nt(ones, (gated * gated).astype(BF16))[0:1, :]
        return carry

    lax.fori_loop(0, subs // 4, outer, 0)

    pl.semaphore_wait(barrier, n_head - 1)
    start_all(sq_copy, n_head)

    def locate(i, carry):
        for j in (2 * i, 2 * i + 1) if blocks % 2 == 0 else (i,):
            for half in range(2):
                lane = iota((T, T), 1)
                rank = jnp.sum(
                    jnp.where(lane == 2 * j + half, rank_ref[...], 0.0), axis=1, keepdims=True
                )
                first = (line_of(start_ref[j], groups) * T).astype(F32)
                place = jnp.broadcast_to(rank + ((T - 1.0) - first), (T, T))
                lane = lane.astype(F32)
                hits = [flag(place == lane + w * T) for w in range(window_of(groups) // T)]
                at = pl.ds(pl.multiple_of(j * BLOCK + half * T, T), T)
                place_ref[at, :] = jnp.concatenate(hits, 1)
        return carry

    lax.fori_loop(0, blocks // 2 if blocks % 2 == 0 else blocks, locate, 0)

    wait_all(squares, sq_send, squares, sq_recv)
    power = squares[0]
    for i in range(1, n_head):
        power = power + squares[i]
    inv_ref[...] = lax.rsqrt(power * (1.0 / (n_head * WIDE)) + EPSILON)


def norm(n_head, groups, length, *args):
    subs = groups // T
    lines = -(-(subs + 1) // 8) * 8
    vmem = pl.BlockSpec(memory_space=pltpu.VMEM)
    return pl.pallas_call(
        functools.partial(norm_kernel, n_head, groups),
        out_shape=[
            on_chip((groups + T, WIDE), BF16),
            on_chip((lines, T), F32),
            on_chip((length, window_of(groups)), BF16),
        ],
        in_specs=[vmem] * 9 + [pl.BlockSpec(memory_space=pltpu.SMEM)],
        out_specs=[vmem] * 3,
        scratch_shapes=[
            pltpu.VMEM((n_head, lines, T), F32),
            pltpu.SemaphoreType.DMA,
            pltpu.SemaphoreType.DMA,
        ],
        compiler_params=pltpu.CompilerParams(
            collective_id=1, has_side_effects=True, vmem_limit_bytes=8 << 20
        ),
        cost_estimate=pl.CostEstimate(
            flops=4 * groups * STATE * WIDE, bytes_accessed=1 << 20, transcendentals=0
        ),
    )(*args)


def layer(n_ctx, groups, *args):
    subs = groups // T
    share = STATE * 4 // n_ctx
    vmem = pl.BlockSpec(memory_space=pltpu.VMEM)
    smem = pl.BlockSpec(memory_space=pltpu.SMEM)
    width = args[0].shape[1]
    sem = pltpu.SemaphoreType.DMA
    return pl.pallas_call(
        functools.partial(layer_kernel, n_ctx, groups),
        out_shape=[
            on_chip((groups, WIDE), F32),
            on_chip((groups, WIDE), F32),
            on_chip((subs, T, WIDE), F32),
            on_chip((subs + 1, STATE, WIDE), F32),
            on_chip((subs + 1, 1, WIDE), F32),
            on_chip((groups, 2 * STATE), BF16),
            on_chip((2, STATE, WIDE), F32),
            on_chip((16, WIDE), F32),
        ],
        in_specs=[vmem] * 11 + [smem] * 3,
        out_specs=[vmem] * 8,
        scratch_shapes=[
            pltpu.VMEM((6, 2 * T + 8, 128), F32),
            pltpu.VMEM((6, 2 * T + 8, 128), F32),
            pltpu.VMEM((6, 2 * T + 8, 128), F32),
            pltpu.VMEM((6, 24, 128), F32),
            pltpu.VMEM((6, 8, 128), F32),
            pltpu.VMEM((subs, 1, WIDE), F32),
            pltpu.VMEM((groups, WIDE), BF16),
            pltpu.VMEM((subs * 8, T), F32),
            pltpu.VMEM((subs, 48, T), BF16),
            pltpu.VMEM((subs, 32, T), BF16),
            pltpu.VMEM((subs, 24, T), F32),
            pltpu.VMEM((24, 8 * T), F32),
            pltpu.VMEM((32, 2 * WIDE), BF16),
            pltpu.VMEM((2, 16, width), BF16),
            pltpu.VMEM((16, WIDE), F32),
            pltpu.VMEM((4, 16, 128), BF16),
            pltpu.VMEM((n_ctx, 16, 128), BF16),
            pltpu.VMEM((n_ctx, share, 128), BF16),
            pltpu.VMEM((n_ctx, share, 128), BF16),
            pltpu.VMEM((n_ctx, share, 128), BF16),
            pltpu.VMEM((n_ctx, share, 128), BF16),
            pltpu.VMEM((STATE, WIDE), BF16),
            sem((2,)),
            sem((2,)),
            sem,
            sem,
            sem,
            sem,
            sem,
            sem,
        ],
        compiler_params=pltpu.CompilerParams(
            collective_id=0, has_side_effects=True, vmem_limit_bytes=14 << 20
        ),
        cost_estimate=pl.CostEstimate(
            flops=2 * groups * width * 1536, bytes_accessed=8 << 20, transcendentals=1 << 22
        ),
    )(*args)


def expand_kernel(groups, start_ref, place_ref, table_ref, inv_ref, gain_ref, out_hbm, ready, sems):
    blocks = out_hbm.shape[0] // BLOCK
    window = window_of(groups)

    def send(j):
        at = pl.ds(pl.multiple_of(j * BLOCK, BLOCK), BLOCK)
        return pltpu.make_async_copy(ready.at[at], out_hbm.at[at], sems.at[j])

    def step(j, carry):
        line = line_of(start_ref[j], groups)
        at = pl.ds(pl.multiple_of(j * BLOCK, BLOCK), BLOCK)
        places = place_ref[at, :]
        got = dot(places, table_ref[pl.ds(pl.multiple_of(line * T, T), window), :])
        scale = jnp.zeros((BLOCK, T), F32)
        for w in range(window // T):
            scale = scale + places[:, w * T : (w + 1) * T].astype(F32) * inv_ref[pl.ds(line + w, 1), :]
        ready[at, :] = got * gain_ref[...] * jnp.sum(scale, axis=1, keepdims=True)
        send(j).start()
        return carry

    def steps(i, carry):
        for q in range(UNROLL):
            step(i * UNROLL + q, 0)
        return carry

    lax.fori_loop(0, blocks // UNROLL, steps, 0)
    for j in range(blocks - blocks % UNROLL, blocks):
        step(j, 0)

    def finish(j, carry):
        send(j).wait()
        return carry

    lax.fori_loop(0, blocks, finish, 0)


def expand(length, groups, starts, places, table, inv, gain):
    vmem = pl.BlockSpec(memory_space=pltpu.VMEM)
    return pl.pallas_call(
        functools.partial(expand_kernel, groups),
        out_shape=jax.ShapeDtypeStruct((length, WIDE), F32),
        in_specs=[pl.BlockSpec(memory_space=pltpu.SMEM), vmem, vmem, vmem, vmem],
        out_specs=pl.BlockSpec(memory_space=pl.ANY),
        scratch_shapes=[
            pltpu.VMEM((length, WIDE), F32),
            pltpu.SemaphoreType.DMA((length // BLOCK,)),
        ],
        compiler_params=pltpu.CompilerParams(vmem_limit_bytes=12 << 20),
        cost_estimate=pl.CostEstimate(
            flops=2 * length * 3 * T * WIDE, bytes_accessed=4 * length * WIDE, transcendentals=0
        ),
    )(starts, places, table, inv, gain)


def shards(
    groups,
    byte_rows,
    boundary,
    gate_proj,
    value_proj,
    state_proj,
    step_proj,
    step_bias,
    decay_log,
    skip_gain,
    value_conv,
    value_shift,
    state_conv,
    state_shift,
    norm_gain,
):
    n_ctx, n_head = lax.axis_size("ctx"), lax.axis_size("head")
    weights = [keep_on_chip(w) for w in (value_proj, gate_proj, state_proj, step_proj.T)]
    rows, tail, count, rank, starts = compact(
        keep_off_chip(boundary), keep_off_chip(byte_rows), groups
    )
    carried = layer(
        n_ctx,
        groups,
        rows,
        tail,
        count,
        *weights,
        value_conv,
        value_shift.reshape(1, -1),
        state_conv,
        state_shift.reshape(1, -1),
        step_bias,
        decay_log,
        skip_gain,
    )
    length = byte_rows.shape[0]
    table, inv, places = norm(n_head, groups, length, *carried, rank, starts)
    return expand(length, groups, starts, places, table, inv, norm_gain.reshape(1, -1))


def solution(mesh, groups=2048):
    placed = (
        P("ctx", None),
        P("ctx"),
        P(None, "head"),
        P(None, "head"),
        P(),
        P(None, "head"),
        P("head"),
        P("head"),
        P("head"),
        P(None, "head"),
        P("head"),
        P(),
        P(),
        P("head"),
    )
    return jax.shard_map(
        functools.partial(shards, groups),
        mesh=mesh,
        in_specs=placed,
        out_specs=P("ctx", "head"),
        check_vma=False,
    )
```

```python
import functools

import jax
import jax.numpy as jnp
from jax import lax
from jax.experimental import pallas as pl
from jax.experimental.pallas import tpu as pltpu
from jax.sharding import PartitionSpec as P

F32 = jnp.float32
BF16 = jnp.bfloat16
I32 = jnp.int32
HEAD_DIM = 64
STATE = 128
HEADS_HERE = 8
WIDE = HEADS_HERE * HEAD_DIM
INNER = 4096
T = 128
BLOCK = 256
SPAN = BLOCK + 16
UNROLL = 6
JOINED = 1
EPSILON = 1e-05
LOG_FLOOR = -1e4
MESH = pl.DeviceIdType.MESH


def on_chip(shape, kind):
    return pltpu.VMEM(shape, kind)


def keep_on_chip(array):
    return pltpu.with_memory_space_constraint(array, pltpu.VMEM)


def keep_off_chip(array):
    return pltpu.with_memory_space_constraint(array, pltpu.HBM)


def dot(a, b):
    return jnp.dot(a, b, preferred_element_type=F32)


def dot_tn(a, b):
    return lax.dot_general(a, b, (((0,), (0,)), ((), ())), preferred_element_type=F32)


def dot_nt(a, b):
    return lax.dot_general(a, b, (((1,), (1,)), ((), ())), preferred_element_type=F32)


def iota(shape, axis):
    return lax.broadcasted_iota(I32, shape, axis)


def silu(v):
    return 0.5 * v * (1.0 + jnp.tanh(0.5 * v))


def flag(condition):
    return jnp.where(condition, 1.0, 0.0).astype(BF16)


def pieces(v, count):
    out = []
    for _ in range(count):
        top = v.astype(BF16).astype(F32)
        out.append(top)
        v = v - top
    return out


def compact_kernel(
    groups,
    bnd_hbm,
    bytes_hbm,
    rows_ref,
    tail_ref,
    count_ref,
    rank_ref,
    start_ref,
    held,
    target,
    bnd_ref,
    sems,
    bnd_sem,
):
    blocks = bytes_hbm.shape[0] // BLOCK
    lines = 2 * blocks
    width = rows_ref.shape[1]

    def fetch(j):
        at = pl.ds(pl.multiple_of(j * BLOCK, BLOCK), BLOCK)
        return pltpu.make_async_copy(bytes_hbm.at[at], held.at[at], sems.at[j])

    def begin(j, carry):
        fetch(j).start()
        return carry

    flags = pltpu.make_async_copy(bnd_hbm, bnd_ref, bnd_sem)
    flags.start()
    lax.fori_loop(0, blocks, begin, 0)
    flags.wait()

    bnd = bnd_ref[...].reshape(lines, 128).astype(F32)
    bnd16 = bnd.astype(BF16)
    inside = dot(bnd16, flag(iota((128, 128), 0) <= iota((128, 128), 1)))
    above = dot(flag(iota((lines, lines), 1) < iota((lines, lines), 0)), bnd16)
    before = jnp.sum(above, axis=1, keepdims=True)
    upto = inside + before
    target[...] = jnp.where(bnd > 0, upto - 1.0, -1.0).astype(I32)
    rank_ref[...] = jnp.concatenate([upto, jnp.zeros((128 - lines, 128), F32)], 0).T
    for j in range(blocks):
        start_ref[j] = before[2 * j, 0].astype(I32)
    count = upto[lines - 1, 127].astype(I32)
    count_ref[...] = jnp.full(count_ref.shape, count, I32)
    rows_ref[0:16, :] = jnp.zeros((16, width), BF16)

    def step(j, carry):
        fetch(j).wait()
        base = pl.multiple_of((start_ref[j] // 16) * 16, 16)
        places = iota((SPAN, 128), 0) + base
        left = places == target[pl.ds(2 * j, 1), :]
        right = places == target[pl.ds(2 * j + 1, 1), :]
        choose = jnp.concatenate([flag(left), flag(right)], 1)
        here = pl.ds(pl.multiple_of(j * BLOCK, BLOCK), BLOCK)
        piece = min(512, width)
        for c in range(0, width, piece):
            cols = pl.ds(c, piece)
            picked = dot(choose, held[here, cols]).astype(BF16)
            rows_ref[pl.ds(base, 16), cols] = rows_ref[pl.ds(base, 16), cols] + picked[:16]
            rows_ref[pl.ds(pl.multiple_of(base + 16, 16), BLOCK), cols] = picked[16:]
        return carry

    def steps(i, carry):
        for q in range(JOINED):
            step(i * JOINED + q, 0)
        return carry

    lax.fori_loop(0, blocks // JOINED, steps, 0)

    clear = (start_ref[blocks - 1] // 16) * 16 + SPAN

    def wipe(i, carry):
        rows_ref[pl.ds(pl.multiple_of(clear + 16 * i, 16), 16), :] = jnp.zeros((16, width), BF16)
        return carry

    lax.fori_loop(0, jnp.maximum(groups + 32 - clear, 0) // 16, wipe, 0)
    near = pl.multiple_of((jnp.maximum(count - 4, 0) // 16) * 16, 16)
    row, column = iota((16, 32), 0), iota((16, 32), 1)
    wanted = count - 16 + row
    choose = flag((row >= 12) & (wanted >= 0) & (column + near == wanted))
    last = dot(choose, rows_ref[pl.ds(near, 32), :])
    few = jnp.minimum(count, 4).astype(F32)
    tail_ref[...] = jnp.where(iota(last.shape, 0) == 0, few, last).astype(BF16)


def compact(boundary, byte_rows, groups):
    length, width = byte_rows.shape
    blocks = length // BLOCK
    vmem = pl.BlockSpec(memory_space=pltpu.VMEM)
    return pl.pallas_call(
        functools.partial(compact_kernel, groups),
        out_shape=[
            on_chip((groups + SPAN, width), BF16),
            on_chip((16, width), BF16),
            on_chip((8, 128), I32),
            on_chip((128, 128), F32),
            jax.ShapeDtypeStruct((blocks,), I32),
        ],
        in_specs=[pl.BlockSpec(memory_space=pltpu.HBM)] * 2,
        out_specs=[vmem, vmem, vmem, vmem, pl.BlockSpec(memory_space=pltpu.SMEM)],
        scratch_shapes=[
            pltpu.VMEM((length, width), BF16),
            pltpu.VMEM((2 * blocks, 128), I32),
            pltpu.VMEM((length,), I32),
            pltpu.SemaphoreType.DMA((blocks,)),
            pltpu.SemaphoreType.DMA,
        ],
        compiler_params=pltpu.CompilerParams(vmem_limit_bytes=18 << 20),
        cost_estimate=pl.CostEstimate(
            flops=2 * SPAN * length * width, bytes_accessed=2 * length * width, transcendentals=0
        ),
    )(boundary, byte_rows)


def head_column(ref, shape):
    head = iota(shape, 0) % HEADS_HERE
    out = jnp.zeros(shape, F32)
    for h in range(HEADS_HERE):
        out = jnp.where(head == h, ref[h], out)
    return out


def start_all(copy, count):
    lax.fori_loop(1, count, lambda d, c: (copy(d).start(), c)[1], 0)


def wait_all(sent, send_sem, landed, recv_sem):
    for ref, sem in ((sent, send_sem), (landed, recv_sem)):
        both = ref.at[pl.ds(0, landed.shape[0] - 1)]
        pltpu.make_async_copy(both, both, sem).wait()


def layer_kernel(
    n_ctx,
    groups,
    rows_ref,
    tail_ref,
    count_ref,
    value_ref,
    gate_ref,
    state_ref,
    step_ref,
    vconv_ref,
    vshift_ref,
    sconv_ref,
    sshift_ref,
    bias_ref,
    log_ref,
    skip_ref,
    mix,
    open_gate,
    grow,
    locs,
    fades,
    maps,
    base,
    lead_ref,
    ext_0,
    ext_a,
    ext_b,
    ext_h,
    taps,
    factors,
    xs,
    raw_step,
    lead_t,
    lead_e,
    minus,
    sel_d,
    sel_e,
    near,
    halo_gate,
    ends_out,
    ends_in,
    out_slices,
    in_slices,
    ret_out,
    ret_in,
    entry,
    near_send,
    near_recv,
    end_send,
    end_recv,
    out_send,
    out_recv,
    ret_send,
    ret_recv,
):
    me = lax.axis_index("ctx")
    subs = groups // T
    share = STATE * 4 // n_ctx
    big = 2 * T
    bigs = groups // big

    barrier = pltpu.get_barrier_semaphore()

    def greet_ctx(d, carry):
        pl.semaphore_signal(
            barrier, inc=1, device_id={"ctx": lax.rem(me + d, n_ctx)}, device_id_type=MESH
        )
        return carry

    lax.fori_loop(1, n_ctx, greet_ctx, 0)

    def near_copy(d):
        return pltpu.make_async_remote_copy(
            src_ref=tail_ref,
            dst_ref=near.at[d - 1],
            send_sem=near_send.at[d - 1],
            recv_sem=near_recv.at[d - 1],
            device_id={"ctx": lax.rem(me + d, n_ctx)},
            device_id_type=MESH,
        )

    def end_copy(d):
        to = lax.rem(me + d, n_ctx)
        return pltpu.make_async_remote_copy(
            src_ref=ends_out.at[lax.rem(to, 4)],
            dst_ref=ends_in.at[me],
            send_sem=end_send,
            recv_sem=end_recv,
            device_id={"ctx": to},
            device_id_type=MESH,
        )

    def out_copy(d):
        to = lax.rem(me + d, n_ctx)
        return pltpu.make_async_remote_copy(
            src_ref=out_slices.at[to],
            dst_ref=in_slices.at[me],
            send_sem=out_send,
            recv_sem=out_recv,
            device_id={"ctx": to},
            device_id_type=MESH,
        )

    def ret_copy(d):
        to = lax.rem(me + d, n_ctx)
        return pltpu.make_async_remote_copy(
            src_ref=ret_out.at[to],
            dst_ref=ret_in.at[me],
            send_sem=ret_send,
            recv_sem=ret_recv,
            device_id={"ctx": to},
            device_id_type=MESH,
        )

    for i in range(groups // 512):
        got = dot_nt(step_ref[...], rows_ref[i * 512 : (i + 1) * 512, :])
        for q in range(4):
            k = i * 4 + q
            raw_step[k * 8 : (k + 1) * 8, :] = got[:, q * T : (q + 1) * T]

    shape = (subs * 8, T)
    raw = raw_step[...] + head_column(bias_ref, shape)
    soft = jnp.maximum(raw, 0.0) + jnp.log1p(jnp.exp(-jnp.abs(raw)))
    valid = (iota(shape, 0) // 8) * T + iota(shape, 1) < count_ref[0:1, :]
    step = jnp.where(valid, soft, 0.0)
    logs = jnp.where(valid, jnp.maximum(jnp.log(soft), LOG_FLOOR), LOG_FLOOR)
    decay = -step * jnp.exp(head_column(log_ref, shape))
    tri = flag(iota((T, T), 0) <= iota((T, T), 1))
    d0, d1, d2 = pieces(decay, 3)
    cum = (dot(d0.astype(BF16), tri) + dot(d1.astype(BF16), tri)) + dot(d2.astype(BF16), tri)
    def project(block, ext):
        here = pl.ds(pl.multiple_of(block * big, big), big)
        for weights, first, count in ((value_ref, 0, 4), (state_ref, 4, 2)):
            got = dot(rows_ref[here, :], weights[...])
            for c in range(count):
                ext[first + c, 8 : 8 + big, :] = got[:, c * 128 : (c + 1) * 128]

    def hand_on(source, ext):
        for c in range(6):
            ext[c, 0:8, :] = source[c, big : big + 8, :]

    project(0, ext_0)
    project(1, ext_a)
    hand_on(ext_0, ext_a)
    total = jnp.broadcast_to(cum[:, T - 1 : T], shape)
    cums = pieces(cum, 3)
    lows = pieces(logs - cum, 3)
    grows = pieces(jnp.exp(cum), 2)
    tails = pieces(jnp.exp(total - cum) * step, 2)

    over = total[0:8]
    for k in range(1, subs):
        over = over + total[k * 8 : (k + 1) * 8]
    high, low = pieces(jnp.exp(over), 2)
    first_half = iota((8, T), 1) < HEAD_DIM
    for c in range(4):
        both = [
            jnp.where(
                first_half,
                jnp.broadcast_to(part[2 * c : 2 * c + 1], (8, T)),
                jnp.broadcast_to(part[2 * c + 1 : 2 * c + 2], (8, T)),
            )
            for part in (high, low)
        ]
        ends_out[c] = jnp.concatenate(both, 0).astype(BF16)

    for k in range(subs):
        at = slice(k * 8, (k + 1) * 8)
        lead_t[k] = jnp.concatenate([p[at] for p in cums] + [jnp.ones((24, T), F32)], 0).astype(BF16)
        lead_e[k] = jnp.concatenate([p[at] for p in grows + tails], 0).astype(BF16)
        minus[k] = jnp.concatenate([p[at] for p in lows], 0)
    wide_shape = (subs * 8, WIDE)
    own = iota(wide_shape, 0) % 8 == iota(wide_shape, 1) // HEAD_DIM
    fade = jnp.where(own, jnp.concatenate([jnp.exp(total)] * 4, 1), 0.0)
    which = flag(iota((subs, subs * 8), 1) // 8 == iota((subs, subs * 8), 0))
    f0, f1 = pieces(fade, 2)
    fade = dot(which, f0.astype(BF16)) + dot(which, f1.astype(BF16))
    for k in range(subs):
        factors[k] = fade[k : k + 1, :]
    head_of = iota((24, 8 * T), 0) % 8
    sel_d[...] = flag(head_of == iota((24, 8 * T), 1) // T).astype(F32)
    row, lane = iota((32, 2 * WIDE), 0), iota((32, 2 * WIDE), 1)
    sel_e[...] = flag((row % 8 == (lane % WIDE) // HEAD_DIM) & ((row < 16) == (lane < WIDE)))
    for c in range(6):
        tap, move, at = (
            (vconv_ref, vshift_ref, slice(c * 128, (c + 1) * 128))
            if c < 4
            else (sconv_ref, sshift_ref, slice((c - 4) * 128, (c - 3) * 128))
        )
        taps[c, 0:4, :] = 0.5 * tap[:, at]
        taps[c, 4:5, :] = 0.5 * move[:, at]

    def convolve(ext, c, at, length):
        h = taps[c, 4:5, :] + taps[c, 0:1, :] * ext[c, at + 5 : at + 5 + length, :]
        for j in range(1, 4):
            h = h + taps[c, j : j + 1, :] * ext[c, at + 5 + j : at + 5 + j + length, :]
        return h + h * jnp.tanh(h)

    for k in (0, 2):
        locs[k] = jnp.zeros((STATE, WIDE), F32)
        fades[k] = jnp.ones((1, WIDE), F32)

    def advance(block, ext, onto, target):
        tails = [dot_tn(lead_e[block * 2 + q], sel_e[:, WIDE:]) for q in range(2)]
        if target is not None:
            project(target, onto)
        for q in range(2):
            k = block * 2 + q
            at = pl.ds(pl.multiple_of(k * T, T), T)
            weighted = []
            for c in range(4):
                x = convolve(ext, c, q * T, T)
                xs[at, c * 128 : (c + 1) * 128] = x.astype(BF16)
                tail = tails[q][:, c * 128 : (c + 1) * 128]
                weighted.append((x * tail).astype(BF16))
            for c in range(2):
                maps[at, c * 128 : (c + 1) * 128] = convolve(ext, 4 + c, q * T, T).astype(BF16)
            new = dot_tn(maps[at, :STATE], jnp.concatenate(weighted, 1))
            factor = factors[k]
            locs[k + 1] = factor * locs[k] + new
            fades[k + 1] = factor * fades[k]

    def local(j, carry):
        advance(2 * j + 1, ext_a, ext_b, 2 * j + 2)
        hand_on(ext_a, ext_b)
        advance(2 * j + 2, ext_b, ext_a, 2 * j + 3)
        hand_on(ext_b, ext_a)
        return carry

    pl.semaphore_wait(barrier, n_ctx - 1)
    near_copy(1).start()
    near_copy(2).start()

    ends_in[me] = ends_out[lax.rem(me, 4)]
    start_all(end_copy, n_ctx)

    lax.fori_loop(0, bigs // 2 - 1, local, 0)

    near_copy(1).wait()
    near_copy(2).wait()
    first = jnp.where(me >= 1, near[0].astype(F32), 0.0)
    second = jnp.where(me >= 2, near[1].astype(F32), 0.0)
    few = jnp.broadcast_to(near[0][0:1, 0:16].astype(F32), (16, 16))
    few = jnp.where(me >= 1, few, 4.0)
    row, lane = iota((16, 16), 0), iota((16, 16), 1)
    shift = flag((row >= 12) & (lane >= 12) & (lane.astype(F32) == row.astype(F32) + few))
    halo = dot(shift, second.astype(BF16)) + jnp.where(iota(first.shape, 0) >= 12, first, 0.0)
    halo = halo.astype(BF16)
    for weights, first, count in ((value_ref, 0, 4), (state_ref, 4, 2)):
        got = dot(halo, weights[...])
        for c in range(count):
            ext_h[first + c, 8:24, :] = got[:, c * 128 : (c + 1) * 128]
    halo_gate[...] = silu(dot(halo, gate_ref[...]))
    for c in range(6):
        ext_h[c, 0:8, :] = jnp.zeros((8, 128), F32)
        ext_0[c, 0:8, :] = ext_h[c, 16:24, :]
    advance(bigs - 1, ext_a, None, None)
    advance(0, ext_0, None, None)
    x_h = jnp.concatenate([convolve(ext_h, c, 0, 16) for c in range(4)], 1)
    c_h = convolve(ext_h, 5, 0, 16).astype(BF16)

    locs[subs] = locs[subs] + fades[subs] * locs[2]

    for k in range(n_ctx):
        r, c = (k // 4) * share, (k % 4) * 128
        out_slices[k] = locs[subs, r : r + share, c : c + 128].astype(BF16)
    in_slices[me] = out_slices[me]
    start_all(out_copy, n_ctx)

    skip = jnp.zeros((1, WIDE), F32)
    for h in range(HEADS_HERE):
        skip = jnp.where(iota((1, WIDE), 1) // HEAD_DIM == h, skip_ref[h], skip)
    lower = iota((T, T), 1) <= iota((T, T), 0)
    left_half = iota((T, T), 1) < HEAD_DIM

    wide = min(8 * T, groups // 2)

    def inside(i, carry):
        g0 = pl.multiple_of(i * wide, wide)
        here = pl.ds(g0, wide)
        parts = []
        for q in range(wide // T):
            k = i * (wide // T) + q
            at = pl.ds(pl.multiple_of(g0 + q * T, T), T)
            grow[k] = dot_tn(lead_e[k], sel_e[:, :WIDE])
            m = maps[at, :]
            scores = jnp.where(lower, dot_nt(m[:, STATE:], m[:, :STATE]), 0.0)
            tile = jnp.concatenate([minus[k]] * HEADS_HERE, 1) * sel_d[...]
            right = jnp.concatenate([sel_d[...], tile], 0).astype(BF16)
            parts.append((at, scores, dot_tn(lead_t[k], right)))
        opened = dot(rows_ref[here, :], gate_ref[...])
        for at, scores, spread in parts:
            x = xs[at, :]
            for p in range(HEADS_HERE // 2):
                pair = x[:, p * T : (p + 1) * T]
                weight = jnp.exp(jnp.minimum(spread[:, 2 * p * T : 2 * (p + 1) * T], 60.0))
                weight = (weight * jnp.concatenate([scores, scores], 1)).astype(BF16)
                stacked = jnp.concatenate(
                    [
                        jnp.where(left_half, pair, jnp.zeros_like(pair)),
                        jnp.where(left_half, jnp.zeros_like(pair), pair),
                    ],
                    0,
                )
                got = dot(weight, stacked)
                cols = slice(p * T, (p + 1) * T)
                mix[at, cols] = got + skip[:, cols] * pair.astype(F32)
        open_gate[here, :] = silu(opened)
        return carry

    half = groups // wide // 2
    lax.fori_loop(0, half, inside, 0)

    wait_all(ends_in, end_send, ends_in, end_recv)
    wait_all(out_slices, out_send, in_slices, out_recv)
    running = jnp.zeros((share, 128), F32)
    for i in range(n_ctx):
        ret_out[i] = running.astype(BF16)
        factor = ends_in[i].astype(F32)
        factor = factor[0:1] + factor[8:9]
        running = factor * running + in_slices[i].astype(F32)
    ret_in[me] = ret_out[me]
    start_all(ret_copy, n_ctx)

    lax.fori_loop(half, groups // wide, inside, 0)

    wait_all(ret_out, ret_send, ret_in, ret_recv)
    for k in range(n_ctx):
        r, c = (k // 4) * share, (k % 4) * 128
        entry[r : r + share, c : c + 128] = ret_in[k]

    base[0] = entry[...].astype(F32)
    base[1] = locs[2] + fades[2] * base[0]
    y_h = dot(c_h, entry[...]) + skip * x_h
    lead_ref[...] = y_h * halo_gate[...]


def line_of(start, groups):
    return jnp.minimum((start + T - 1) // T, (groups + T - window_of(groups)) // T)


def window_of(groups):
    return min(3 * T, groups + T)


def norm_kernel(
    n_head,
    groups,
    mix,
    open_gate,
    grow,
    locs,
    fades,
    maps,
    base,
    lead_ref,
    rank_ref,
    start_ref,
    table,
    inv_ref,
    place_ref,
    squares,
    sq_send,
    sq_recv,
):
    column = lax.axis_index("head")
    subs = groups // T
    blocks = place_ref.shape[0] // BLOCK
    barrier = pltpu.get_barrier_semaphore()

    def greet_head(d, carry):
        pl.semaphore_signal(
            barrier, inc=1, device_id={"head": lax.rem(column + d, n_head)}, device_id_type=MESH
        )
        return carry

    lax.fori_loop(1, n_head, greet_head, 0)

    def sq_copy(d):
        return pltpu.make_async_remote_copy(
            src_ref=squares.at[column],
            dst_ref=squares.at[column],
            send_sem=sq_send,
            recv_sem=sq_recv,
            device_id={"head": lax.rem(column + d, n_head)},
            device_id_type=MESH,
        )

    ones = jnp.ones((8, WIDE), BF16)
    g_h = lead_ref[...]
    table[0 : T - 16, :] = jnp.zeros((T - 16, WIDE), BF16)
    table[T - 16 : T, :] = g_h.astype(BF16)
    power = jnp.concatenate([jnp.zeros((T - 16, WIDE), F32), g_h * g_h], 0).astype(BF16)
    mine = squares.at[column]
    mine[...] = jnp.zeros(mine.shape, F32)
    mine[0:1, :] = dot_nt(ones, power)[0:1, :]

    together = min(8, subs)

    def outer(i, carry):
        for q in range(together):
            k = i * together + q
            at = pl.ds(pl.multiple_of(k * T, T), T)
            state = (locs[k] + fades[k] * base[jnp.where(k > 2, 1, 0)]).astype(BF16)
            gated = mix[at, :] + grow[k] * dot(maps[at, STATE:], state)
            gated = gated * open_gate[at, :]
            table[pl.ds(pl.multiple_of((k + 1) * T, T), T), :] = gated.astype(BF16)
            squares[column, pl.ds(k + 1, 1), :] = dot_nt(ones, (gated * gated).astype(BF16))[0:1, :]
        return carry

    lax.fori_loop(0, subs // together, outer, 0)

    pl.semaphore_wait(barrier, n_head - 1)
    start_all(sq_copy, n_head)

    def locate(i, carry):
        for j in (2 * i, 2 * i + 1) if blocks % 2 == 0 else (i,):
            for half in range(2):
                lane = iota((T, T), 1)
                rank = jnp.sum(
                    jnp.where(lane == 2 * j + half, rank_ref[...], 0.0), axis=1, keepdims=True
                )
                first = (line_of(start_ref[j], groups) * T).astype(F32)
                place = jnp.broadcast_to(rank + ((T - 1.0) - first), (T, T))
                lane = lane.astype(F32)
                hits = [flag(place == lane + w * T) for w in range(window_of(groups) // T)]
                at = pl.ds(pl.multiple_of(j * BLOCK + half * T, T), T)
                place_ref[at, :] = jnp.concatenate(hits, 1)
        return carry

    lax.fori_loop(0, blocks // 2 if blocks % 2 == 0 else blocks, locate, 0)

    wait_all(squares, sq_send, squares, sq_recv)
    power = squares[0]
    for i in range(1, n_head):
        power = power + squares[i]
    inv_ref[...] = lax.rsqrt(power * (1.0 / (n_head * WIDE)) + EPSILON)


def norm(n_head, groups, length, *args):
    subs = groups // T
    lines = -(-(subs + 1) // 8) * 8
    vmem = pl.BlockSpec(memory_space=pltpu.VMEM)
    return pl.pallas_call(
        functools.partial(norm_kernel, n_head, groups),
        out_shape=[
            on_chip((groups + T, WIDE), BF16),
            on_chip((lines, T), F32),
            on_chip((length, window_of(groups)), BF16),
        ],
        in_specs=[vmem] * 9 + [pl.BlockSpec(memory_space=pltpu.SMEM)],
        out_specs=[vmem] * 3,
        scratch_shapes=[
            pltpu.VMEM((n_head, lines, T), F32),
            pltpu.SemaphoreType.DMA,
            pltpu.SemaphoreType.DMA,
        ],
        compiler_params=pltpu.CompilerParams(
            collective_id=1, has_side_effects=True, vmem_limit_bytes=8 << 20
        ),
        cost_estimate=pl.CostEstimate(
            flops=4 * groups * STATE * WIDE, bytes_accessed=1 << 20, transcendentals=0
        ),
    )(*args)


def layer(n_ctx, groups, *args):
    subs = groups // T
    share = STATE * 4 // n_ctx
    vmem = pl.BlockSpec(memory_space=pltpu.VMEM)
    smem = pl.BlockSpec(memory_space=pltpu.SMEM)
    width = args[0].shape[1]
    sem = pltpu.SemaphoreType.DMA
    return pl.pallas_call(
        functools.partial(layer_kernel, n_ctx, groups),
        out_shape=[
            on_chip((groups, WIDE), F32),
            on_chip((groups, WIDE), F32),
            on_chip((subs, T, WIDE), F32),
            on_chip((subs + 1, STATE, WIDE), F32),
            on_chip((subs + 1, 1, WIDE), F32),
            on_chip((groups, 2 * STATE), BF16),
            on_chip((2, STATE, WIDE), F32),
            on_chip((16, WIDE), F32),
        ],
        in_specs=[vmem] * 11 + [smem] * 3,
        out_specs=[vmem] * 8,
        scratch_shapes=[
            pltpu.VMEM((6, 2 * T + 8, 128), F32),
            pltpu.VMEM((6, 2 * T + 8, 128), F32),
            pltpu.VMEM((6, 2 * T + 8, 128), F32),
            pltpu.VMEM((6, 24, 128), F32),
            pltpu.VMEM((6, 8, 128), F32),
            pltpu.VMEM((subs, 1, WIDE), F32),
            pltpu.VMEM((groups, WIDE), BF16),
            pltpu.VMEM((subs * 8, T), F32),
            pltpu.VMEM((subs, 48, T), BF16),
            pltpu.VMEM((subs, 32, T), BF16),
            pltpu.VMEM((subs, 24, T), F32),
            pltpu.VMEM((24, 8 * T), F32),
            pltpu.VMEM((32, 2 * WIDE), BF16),
            pltpu.VMEM((2, 16, width), BF16),
            pltpu.VMEM((16, WIDE), F32),
            pltpu.VMEM((4, 16, 128), BF16),
            pltpu.VMEM((n_ctx, 16, 128), BF16),
            pltpu.VMEM((n_ctx, share, 128), BF16),
            pltpu.VMEM((n_ctx, share, 128), BF16),
            pltpu.VMEM((n_ctx, share, 128), BF16),
            pltpu.VMEM((n_ctx, share, 128), BF16),
            pltpu.VMEM((STATE, WIDE), BF16),
            sem((2,)),
            sem((2,)),
            sem,
            sem,
            sem,
            sem,
            sem,
            sem,
        ],
        compiler_params=pltpu.CompilerParams(
            collective_id=0, has_side_effects=True, vmem_limit_bytes=14 << 20
        ),
        cost_estimate=pl.CostEstimate(
            flops=2 * groups * width * 1536, bytes_accessed=8 << 20, transcendentals=1 << 22
        ),
    )(*args)


def expand_kernel(groups, start_ref, place_ref, table_ref, inv_ref, gain_ref, out_hbm, ready, sems):
    blocks = out_hbm.shape[0] // BLOCK
    window = window_of(groups)

    def send(j):
        at = pl.ds(pl.multiple_of(j * BLOCK, BLOCK), BLOCK)
        return pltpu.make_async_copy(ready.at[at], out_hbm.at[at], sems.at[j])

    def step(j, carry):
        line = line_of(start_ref[j], groups)
        at = pl.ds(pl.multiple_of(j * BLOCK, BLOCK), BLOCK)
        places = place_ref[at, :]
        got = dot(places, table_ref[pl.ds(pl.multiple_of(line * T, T), window), :])
        scale = jnp.zeros((BLOCK, T), F32)
        for w in range(window // T):
            scale = scale + places[:, w * T : (w + 1) * T].astype(F32) * inv_ref[pl.ds(line + w, 1), :]
        ready[at, :] = got * gain_ref[...] * jnp.sum(scale, axis=1, keepdims=True)
        send(j).start()
        return carry

    def steps(i, carry):
        for q in range(UNROLL):
            step(i * UNROLL + q, 0)
        return carry

    lax.fori_loop(0, blocks // UNROLL, steps, 0)
    for j in range(blocks - blocks % UNROLL, blocks):
        step(j, 0)

    def finish(j, carry):
        send(j).wait()
        return carry

    lax.fori_loop(0, blocks, finish, 0)


def expand(length, groups, starts, places, table, inv, gain):
    vmem = pl.BlockSpec(memory_space=pltpu.VMEM)
    return pl.pallas_call(
        functools.partial(expand_kernel, groups),
        out_shape=jax.ShapeDtypeStruct((length, WIDE), F32),
        in_specs=[pl.BlockSpec(memory_space=pltpu.SMEM), vmem, vmem, vmem, vmem],
        out_specs=pl.BlockSpec(memory_space=pl.ANY),
        scratch_shapes=[
            pltpu.VMEM((length, WIDE), F32),
            pltpu.SemaphoreType.DMA((length // BLOCK,)),
        ],
        compiler_params=pltpu.CompilerParams(vmem_limit_bytes=12 << 20),
        cost_estimate=pl.CostEstimate(
            flops=2 * length * 3 * T * WIDE, bytes_accessed=4 * length * WIDE, transcendentals=0
        ),
    )(starts, places, table, inv, gain)


def shards(
    groups,
    byte_rows,
    boundary,
    gate_proj,
    value_proj,
    state_proj,
    step_proj,
    step_bias,
    decay_log,
    skip_gain,
    value_conv,
    value_shift,
    state_conv,
    state_shift,
    norm_gain,
):
    n_ctx, n_head = lax.axis_size("ctx"), lax.axis_size("head")
    weights = [keep_on_chip(w) for w in (value_proj, gate_proj, state_proj, step_proj.T)]
    rows, tail, count, rank, starts = compact(
        keep_off_chip(boundary), keep_off_chip(byte_rows), groups
    )
    carried = layer(
        n_ctx,
        groups,
        rows,
        tail,
        count,
        *weights,
        value_conv,
        value_shift.reshape(1, -1),
        state_conv,
        state_shift.reshape(1, -1),
        step_bias,
        decay_log,
        skip_gain,
    )
    length = byte_rows.shape[0]
    table, inv, places = norm(n_head, groups, length, *carried, rank, starts)
    return expand(length, groups, starts, places, table, inv, norm_gain.reshape(1, -1))


def solution(mesh, groups=2048):
    placed = (
        P("ctx", None),
        P("ctx"),
        P(None, "head"),
        P(None, "head"),
        P(),
        P(None, "head"),
        P("head"),
        P("head"),
        P("head"),
        P(None, "head"),
        P("head"),
        P(),
        P(),
        P("head"),
    )
    return jax.shard_map(
        functools.partial(shards, groups),
        mesh=mesh,
        in_specs=placed,
        out_specs=P("ctx", "head"),
        check_vma=False,
    )
```
